128 devices in a mesh: dp: 2 (over z_lo), row: 8 (over y, core), col: 8 (over x, z_hi).
Axes of the slice: x: 4, y: 4, z: 4 (z_hi: 2, z_lo: 2; z = z_hi * 2 + z_lo), core: 2. Of those that a mesh axis runs over, the one named last changes fastest.
Arguments:
- hidden_in: bfloat16 [16384, 2048], P(('dp', 'row'), 'col'), may hold values from -64 to 64
- segment_ids: int32 [16, 1024], P(('dp', 'col')), may hold values from 0 to 3, never falling along the last dimension, each value on 1 to 768 neighbouring positions
- attn_gain: float32 [2048], P('col'), may hold values from 0.25 to 1.75
- w_query: bfloat16 [2048, 2048], P('col', 'row'), may hold values from -0.1875 to 0.1875
- w_key: bfloat16 [2048, 256], P('col', 'row'), may hold values from -0.1875 to 0.1875
- w_value: bfloat16 [2048, 256], P('col', 'row'), may hold values from -0.125 to 0.125
- w_out: bfloat16 [2048, 2048], P('row', 'col'), may hold values from -0.375 to 0.375
- mlp_gain: float32 [2048], P('col'), may hold values from 0.25 to 1.75
- w_gate: bfloat16 [2048, 5632], P('col', 'row'), may hold values from -0.125 to 0.125
- w_up: bfloat16 [2048, 5632], P('col', 'row'), may hold values from -0.125 to 0.125
- w_down: bfloat16 [5632, 2048], P('row', 'col'), may hold values from -0.078125 to 0.078125
- grad_output: bfloat16 [16384, 2048], P(('dp', 'row'), 'col'), may hold values from -6 to 6
Outputs:
- layer_output: bfloat16 [16384, 2048], P(('dp', 'row'), 'col')
- grad_input: float32 [16384, 2048], P(('dp', 'row'), 'col')
- grad_attn_gain: float32 [2048], P('col')
- grad_query: float32 [2048, 2048], P('col', 'row')
- grad_key: float32 [2048, 256], P('col', 'row')
- grad_value: float32 [2048, 256], P('col', 'row')
- grad_out_proj: float32 [2048, 2048], P('row', 'col')
- grad_mlp_gain: float32 [2048], P('col')
- grad_gate: float32 [2048, 5632], P('col', 'row')
- grad_up: float32 [2048, 5632], P('col', 'row')
- grad_down: float32 [5632, 2048], P('row', 'col')
The draws below stay inside these ranges and needn't reach their ends.
Inputs may be any that keep to these rules, and one draw needn't show every extreme that they name: `segment_ids`: along every sequence the numbers never fall; a document holds at most 768 tokens.
All inputs are finite; a program needn't handle non-finite values.
Results may differ from the reference program's by a relative error of at most 0.025.
Values may be sent and summed in bfloat16 or wider, within the bound.
A program may use at most 256 MiB of HBM per device.

```python
import math
import jax
import jax.numpy as jnp
import numpy as np
from jax import lax

D = 2048
QH = 32
KVH = 4
HD = 64
FF = 5632
LEN = 1024
DOCS = 4
DOC_MOST = 768
SEQS = 16
TOKENS = 16384


def draw_hidden_in(key, part):
    key = jax.random.fold_in(key, 11)
    base_key, column_key, row_key = jax.random.split(key, 3)
    base_draw = jnp.clip(jax.random.normal(base_key, (TOKENS, D), jnp.float32), -5.0, 5.0)
    column_ramp = 3.0 ** (jnp.arange(D, dtype=jnp.float32) / D - 0.5)
    columns = column_ramp * jax.random.uniform(column_key, (D,), jnp.float32, 0.7, 1.4)
    row_scales = 10.0 ** jax.random.uniform(row_key, (TOKENS, 1), jnp.float32, -0.5, 0.5)
    values = row_scales * base_draw * columns
    return values.astype(jnp.bfloat16)


def steps_of(own_key, extent, cuts, smallest, largest):
    def one(position, parts):
        draws = jax.random.uniform(jax.random.fold_in(jax.random.fold_in(own_key, 6), position), (parts,), jnp.float32, smallest / len(cuts), largest / len(cuts))
        return jnp.repeat(jnp.exp(draws), extent[position] // parts).reshape((-1,) + (1,) * (len(extent) - position - 1))

    level = one(*cuts[0])
    for cut in cuts[1:]:
        level = level * one(*cut)
    return level


def profile(amount, total, reach, skew):
    portions = [(1 << 20) // math.isqrt(grade ** skew) + 1 for grade in range(2, amount + 1)]
    surplus, holding = total - reach - (amount - 1), [1] * (amount - 1)
    while surplus > 0:
        candidates = [i for i in range(amount - 1) if holding[i] < reach]
        whole, budget = sum([portions[i] for i in candidates]), surplus
        for i in candidates:
            more = min(reach - holding[i], max(1, budget * portions[i] // whole), surplus)
            holding[i] = holding[i] + more
            surplus = surplus - more
    return np.array([reach] + holding)


def uneven(stream_key, count, total, most, slope):
    if count == 2:
        one = jax.random.randint(stream_key, (), max(1, total - most), min(most, total - 1) + 1)
        return jnp.stack([one, total - one])
    lengths = jnp.asarray(profile(count, total, most, slope), jnp.int32)
    twos = (count - 1) // 2
    donor, taker = lengths[1:1 + 2 * twos:2], lengths[2:2 + 2 * twos:2]
    slack = jnp.minimum(donor - 1, most - taker)
    passed = jax.random.randint(jax.random.fold_in(stream_key, 1), (twos,), 0, 1 << 20) % (slack + 1)
    lengths = lengths.at[1:1 + 2 * twos:2].set(donor - passed).at[2:2 + 2 * twos:2].set(taker + passed)
    return lengths[jax.random.permutation(jax.random.fold_in(stream_key, 2), count)]


def bell_draw(rng, dims, spread, reach, shards=(), kind=jnp.bfloat16):
    entries = spread * jax.random.normal(rng, dims, jnp.float32)
    if shards:
        entries = entries * steps_of(rng, dims, shards, -0.22, 0.18)
    return jnp.clip(entries, -reach, reach).astype(kind)


def setup_inputs(seed: int = 0) -> dict:
    seeds = jax.random.split(jax.random.key(seed), 13)
    return {
        "hidden_in": draw_hidden_in(jax.random.fold_in(seeds[12], 71), 0),
        "segment_ids": jax.vmap(lambda own: jnp.searchsorted(jnp.cumsum(uneven(own, DOCS, LEN, DOC_MOST, 1)), jnp.arange(LEN), side="right"))(jax.random.split(seeds[1], SEQS)).reshape((SEQS, LEN)).astype(jnp.int32),
        "attn_gain": jnp.clip(1.0 + 0.15 * jax.random.normal(seeds[2], (D,), jnp.float32), 0.25, 1.75),
        "w_query": bell_draw(seeds[3], (D, QH * HD), (D // 2) ** -0.5, 0.1875, ((0, 8), (1, 8))),
        "w_key": bell_draw(seeds[4], (D, KVH * HD), (D // 2) ** -0.5, 0.1875, ((0, 8), (1, 8))),
        "w_value": bell_draw(seeds[5], (D, KVH * HD), D ** -0.5, 0.125, ((0, 8), (1, 8))),
        "w_out": bell_draw(seeds[6], (QH * HD, D), (QH * HD // 8) ** -0.5, 0.375, ((0, 8), (1, 8))),
        "mlp_gain": jnp.clip(1.0 + 0.15 * jax.random.normal(seeds[7], (D,), jnp.float32), 0.25, 1.75),
        "w_gate": bell_draw(seeds[8], (D, FF), D ** -0.5, 0.125, ((0, 8), (1, 8))),
        "w_up": bell_draw(seeds[9], (D, FF), D ** -0.5, 0.125, ((0, 8), (1, 8))),
        "w_down": bell_draw(seeds[10], (FF, D), FF ** -0.5, 0.078125, ((0, 8), (1, 8))),
        "grad_output": bell_draw(seeds[11], (TOKENS, D), 1.0, 6.0, ((0, 16), (1, 8))),
    }


EPSILON = 1e-05
FLOOR_SCORE = -1e+30
HIGHEST = lax.Precision.HIGHEST

@jax.custom_vjp
def low(v):
    return lax.optimization_barrier(v.astype(jnp.bfloat16)).astype(jnp.float32)

@jax.custom_vjp
def low_back(v):
    return v

def low_keep(v):
    return (low(v), None)

def low_pass(kept, grad):
    return (grad,)

def back_keep(v):
    return (v, None)

def back_low(kept, grad):
    return (low(grad),)
low.defvjp(low_keep, low_pass)
low_back.defvjp(back_keep, back_low)

def doc_positions(segments):
    length = segments.shape[-1]
    places = jnp.arange(length, dtype=jnp.int32)
    change = jnp.concatenate([jnp.ones(segments.shape[:-1] + (1,), jnp.bool_), segments[..., 1:] != segments[..., :-1]], axis=-1)
    starts = jnp.where(change, places, 0).astype(jnp.int32)
    return (places - lax.cummax(starts, axis=segments.ndim - 1)).astype(jnp.int32)

def rope_tables(positions, head_width):
    frequency = jnp.exp(jnp.arange(0, head_width, 2, dtype=jnp.float32) * (-math.log(10000.0) / head_width))
    angles = positions.astype(jnp.float32)[..., None] * frequency
    angles = jnp.concatenate([angles, angles], axis=-1)
    return (jnp.cos(angles), jnp.sin(angles))

def rotate(values, cos_table, sin_table):
    half_width = values.shape[-1] // 2
    turned = jnp.concatenate([-values[..., half_width:], values[..., :half_width]], axis=-1)
    return values * cos_table + turned * sin_table

def rms_norm(values, gain_vector):
    return values * lax.rsqrt(lax.optimization_barrier(jnp.mean(values * values, axis=-1, keepdims=True)) + EPSILON) * gain_vector

def attend_sequence(query_rows, key_rows, value_rows, segments):
    group_size = query_rows.shape[1] // key_rows.shape[1]
    keys_all = jnp.repeat(key_rows, group_size, axis=1)
    values_all = jnp.repeat(value_rows, group_size, axis=1)
    scores = low_back(jnp.einsum('qhd,khd->hqk', query_rows, keys_all, precision=HIGHEST) * query_rows.shape[2] ** (-0.5))
    places = jnp.arange(query_rows.shape[0], dtype=jnp.int32)
    allowed = (segments[:, None] == segments[None, :]) & (places[None, :] <= places[:, None])
    scores = jnp.where(allowed[None], scores, FLOOR_SCORE)
    row_max = lax.optimization_barrier(jnp.max(scores, axis=-1, keepdims=True))
    exp_scores = jnp.exp(scores - row_max)
    probabilities = low(exp_scores / lax.optimization_barrier(jnp.sum(exp_scores, axis=-1, keepdims=True)))
    return jnp.einsum('hqk,khd->qhd', probabilities, values_all, precision=HIGHEST)

def attend_packed(packed):
    return attend_sequence(packed[0], packed[1], packed[2], packed[3])

def forward(inputs, attn_gain, w_query, w_key, w_value, w_out, mlp_gain, w_gate, w_up, w_down, segments):
    seq_count, length = segments.shape
    row_count = inputs.shape[0]
    normed_one = low(rms_norm(inputs, attn_gain))
    query_pre = low_back(jnp.dot(normed_one, w_query, precision=HIGHEST))
    key_pre = low_back(jnp.dot(normed_one, w_key, precision=HIGHEST))
    value_pre = low_back(jnp.dot(normed_one, w_value, precision=HIGHEST))
    cos_table, sin_table = rope_tables(doc_positions(segments).reshape(-1), HD)
    query_low = low(rotate(query_pre.reshape(row_count, -1, HD), cos_table[:, None], sin_table[:, None]))
    key_low = low(rotate(key_pre.reshape(row_count, -1, HD), cos_table[:, None], sin_table[:, None]))
    value_low = low(value_pre.reshape(row_count, -1, HD))
    mixed = lax.map(jax.checkpoint(attend_packed), (query_low.reshape(seq_count, length, -1, HD), key_low.reshape(seq_count, length, -1, HD), value_low.reshape(seq_count, length, -1, HD), segments))
    mixed_low = low(low_back(mixed.reshape(row_count, -1)))
    residual = inputs + low_back(jnp.dot(mixed_low, w_out, precision=HIGHEST))
    normed_two = low(rms_norm(residual, mlp_gain))
    gate_proj = low_back(jnp.dot(normed_two, w_gate, precision=HIGHEST))
    up_proj = low_back(jnp.dot(normed_two, w_up, precision=HIGHEST))
    activated = low(jax.nn.silu(gate_proj) * up_proj)
    return residual + jnp.dot(activated, w_down, precision=HIGHEST)

def reference(hidden_in, segment_ids, attn_gain, w_query, w_key, w_value, w_out, mlp_gain, w_gate, w_up, w_down, grad_output):
    params = (attn_gain.astype(jnp.float32), w_query.astype(jnp.float32), w_key.astype(jnp.float32), w_value.astype(jnp.float32), w_out.astype(jnp.float32), mlp_gain.astype(jnp.float32), w_gate.astype(jnp.float32), w_up.astype(jnp.float32), w_down.astype(jnp.float32))
    group_size = math.gcd(SEQS, max(1, 4096 // LEN))
    groups = SEQS // group_size
    inputs = hidden_in.astype(jnp.float32).reshape(groups, group_size * LEN, D)
    cotangents = grad_output.astype(jnp.float32).reshape(groups, group_size * LEN, D)
    segments = segment_ids.reshape(groups, group_size, LEN)

    def one_group(running, packed):
        block_inputs, block_cotangent, block_segments = packed

        def layer_fn(layer_inputs, gain_one, query_weight, key_weight, value_weight, out_weight, gain_two, gate_weight, up_weight, down_weight):
            return forward(layer_inputs, gain_one, query_weight, key_weight, value_weight, out_weight, gain_two, gate_weight, up_weight, down_weight, block_segments)
        result, pullback = jax.vjp(layer_fn, block_inputs, *params)
        gradients = pullback(block_cotangent)
        running = tuple((total_grad + new_grad for total_grad, new_grad in zip(running, gradients[1:])))
        return (running, (result.astype(jnp.bfloat16), gradients[0]))
    initial = tuple((jnp.zeros_like(weight_arg) for weight_arg in params))
    totals, (outputs, input_grads) = lax.scan(one_group, initial, (inputs, cotangents, segments))
    return (outputs.reshape(TOKENS, D), input_grads.reshape(TOKENS, D), totals[0], totals[1], totals[2], totals[3], totals[4], totals[5], totals[6], totals[7], totals[8])
```

```python
import math

import jax
import jax.numpy as jnp
from jax import lax
from jax.sharding import PartitionSpec as P

D = 2048
HD = 64
EPSILON = 1e-05
FLOOR_SCORE = -1e30
BF16 = jnp.bfloat16
F32 = jnp.float32


def doc_positions(segments):
    length = segments.shape[-1]
    places = jnp.arange(length, dtype=jnp.int32)
    change = jnp.concatenate(
        [jnp.ones(segments.shape[:-1] + (1,), jnp.bool_), segments[..., 1:] != segments[..., :-1]],
        axis=-1,
    )
    starts = jnp.where(change, places, 0)
    return places - lax.cummax(starts, axis=segments.ndim - 1)


def rope_tables(positions, head_width):
    frequency = jnp.exp(
        jnp.arange(0, head_width, 2, dtype=F32) * (-math.log(10000.0) / head_width)
    )
    angles = positions.astype(F32)[..., None] * frequency
    angles = jnp.concatenate([angles, angles], axis=-1)
    return (jnp.cos(angles), jnp.sin(angles))


def rotate(values, cos_table, sin_table):
    half_width = values.shape[-1] // 2
    turned = jnp.concatenate([-values[..., half_width:], values[..., :half_width]], axis=-1)
    return values * cos_table + turned * sin_table


def transposed_blocks(values):
    size = lax.axis_size("row")
    pairs = [(a * size + b, b * size + a) for a in range(size) for b in range(size)]
    return lax.ppermute(values, ("row", "col"), pairs)


def partner(values):
    pairs = [(a, a ^ 1) for a in range(lax.axis_size("row"))]
    return lax.ppermute(values, "row", pairs)


def mm(a, b):
    return jnp.dot(a, b, preferred_element_type=F32)


def mm_tn(a, b):
    return lax.dot_general(a, b, (((0,), (0,)), ((), ())), preferred_element_type=F32)


def mm_nt(a, b):
    return lax.dot_general(a, b, (((1,), (1,)), ((), ())), preferred_element_type=F32)


def gather_rows(values, axis):
    return lax.all_gather(values, "row", axis=axis, tiled=True)


def sum_rows(values, axis):
    return lax.psum_scatter(values.astype(BF16), "row", scatter_dimension=axis, tiled=True)


def gather_cols(values, axis):
    return lax.all_gather(values, "col", axis=axis, tiled=True)


def weight_sum(values, axis):
    part = lax.psum_scatter(values.astype(BF16), "col", scatter_dimension=axis, tiled=True)
    return lax.psum(part, "dp").astype(F32)


def norm_scale(values):
    return lax.rsqrt(jnp.mean(values * values, axis=1, keepdims=True) + EPSILON)


def norm_back(d_normed, values, scales, gain_vector):
    d_scaled = d_normed * gain_vector
    inner = jnp.mean(d_scaled * values, axis=1, keepdims=True)
    return scales * d_scaled - values * (scales * scales * scales * inner)


def scores_of(query, key, segments):
    places = jnp.arange(key.shape[0], dtype=jnp.int32)
    allowed = (segments[:, None] == segments[None, :]) & (places[None, :] <= places[:, None])
    scores = jnp.einsum("qhd,kd->hqk", query, key, preferred_element_type=F32) * HD ** (-0.5)
    return jnp.where(allowed[None], scores, FLOOR_SCORE)


def attend(query, key, value, segments):
    scores = scores_of(query, key, segments)
    row_max = jnp.max(scores, axis=-1, keepdims=True)
    exp_scores = jnp.exp(scores - row_max)
    row_sums = jnp.sum(exp_scores, axis=-1, keepdims=True)
    probs = (exp_scores / row_sums).astype(BF16)
    mixed = jnp.einsum("hqk,kd->qhd", probs, value, preferred_element_type=F32)
    return mixed.reshape(query.shape[0], -1), row_max + jnp.log(row_sums)


def attend_back(query, key, value, d_mixed, totals, segments):
    scores = scores_of(query, key, segments)
    grads = d_mixed.reshape(query.shape)
    probs = jnp.exp(scores - totals)
    d_probs = jnp.einsum("qhd,kd->hqk", grads, value, preferred_element_type=F32)
    inner = jnp.sum(probs * d_probs, axis=-1, keepdims=True)
    d_scores = (probs * (d_probs - inner)).astype(BF16)
    d_query = jnp.einsum("hqk,kd->qhd", d_scores, key, preferred_element_type=F32) * HD ** (-0.5)
    d_key = jnp.einsum("hqk,qhd->kd", d_scores, query, preferred_element_type=F32) * HD ** (-0.5)
    d_value = jnp.einsum("hqk,qhd->kd", probs.astype(BF16), grads, preferred_element_type=F32)
    return d_query, d_key, d_value


def body(
    hidden_in,
    segment_ids,
    attn_gain,
    w_query,
    w_key,
    w_value,
    w_out,
    mlp_gain,
    w_gate,
    w_up,
    w_down,
    grad_output,
):
    row = lax.axis_index("row")
    upper = row % 2 == 1
    query_width = w_query.shape[1]
    kv_width = w_key.shape[1]
    ff_width = w_gate.shape[1]
    head_count = query_width // HD
    segments = segment_ids.reshape(-1)
    cos_table, sin_table = rope_tables(doc_positions(segments), HD)

    gains = gather_cols(jnp.stack([attn_gain, mlp_gain], axis=1), 0)
    gain_one, gain_two = gains[:, 0], gains[:, 1]

    kv_own = jnp.concatenate([w_key, w_value], axis=1)
    kv_other = partner(kv_own)
    kv_first = jnp.where(upper, kv_other, kv_own)
    kv_second = jnp.where(upper, kv_own, kv_other)
    w_project = gather_cols(
        jnp.concatenate(
            [
                w_query,
                kv_first[:, :kv_width],
                kv_second[:, :kv_width],
                kv_first[:, kv_width:],
                kv_second[:, kv_width:],
            ],
            axis=1,
        ),
        0,
    )
    x_all = gather_rows(transposed_blocks(hidden_in), 1)
    w_out_all = gather_cols(w_out, 1)
    w_both = gather_cols(jnp.concatenate([w_gate, w_up], axis=1), 0)
    w_down_all = gather_cols(w_down, 1)
    grad_all = gather_rows(transposed_blocks(grad_output), 1)

    x_float = x_all.astype(F32)
    scale_one = norm_scale(x_float)
    normed_one = (x_float * scale_one * gain_one).astype(BF16)
    projected = mm(normed_one, w_project)
    query = rotate(
        projected[:, :query_width].reshape(-1, head_count, HD),
        cos_table[:, None],
        sin_table[:, None],
    ).astype(BF16)
    key = rotate(projected[:, query_width : query_width + HD], cos_table, sin_table).astype(BF16)
    value = projected[:, query_width + HD :].astype(BF16)
    mixed, totals = attend(query, key, value, segments)
    mixed_low = mixed.astype(BF16)

    token_rows = x_all.shape[0] // lax.axis_size("row")
    x_mine = lax.dynamic_slice_in_dim(x_all, row * token_rows, token_rows, 0).astype(F32)
    scale_mine = lax.dynamic_slice_in_dim(scale_one, row * token_rows, token_rows, 0)
    residual = x_mine + sum_rows(mm(mixed_low, w_out_all), 0).astype(F32)
    scale_two = norm_scale(residual)
    normed_two = gather_rows((residual * scale_two * gain_two).astype(BF16), 0)
    both = mm(normed_two, w_both)
    gate, up = both[:, :ff_width], both[:, ff_width:]
    sig = jax.nn.sigmoid(gate)
    activated = (gate * sig * up).astype(BF16)
    down = mm(activated, w_down_all)
    here = lax.dynamic_slice_in_dim(down, row * token_rows, token_rows, 0) + residual
    down = lax.dynamic_update_slice_in_dim(down, here, row * token_rows, 0)
    layer_output = transposed_blocks(sum_rows(down, 1))

    d_activated = mm_nt(grad_all, w_down_all)
    grad_down = mm_tn(activated, grad_all)
    d_gate = (d_activated * up * sig * (1.0 + gate * (1.0 - sig))).astype(BF16)
    d_up = (d_activated * (gate * sig)).astype(BF16)
    d_both = jnp.concatenate([d_gate, d_up], axis=1)
    d_normed_two = sum_rows(mm_nt(d_both, w_both), 0).astype(F32)
    grad_both = mm_tn(normed_two, d_both)
    d_gain_two = jnp.sum(d_normed_two * residual * scale_two, axis=0)
    grad_mine = lax.dynamic_slice_in_dim(grad_all, row * token_rows, token_rows, 0)
    d_residual = grad_mine.astype(F32) + norm_back(d_normed_two, residual, scale_two, gain_two)
    d_residual_all = gather_rows(d_residual.astype(BF16), 0)
    d_mixed = mm_nt(d_residual_all, w_out_all).astype(BF16)
    grad_out_proj = mm_tn(mixed_low, d_residual_all)
    d_query_rot, d_key_rot, d_value = attend_back(query, key, value, d_mixed, totals, segments)
    d_query = rotate(d_query_rot, cos_table[:, None], -sin_table[:, None]).reshape(-1, query_width)
    d_key = rotate(d_key_rot, cos_table, -sin_table)
    d_projected = jnp.concatenate([d_query, d_key, d_value], axis=1).astype(BF16)
    grad_project = mm_tn(normed_one, d_projected)
    d_normed_one = sum_rows(mm_nt(d_projected, w_project), 0).astype(F32)
    d_gain_one = jnp.sum(d_normed_one * x_mine * scale_mine, axis=0)
    grad_input = d_residual + norm_back(d_normed_one, x_mine, scale_mine, gain_one)
    grad_input = lax.all_to_all(
        grad_input.astype(BF16), "row", split_axis=1, concat_axis=0, tiled=True
    )
    grad_input = transposed_blocks(grad_input).astype(F32)

    d_gains = lax.psum_scatter(
        jnp.stack([d_gain_one, d_gain_two], axis=1), "col", scatter_dimension=0, tiled=True
    )
    d_gains = lax.psum(d_gains, ("dp", "row"))
    grad_down = weight_sum(grad_down, 1)
    grad_both = weight_sum(grad_both, 0)
    grad_out_proj = weight_sum(grad_out_proj, 1)
    grad_project = lax.psum_scatter(
        grad_project.astype(BF16), "col", scatter_dimension=0, tiled=True
    )
    grad_kv = grad_project[:, query_width:].reshape(-1, 2, 2, kv_width)
    keep = jnp.where(upper, grad_kv[:, :, 1], grad_kv[:, :, 0])
    give = jnp.where(upper, grad_kv[:, :, 0], grad_kv[:, :, 1])
    grad_kv = (keep.astype(F32) + partner(give).astype(F32)).astype(BF16)
    grad_query, grad_kv = lax.psum((grad_project[:, :query_width], grad_kv), "dp")
    grad_kv = grad_kv.astype(F32)
    return (
        layer_output,
        grad_input,
        d_gains[:, 0],
        grad_query.astype(F32),
        grad_kv[:, 0],
        grad_kv[:, 1],
        grad_out_proj,
        d_gains[:, 1],
        grad_both[:, :ff_width],
        grad_both[:, ff_width:],
        grad_down,
    )


def solution(mesh):
    return jax.shard_map(
        body,
        mesh=mesh,
        in_specs=(
            P(("dp", "row"), "col"),
            P(("dp", "col"), None),
            P("col"),
            P("col", "row"),
            P("col", "row"),
            P("col", "row"),
            P("row", "col"),
            P("col"),
            P("col", "row"),
            P("col", "row"),
            P("row", "col"),
            P(("dp", "row"), "col"),
        ),
        out_specs=(
            P(("dp", "row"), "col"),
            P(("dp", "row"), "col"),
            P("col"),
            P("col", "row"),
            P("col", "row"),
            P("col", "row"),
            P("row", "col"),
            P("col"),
            P("col", "row"),
            P("col", "row"),
            P("row", "col"),
        ),
        check_vma=False,
    )
```

```python
import functools
import math

import jax
import jax.numpy as jnp
from jax import lax
from jax.experimental import pallas as pl
from jax.experimental.pallas import tpu as pltpu
from jax.sharding import PartitionSpec as P

D = 2048
HD = 64
LEN = 1024
ROWS = 8
CHIPS = 4
TOK = LEN // ROWS
FEAT = D // 8
EPSILON = 1e-05
FLOOR_SCORE = -1e30
BF16 = jnp.bfloat16
F32 = jnp.float32
MESH = pl.DeviceIdType.MESH
VMEM_BYTES = 60 * 2**20


def remote(src, dst, send, recv, device):
    return pltpu.make_async_remote_copy(
        src_ref=src, dst_ref=dst, send_sem=send, recv_sem=recv, device_id=device, device_id_type=MESH
    )


def meet(peers):
    barrier = pltpu.get_barrier_semaphore()
    for peer in peers:
        pl.semaphore_signal(barrier, inc=1, device_id=peer, device_id_type=MESH)
    pl.semaphore_wait(barrier, len(peers))


def ds(start, size):
    return pl.ds(pl.multiple_of(start, size), size)


class Place:
    def __init__(self):
        self.d = lax.axis_index("dp")
        self.r = lax.axis_index("row")
        self.c = lax.axis_index("col")
        self.y, self.k = self.r // 2, lax.rem(self.r, 2)
        self.x, self.h = self.c // 2, lax.rem(self.c, 2)
        self.partner = {"row": self.y * 2 + 1 - self.k}
        self.up = {"row": self.row_of(1)}
        self.down = {"row": self.row_of(3)}
        self.other = {"dp": 1 - self.d, "col": self.x * 2 + 1 - self.h}
        self.x_peers = [{"col": self.col_of(s)} for s in (1, 3, 2)]

    def row_of(self, step):
        return lax.rem(self.y + step, CHIPS) * 2 + self.k

    def col_of(self, step):
        return lax.rem(self.x + step, 4) * 2 + self.h

    def col_from(self, step):
        return lax.rem(self.x + 4 - step, 4) * 2 + self.h


class RowGather:
    SEMS = 13

    def __init__(self, here, place, shard, send, recv):
        self.here, self.place = here, place
        y, k = here.y, here.k
        self.low, self.high, self.far_row = here.row_of(3), here.row_of(1), here.row_of(2)
        self.ups = [
            remote(shard(a), place(here.r, a), send.at[a], recv.at[a], here.up) for a in (0, 1)
        ]
        self.downs = [
            remote(shard(a), place(here.r, a), send.at[2 + a], recv.at[2 + a], here.down)
            for a in (0, 1)
        ]
        self.fars = [
            self.hand_on(self.low, 0, send.at[4], recv.at[4], here.up),
            self.hand_on(self.high, 1, send.at[5], recv.at[5], here.down),
        ]
        self.passes = {}
        for index, (row, a) in enumerate(
            [(self.low, 0), (self.low, 1), (self.high, 0), (self.high, 1), (self.far_row, 0), (self.far_row, 1)]
        ):
            self.passes[index] = self.hand_on(
                row, a, send.at[6 + index], recv.at[6 + index], here.partner
            )
        self.own = [
            remote(shard(None), place(here.r, None), send.at[12], recv.at[12], here.partner)
        ]

    def hand_on(self, row, a, send, recv, device):
        return remote(self.place(row, a), self.place(row, a), send, recv, device)

    def start(self):
        for a, b in ((0, 1), (1, 0)):
            self.ups[a].start()
            self.downs[b].start()
        self.own[0].start()

    def near(self):
        for a, b in ((0, 1), (1, 0)):
            self.ups[a].wait_recv()
            if a == 0:
                self.fars[0].start()
            self.passes[a].start()
            self.downs[b].wait_recv()
            if b == 1:
                self.fars[1].start()
            self.passes[2 + b].start()

    def far(self):
        for a in (0, 1):
            self.fars[a].wait_recv()
            self.passes[4 + a].start()

    def got_own(self):
        self.own[0].wait_recv()

    def got_near(self):
        for index in range(4):
            self.passes[index].wait_recv()

    def got_far(self):
        for index in (4, 5):
            self.passes[index].wait_recv()

    def sent(self):
        for copy in self.ups + self.downs + self.fars + self.own + list(self.passes.values()):
            copy.wait_send()


class ColGather:
    SEMS = 7

    def __init__(self, here, shard, place, send, recv, local, across_first):
        self.here, self.place, self.across_first = here, place, across_first
        self.local = pltpu.make_async_copy(shard, place(here.c), local)
        self.lines = [
            remote(shard, place(here.c), send.at[i], recv.at[i], here.x_peers[i]) for i in range(3)
        ]
        self.across = [remote(shard, place(here.c), send.at[3], recv.at[3], here.other)]
        there = here.x * 2 + 1 - here.h
        if across_first:
            self.seconds = [
                remote(place(there), place(there), send.at[4 + i], recv.at[4 + i], here.x_peers[i])
                for i in range(3)
            ]
        else:
            self.seconds = []
            for i, step in enumerate((1, 3, 2)):
                source = here.col_from(step)
                self.seconds.append(
                    remote(place(source), place(source), send.at[4 + i], recv.at[4 + i], here.other)
                )

    def start(self):
        self.local.start()
        if self.across_first:
            self.across[0].start()
        for copy in self.lines:
            copy.start()
        if not self.across_first:
            self.across[0].start()

    def middle(self):
        if self.across_first:
            self.across[0].wait_recv()
            for copy in self.seconds:
                copy.start()
        else:
            for copy, second in zip(self.lines, self.seconds):
                copy.wait_recv()
                second.start()

    def end(self):
        self.local.wait()
        if self.across_first:
            for copy in self.lines:
                copy.wait_recv()
        else:
            self.across[0].wait_recv()
        for copy in self.seconds:
            copy.wait_recv()
        for copy in self.lines + self.across + self.seconds:
            copy.wait_send()


class RowSum:
    SEMS = 10

    def __init__(self, here, blocks, paired, relayed, landed, send, recv):
        self.here, self.blocks, self.paired = here, blocks, paired
        self.relayed, self.landed = relayed, landed
        k, half = here.k, TOK // 2
        self.mine, self.half = k * TOK, half
        self.pairs = [
            remote(
                blocks.at[s, ds((1 - k) * TOK, TOK)], paired.at[s], send.at[s], recv.at[s], here.partner
            )
            for s in range(4)
        ]
        self.fars = [
            remote(self.part(2, 0), relayed.at[0], send.at[4], recv.at[4], here.up),
            remote(self.part(2, 1), relayed.at[1], send.at[5], recv.at[5], here.down),
        ]
        self.nears = {}
        for index, (s, a, device) in enumerate(
            [(1, 1, here.up), (3, 0, here.down), (1, 0, here.up), (3, 1, here.down)]
        ):
            slot = 0 if s == 1 else 1
            self.nears[s, a] = remote(
                self.part(s, a),
                landed.at[slot, pl.ds(a * half, half)],
                send.at[6 + index],
                recv.at[6 + index],
                device,
            )

    def part(self, s, a):
        return self.blocks.at[s, ds(self.mine + a * self.half, self.half)]

    def add(self, s, a, other):
        part = self.part(s, a)
        part[...] = (part[...].astype(F32) + other[...].astype(F32)).astype(BF16)

    def pair(self, s):
        self.pairs[s].start()

    def join(self, s):
        self.pairs[s].wait_recv()
        for a in (0, 1):
            self.add(s, a, self.paired.at[s, pl.ds(a * self.half, self.half)])

    def far(self):
        self.join(2)
        self.fars[0].start()
        self.fars[1].start()

    def near(self):
        self.join(1)
        self.nears[1, 1].start()
        self.join(3)
        self.nears[3, 0].start()

    def relay(self):
        self.fars[0].wait_recv()
        self.add(1, 0, self.relayed.at[0])
        self.nears[1, 0].start()
        self.fars[1].wait_recv()
        self.add(3, 1, self.relayed.at[1])
        self.nears[3, 1].start()

    def arrive(self):
        self.pairs[0].wait_recv()
        for copy in self.nears.values():
            copy.wait_recv()

    def total(self, start, rows):
        own = self.blocks[0, pl.ds(pl.multiple_of(self.mine + start, rows), rows)].astype(F32)
        here = pl.ds(pl.multiple_of(start, rows), rows)
        return (
            own
            + self.paired[0, here].astype(F32)
            + self.landed[0, here].astype(F32)
            + self.landed[1, here].astype(F32)
        )

    def sent(self):
        for copy in self.pairs + self.fars + list(self.nears.values()):
            copy.wait_send()


def nn(a, b):
    return jnp.dot(a, b, preferred_element_type=F32)


def nt(a, b):
    return lax.dot_general(a, b, (((1,), (1,)), ((), ())), preferred_element_type=F32)


def tn(a, b):
    return lax.dot_general(a, b, (((0,), (0,)), ((), ())), preferred_element_type=F32)


def swap_halves(values):
    width = values.shape[-1]
    lane = lax.broadcasted_iota(jnp.int32, values.shape, 1)
    return jnp.where(
        lax.rem(lane, HD) < HD // 2, pltpu.roll(values, width - HD // 2, 1), pltpu.roll(values, HD // 2, 1)
    )


def turn(values, cos, sin):
    return values * cos + swap_halves(values) * sin


def gain_row(gains, which):
    return jnp.concatenate([gains[pl.ds(8 * j + which, 1), :] for j in range(8)], axis=1)


def score_bias(seg_col, seg_row, first, rows, keys):
    row = lax.broadcasted_iota(jnp.int32, (rows, keys), 0) + first
    key = lax.broadcasted_iota(jnp.int32, (rows, keys), 1)
    same = seg_col[pl.ds(first, rows), 0:1] == seg_row[0:1, pl.ds(0, keys)]
    return jnp.where(same & (key <= row), 0.0, FLOOR_SCORE)


def forward_kernel(
    x_in,
    g_in,
    wp_in,
    wo_in,
    wg_in,
    wu_in,
    wd_in,
    gain_in,
    cos,
    sin,
    seg_col,
    seg_row,
    normed_out,
    x_mine_out,
    query_out,
    kv_out,
    mixed_out,
    totals_out,
    residual_out,
    normed_two_out,
    gate_out,
    up_out,
    act_out,
    wp_out,
    wo_out,
    wg_out,
    wu_out,
    wd_out,
    g_out,
    gain_out,
    x_all,
    normed,
    wp,
    wo,
    wg,
    wu,
    gains,
    query,
    kv,
    k_low,
    k_high,
    v_low,
    v_high,
    mixed,
    totals,
    blocks,
    paired,
    relayed,
    landed,
    residual,
    normed_two,
    gate,
    up,
    act,
    x_send,
    x_recv,
    g_send,
    g_recv,
    n_send,
    n_recv,
    s_send,
    s_recv,
    w_send,
    w_recv,
    w_local,
    keep_sem,
):
    here = Place()
    meet([here.partner, here.up, here.down, here.other] + here.x_peers)
    half = LEN // 2

    def columns_of(ref):
        def place(row, a):
            lanes = ds(row * FEAT, FEAT)
            return ref.at[:, lanes] if a is None else ref.at[pl.ds(a * half, half), lanes]

        return place

    def halves_of(ref):
        return lambda a: ref if a is None else ref.at[pl.ds(a * half, half)]

    def token_place(row, a):
        if a is None:
            return normed_two.at[ds(row * TOK, TOK)]
        return normed_two.at[ds(row * TOK + a * (TOK // 2), TOK // 2)]

    x_gather = RowGather(here, columns_of(x_all), halves_of(x_in), x_send, x_recv)
    g_gather = RowGather(here, columns_of(g_out), halves_of(g_in), g_send, g_recv)
    n_gather = RowGather(
        here, token_place, functools.partial(token_place, here.r), n_send, n_recv
    )

    def col_gather(index, shard, place, across_first):
        return ColGather(
            here, shard, place, w_send.at[index], w_recv.at[index], w_local.at[index], across_first
        )

    gain_gather = col_gather(0, gain_in, lambda c: gains.at[ds(c * 8, 8)], True)
    wp_gather = col_gather(1, wp_in, lambda c: wp.at[ds(c * FEAT, FEAT)], True)
    wo_gather = col_gather(2, wo_in, lambda c: wo.at[:, ds(c * FEAT, FEAT)], False)
    wg_gather = col_gather(3, wg_in, lambda c: wg.at[ds(c * FEAT, FEAT)], True)
    wu_gather = col_gather(4, wu_in, lambda c: wu.at[ds(c * FEAT, FEAT)], False)
    wd_gather = col_gather(5, wd_in, lambda c: wd_out.at[:, ds(c * FEAT, FEAT)], False)
    kept = []

    def keep(src, dst):
        copy = pltpu.make_async_copy(src, dst, keep_sem.at[len(kept)])
        copy.start()
        kept.append(copy)

    own_x = pltpu.make_async_copy(x_in, x_all.at[:, ds(here.r * FEAT, FEAT)], keep_sem.at[30])
    own_g = pltpu.make_async_copy(g_in, g_out.at[:, ds(here.r * FEAT, FEAT)], keep_sem.at[31])
    own_x.start()
    x_gather.start()
    gain_gather.start()
    wp_gather.start()
    wo_gather.start()
    own_g.start()
    gain_gather.middle()
    wp_gather.middle()
    x_gather.near()
    wo_gather.middle()
    wg_gather.start()
    x_gather.far()
    x_gather.got_own()
    x_gather.got_near()
    x_gather.got_far()
    own_x.wait()
    g_gather.start()
    wu_gather.start()
    gain_gather.end()
    gain_one = gain_row(gains, 0)

    def norm_rows(t, carry):
        rows = ds(t * 16, 16)
        values = x_all[rows, :].astype(F32)
        scale = lax.rsqrt(jnp.sum(values * values, axis=1, keepdims=True) * (1.0 / D) + EPSILON)
        normed[rows, :] = (values * scale * gain_one).astype(BF16)
        return carry

    lax.fori_loop(0, LEN // 16, norm_rows, 0)
    keep(normed, normed_out)
    keep(x_all.at[ds(here.r * TOK, TOK)], x_mine_out)
    wp_gather.end()
    keep(wp, wp_out)

    def project_rows(t, carry):
        rows = ds(t * 256, 256)
        projected = nn(normed[rows, :], wp[...])
        cos_rows, sin_rows = cos[rows, :], sin[rows, :]
        for p in range(2):
            pair = turn(projected[:, p * 128 : (p + 1) * 128], cos_rows, sin_rows)
            query[rows, pl.ds(p * 128, 128)] = (pair * HD**-0.5).astype(BF16)
        key_value = projected[:, 256:384]
        lane = lax.broadcasted_iota(jnp.int32, key_value.shape, 1)
        key = turn(key_value, cos_rows, sin_rows)
        both = jnp.where(lane < HD, key, key_value)
        kv[rows, :] = both.astype(BF16)
        key = jnp.where(lane < HD, both, 0.0)
        value = jnp.where(lane < HD, 0.0, both)
        k_low[rows, :] = key.astype(BF16)
        k_high[rows, :] = pltpu.roll(key, HD, 1).astype(BF16)
        v_high[rows, :] = value.astype(BF16)
        v_low[rows, :] = pltpu.roll(value, HD, 1).astype(BF16)
        return carry

    lax.fori_loop(0, LEN // 256, project_rows, 0)
    keep(query, query_out)
    keep(kv, kv_out)
    wg_gather.middle()

    for block in range(4):
        first, keys = block * 256, (block + 1) * 256
        rows = pl.ds(first, 256)
        bias = score_bias(seg_col, seg_row, first, 256, keys)

        def one_pair(p, carry):
            lanes = ds(p * 128, 128)
            pair = query[rows, lanes]
            lane = lax.broadcasted_iota(jnp.int32, (256, 128), 1)
            out = jnp.zeros((256, 128), F32)
            sums = carry
            for side, (key, value) in enumerate(((k_low, v_low), (k_high, v_high))):
                scores = nt(pair, key[pl.ds(0, keys), :]) + bias
                row_max = jnp.max(scores, axis=1, keepdims=True)
                exps = jnp.exp(scores - row_max)
                row_sum = jnp.sum(exps, axis=1, keepdims=True)
                out = out + nn(exps.astype(BF16), value[pl.ds(0, keys), :]) * (1.0 / row_sum)
                sums = jnp.where(lane == 2 * p + side, row_max + jnp.log(row_sum), sums)
            mixed[rows, lanes] = out.astype(BF16)
            return sums

        totals[rows, :] = lax.fori_loop(0, 2, one_pair, jnp.zeros((256, 128), F32))

    keep(mixed, mixed_out)
    keep(totals, totals_out)
    g_gather.near()
    wu_gather.middle()
    wo_gather.end()
    keep(wo, wo_out)
    row_sum = RowSum(here, blocks, paired, relayed, landed, s_send, s_recv)
    for s in (2, 1, 3, 0):
        rows = ds(lax.rem(here.y + s, CHIPS) * 256, 256)
        blocks[s] = nn(mixed[rows, :], wo[...]).astype(BF16)
        row_sum.pair(s)
    row_sum.far()
    row_sum.near()
    wd_gather.start()
    g_gather.far()
    row_sum.relay()
    row_sum.arrive()
    gain_two = gain_row(gains, 1)

    def residual_rows(t, carry):
        rows = ds(t * 16, 16)
        mine = ds(here.r * TOK + t * 16, 16)
        values = x_all[mine, :].astype(F32) + row_sum.total(t * 16, 16)
        residual[rows, :] = values
        scale = lax.rsqrt(jnp.sum(values * values, axis=1, keepdims=True) * (1.0 / D) + EPSILON)
        normed_two[mine, :] = (values * scale * gain_two).astype(BF16)
        return carry

    lax.fori_loop(0, TOK // 16, residual_rows, 0)
    n_gather.start()
    keep(residual, residual_out)
    wg_gather.end()
    wu_gather.end()
    keep(wg, wg_out)
    keep(wu, wu_out)

    def feed(s):
        rows = ds(lax.rem(here.y + s, CHIPS) * 256, 256)
        values = normed_two[rows, :]
        gate_rows = nn(values, wg[...])
        up_rows = nn(values, wu[...])
        gate[rows, :] = gate_rows.astype(BF16)
        up[rows, :] = up_rows.astype(BF16)
        act[rows, :] = (gate_rows * (1.0 / (1.0 + jnp.exp(-gate_rows))) * up_rows).astype(BF16)

    n_gather.got_own()
    feed(0)
    n_gather.near()
    wd_gather.middle()
    n_gather.got_near()
    feed(1)
    n_gather.far()
    feed(3)
    n_gather.got_far()
    feed(2)
    keep(normed_two, normed_two_out)
    keep(gate, gate_out)
    keep(up, up_out)
    keep(act, act_out)
    keep(gains, gain_out)
    g_gather.got_own()
    g_gather.got_near()
    g_gather.got_far()
    own_g.wait()
    wd_gather.end()
    for gather in (x_gather, g_gather, n_gather, row_sum):
        gather.sent()
    for copy in kept:
        copy.wait()


def forward_call(x, g, wp, wo, wg, wu, wd, gains, cos, sin, seg_col, seg_row):
    ff = wg.shape[1]
    any_space = pl.BlockSpec(memory_space=pl.ANY)
    vmem_space = pl.BlockSpec(memory_space=pltpu.VMEM)
    dma = pltpu.SemaphoreType.DMA

    def low(*shape):
        return jax.ShapeDtypeStruct(shape, BF16)

    def wide(*shape):
        return jax.ShapeDtypeStruct(shape, F32)

    outs = (
        low(LEN, D),
        low(TOK, D),
        low(LEN, 256),
        low(LEN, 128),
        low(LEN, 256),
        wide(LEN, 128),
        wide(TOK, D),
        low(LEN, D),
        low(LEN, ff),
        low(LEN, ff),
        low(LEN, ff),
        low(D, 384),
        low(256, D),
        low(D, ff),
        low(D, ff),
        low(ff, D),
        low(LEN, D),
        wide(64, 256),
    )

    def vmem(*shape, dtype=BF16):
        return pltpu.VMEM(shape, dtype)

    scratch = [
        vmem(LEN, D),
        vmem(LEN, D),
        vmem(D, 384),
        vmem(256, D),
        vmem(D, ff),
        vmem(D, ff),
        vmem(64, 256, dtype=F32),
        vmem(LEN, 256),
        vmem(LEN, 128),
        vmem(LEN, 128),
        vmem(LEN, 128),
        vmem(LEN, 128),
        vmem(LEN, 128),
        vmem(LEN, 256),
        vmem(LEN, 128, dtype=F32),
        vmem(4, 256, D),
        vmem(4, TOK, D),
        vmem(2, TOK // 2, D),
        vmem(2, TOK, D),
        vmem(TOK, D, dtype=F32),
        vmem(LEN, D),
        vmem(LEN, ff),
        vmem(LEN, ff),
        vmem(LEN, ff),
    ]
    scratch += [dma((RowGather.SEMS,))] * 6 + [dma((RowSum.SEMS,))] * 2
    scratch += [dma((6, ColGather.SEMS))] * 2 + [dma((6,)), dma((32,))]
    return pl.pallas_call(
        forward_kernel,
        out_shape=outs,
        in_specs=[any_space] * 8 + [vmem_space] * 4,
        out_specs=tuple(any_space for _ in outs),
        scratch_shapes=scratch,
        compiler_params=pltpu.CompilerParams(
            collective_id=0, has_side_effects=True, vmem_limit_bytes=VMEM_BYTES
        ),
        cost_estimate=pl.CostEstimate(flops=12 * 10**9, bytes_accessed=60 * 10**6, transcendentals=0),
        name="forward_layer",
    )(x, g, wp, wo, wg, wu, wd, gains, cos, sin, seg_col, seg_row)


def doc_positions(segments):
    places = jnp.arange(segments.shape[0], dtype=jnp.int32)
    change = jnp.concatenate([jnp.ones((1,), jnp.bool_), segments[1:] != segments[:-1]])
    return places - lax.cummax(jnp.where(change, places, 0), axis=0)


def rope_tables(positions):
    frequency = jnp.exp(jnp.arange(0, HD, 2, dtype=F32) * (-math.log(10000.0) / HD))
    angles = positions.astype(F32)[:, None] * frequency
    cos, sin = jnp.cos(angles), jnp.sin(angles)
    return (
        jnp.concatenate([cos, cos, cos, cos], axis=1),
        jnp.concatenate([-sin, sin, -sin, sin], axis=1),
    )


def transposed_blocks(values):
    size = lax.axis_size("row")
    pairs = [(a * size + b, b * size + a) for a in range(size) for b in range(size)]
    return lax.ppermute(values, ("row", "col"), pairs)


def partner_of(values):
    pairs = [(a, a ^ 1) for a in range(lax.axis_size("row"))]
    return lax.ppermute(values, "row", pairs)


def shuffle(values, cos, sin):
    turned = jnp.concatenate([values[..., HD // 2 :], values[..., : HD // 2]], axis=-1)
    return values * cos + turned * sin


def gather_rows(values, axis):
    return lax.all_gather(values, "row", axis=axis, tiled=True)


def sum_rows(values, axis):
    return lax.psum_scatter(values.astype(BF16), "row", scatter_dimension=axis, tiled=True)


def weight_sum(values, axis):
    part = lax.psum_scatter(values.astype(BF16), "col", scatter_dimension=axis, tiled=True)
    return lax.psum(part, "dp").astype(F32)


def norm_scale(values):
    return lax.rsqrt(jnp.mean(values * values, axis=1, keepdims=True) + EPSILON)


def norm_back(d_normed, values, scales, gain_vector):
    d_scaled = d_normed * gain_vector
    inner = jnp.mean(d_scaled * values, axis=1, keepdims=True)
    return scales * d_scaled - values * (scales * scales * scales * inner)


def attend_back(query, key, value, d_mixed, totals, segments):
    places = jnp.arange(key.shape[0], dtype=jnp.int32)
    allowed = (segments[:, None] == segments[None, :]) & (places[None, :] <= places[:, None])
    scores = jnp.einsum("qhd,kd->hqk", query, key, preferred_element_type=F32)
    scores = jnp.where(allowed[None], scores, FLOOR_SCORE)
    grads = d_mixed.reshape(query.shape)
    probs = jnp.exp(scores - totals)
    d_probs = jnp.einsum("qhd,kd->hqk", grads, value, preferred_element_type=F32)
    inner = jnp.sum(probs * d_probs, axis=-1, keepdims=True)
    d_scores = (probs * (d_probs - inner)).astype(BF16)
    d_query = jnp.einsum("hqk,kd->qhd", d_scores, key, preferred_element_type=F32) * HD ** (-0.5)
    d_key = jnp.einsum("hqk,qhd->kd", d_scores, query, preferred_element_type=F32)
    d_value = jnp.einsum("hqk,qhd->kd", probs.astype(BF16), grads, preferred_element_type=F32)
    return d_query, d_key, d_value


def body(
    hidden_in,
    segment_ids,
    attn_gain,
    w_query,
    w_key,
    w_value,
    w_out,
    mlp_gain,
    w_gate,
    w_up,
    w_down,
    grad_output,
):
    row = lax.axis_index("row")
    upper = row % 2 == 1
    query_width = w_query.shape[1]
    kv_width = w_key.shape[1]
    ff_width = w_gate.shape[1]
    head_count = query_width // HD
    segments = segment_ids.reshape(-1)
    cos, sin = rope_tables(doc_positions(segments))
    seg_col = jnp.broadcast_to(segments[:, None], (LEN, 128))
    seg_row = jnp.broadcast_to(segments[None, :], (8, LEN))
    gains = jnp.concatenate(
        [attn_gain[None], mlp_gain[None], jnp.zeros((6, attn_gain.shape[0]), F32)], axis=0
    )
    x_block = transposed_blocks(hidden_in)
    g_block = transposed_blocks(grad_output)
    kv_own = jnp.concatenate([w_key, w_value], axis=1)
    kv_other = partner_of(kv_own)
    kv_first = jnp.where(upper, kv_other, kv_own)
    kv_second = jnp.where(upper, kv_own, kv_other)
    w_project = jnp.concatenate(
        [
            w_query,
            kv_first[:, :kv_width],
            kv_second[:, :kv_width],
            kv_first[:, kv_width:],
            kv_second[:, kv_width:],
        ],
        axis=1,
    )
    (
        normed_one,
        x_mine,
        query,
        kv,
        mixed_low,
        totals,
        residual,
        normed_two,
        gate,
        up,
        activated,
        w_project,
        w_out_all,
        w_gate_all,
        w_up_all,
        w_down_all,
        grad_all,
        gains_all,
    ) = forward_call(
        x_block, g_block, w_project, w_out, w_gate, w_up, w_down, gains, cos, sin, seg_col, seg_row
    )
    gain_one = gains_all.reshape(8, 8, -1)[:, 0].reshape(1, -1)
    gain_two = gains_all.reshape(8, 8, -1)[:, 1].reshape(1, -1)
    gate, up = gate.astype(F32), up.astype(F32)
    sig = jax.nn.sigmoid(gate)
    query = query.reshape(LEN, head_count, HD)
    key, value = kv[:, :HD], kv[:, HD:]
    totals = totals[:, :head_count].T[..., None]
    x_mine = x_mine.astype(F32)
    scale_mine = norm_scale(x_mine)
    scale_two = norm_scale(residual)
    token_rows = TOK
    down = nn(activated, w_down_all)
    here = lax.dynamic_slice_in_dim(down, row * token_rows, token_rows, 0) + residual
    down = lax.dynamic_update_slice_in_dim(down, here, row * token_rows, 0)
    layer_output = transposed_blocks(sum_rows(down, 1))

    d_activated = nt(grad_all, w_down_all)
    grad_down = tn(activated, grad_all)
    d_gate = (d_activated * up * sig * (1.0 + gate * (1.0 - sig))).astype(BF16)
    d_up = (d_activated * (gate * sig)).astype(BF16)
    d_normed_two = sum_rows(nt(d_gate, w_gate_all) + nt(d_up, w_up_all), 0).astype(F32)
    grad_gate = tn(normed_two, d_gate)
    grad_up = tn(normed_two, d_up)
    d_gain_two = jnp.sum(d_normed_two * residual * scale_two, axis=0)
    grad_mine = lax.dynamic_slice_in_dim(grad_all, row * token_rows, token_rows, 0)
    d_residual = grad_mine.astype(F32) + norm_back(d_normed_two, residual, scale_two, gain_two)
    d_residual_all = gather_rows(d_residual.astype(BF16), 0)
    d_mixed = nt(d_residual_all, w_out_all).astype(BF16)
    grad_out_proj = tn(mixed_low, d_residual_all)
    d_query_rot, d_key_rot, d_value = attend_back(query, key, value, d_mixed, totals, segments)
    cos, sin = cos[:, :HD], sin[:, :HD]
    d_query = shuffle(d_query_rot, cos[:, None], -sin[:, None]).reshape(-1, query_width)
    d_key = shuffle(d_key_rot, cos, -sin)
    d_projected = jnp.concatenate([d_query, d_key, d_value], axis=1).astype(BF16)
    grad_project = tn(normed_one, d_projected)
    d_normed_one = sum_rows(nt(d_projected, w_project), 0).astype(F32)
    d_gain_one = jnp.sum(d_normed_one * x_mine * scale_mine, axis=0)
    grad_input = d_residual + norm_back(d_normed_one, x_mine, scale_mine, gain_one)
    grad_input = lax.all_to_all(
        grad_input.astype(BF16), "row", split_axis=1, concat_axis=0, tiled=True
    )
    grad_input = transposed_blocks(grad_input).astype(F32)

    d_gains = lax.psum_scatter(
        jnp.stack([d_gain_one, d_gain_two], axis=1), "col", scatter_dimension=0, tiled=True
    )
    d_gains = lax.psum(d_gains, ("dp", "row"))
    grad_down = weight_sum(grad_down, 1)
    grad_gate = weight_sum(grad_gate, 0)
    grad_up = weight_sum(grad_up, 0)
    grad_out_proj = weight_sum(grad_out_proj, 1)
    grad_project = lax.psum_scatter(
        grad_project.astype(BF16), "col", scatter_dimension=0, tiled=True
    )
    grad_kv = grad_project[:, query_width:].reshape(-1, 2, 2, kv_width)
    keep = jnp.where(upper, grad_kv[:, :, 1], grad_kv[:, :, 0])
    give = jnp.where(upper, grad_kv[:, :, 0], grad_kv[:, :, 1])
    grad_kv = (keep.astype(F32) + partner_of(give).astype(F32)).astype(BF16)
    grad_query, grad_kv = lax.psum((grad_project[:, :query_width], grad_kv), "dp")
    grad_kv = grad_kv.astype(F32)
    return (
        layer_output,
        grad_input,
        d_gains[:, 0],
        grad_query.astype(F32),
        grad_kv[:, 0],
        grad_kv[:, 1],
        grad_out_proj,
        d_gains[:, 1],
        grad_gate,
        grad_up,
        grad_down,
    )


def solution(mesh):
    return jax.shard_map(
        body,
        mesh=mesh,
        in_specs=(
            P(("dp", "row"), "col"),
            P(("dp", "col"), None),
            P("col"),
            P("col", "row"),
            P("col", "row"),
            P("col", "row"),
            P("row", "col"),
            P("col"),
            P("col", "row"),
            P("col", "row"),
            P("row", "col"),
            P(("dp", "row"), "col"),
        ),
        out_specs=(
            P(("dp", "row"), "col"),
            P(("dp", "row"), "col"),
            P("col"),
            P("col", "row"),
            P("col", "row"),
            P("col", "row"),
            P("row", "col"),
            P("col"),
            P("col", "row"),
            P("col", "row"),
            P("row", "col"),
        ),
        check_vma=False,
    )
```

```python
import functools
import math

import jax
import jax.numpy as jnp
from jax import lax
from jax.experimental import pallas as pl
from jax.experimental.pallas import tpu as pltpu
from jax.sharding import PartitionSpec as P

D = 2048
HD = 64
LEN = 1024
ROWS = 8
CHIPS = 4
TOK = LEN // ROWS
FEAT = D // 8
EPSILON = 1e-05
FLOOR_SCORE = -1e30
BF16 = jnp.bfloat16
F32 = jnp.float32
MESH = pl.DeviceIdType.MESH
VMEM_BYTES = 62 * 2**20


def remote(src, dst, send, recv, device):
    return pltpu.make_async_remote_copy(
        src_ref=src, dst_ref=dst, send_sem=send, recv_sem=recv, device_id=device, device_id_type=MESH
    )


def meet(peers):
    barrier = pltpu.get_barrier_semaphore()
    for peer in peers:
        pl.semaphore_signal(barrier, inc=1, device_id=peer, device_id_type=MESH)
    pl.semaphore_wait(barrier, len(peers))


def ds(start, size):
    return pl.ds(pl.multiple_of(start, size), size)


class Place:
    def __init__(self):
        self.d = lax.axis_index("dp")
        self.r = lax.axis_index("row")
        self.c = lax.axis_index("col")
        self.y, self.k = self.r // 2, lax.rem(self.r, 2)
        self.x, self.h = self.c // 2, lax.rem(self.c, 2)
        self.partner = {"row": self.y * 2 + 1 - self.k}
        self.up = {"row": self.row_of(1)}
        self.down = {"row": self.row_of(3)}
        self.other = {"dp": 1 - self.d, "col": self.x * 2 + 1 - self.h}
        self.x_peers = [{"col": self.col_of(s)} for s in (1, 3, 2)]

    def row_of(self, step):
        return lax.rem(self.y + step, CHIPS) * 2 + self.k

    def col_of(self, step):
        return lax.rem(self.x + step, 4) * 2 + self.h

    def col_from(self, step):
        return lax.rem(self.x + 4 - step, 4) * 2 + self.h


class RowGather:
    SEMS = 13

    def __init__(self, here, place, shard, send, recv):
        self.here, self.place = here, place
        y, k = here.y, here.k
        self.low, self.high, self.far_row = here.row_of(3), here.row_of(1), here.row_of(2)
        self.ups = [
            remote(shard(a), place(here.r, a), send.at[a], recv.at[a], here.up) for a in (0, 1)
        ]
        self.downs = [
            remote(shard(a), place(here.r, a), send.at[2 + a], recv.at[2 + a], here.down)
            for a in (0, 1)
        ]
        self.fars = [
            self.hand_on(self.low, 0, send.at[4], recv.at[4], here.up),
            self.hand_on(self.high, 1, send.at[5], recv.at[5], here.down),
        ]
        self.passes = {}
        for index, (row, a) in enumerate(
            [(self.low, 0), (self.low, 1), (self.high, 0), (self.high, 1), (self.far_row, 0), (self.far_row, 1)]
        ):
            self.passes[index] = self.hand_on(
                row, a, send.at[6 + index], recv.at[6 + index], here.partner
            )
        self.own = [
            remote(shard(None), place(here.r, None), send.at[12], recv.at[12], here.partner)
        ]

    def hand_on(self, row, a, send, recv, device):
        return remote(self.place(row, a), self.place(row, a), send, recv, device)

    def start(self):
        for a, b in ((0, 1), (1, 0)):
            self.ups[a].start()
            self.downs[b].start()
        self.own[0].start()

    def near(self):
        for a, b in ((0, 1), (1, 0)):
            self.ups[a].wait_recv()
            if a == 0:
                self.fars[0].start()
            self.passes[a].start()
            self.downs[b].wait_recv()
            if b == 1:
                self.fars[1].start()
            self.passes[2 + b].start()

    def far(self):
        for a in (0, 1):
            self.fars[a].wait_recv()
            self.passes[4 + a].start()

    def got_own(self):
        self.own[0].wait_recv()

    def got_near(self):
        for index in range(4):
            self.passes[index].wait_recv()

    def got_far(self):
        for index in (4, 5):
            self.passes[index].wait_recv()

    def sent(self):
        for copy in self.ups + self.downs + self.fars + self.own + list(self.passes.values()):
            copy.wait_send()


class ColGather:
    SEMS = 7

    def __init__(self, here, shard, place, send, recv, local, across_first):
        self.here, self.place, self.across_first = here, place, across_first
        self.local = pltpu.make_async_copy(shard, place(here.c), local)
        self.lines = [
            remote(shard, place(here.c), send.at[i], recv.at[i], here.x_peers[i]) for i in range(3)
        ]
        self.across = [remote(shard, place(here.c), send.at[3], recv.at[3], here.other)]
        there = here.x * 2 + 1 - here.h
        if across_first:
            self.seconds = [
                remote(place(there), place(there), send.at[4 + i], recv.at[4 + i], here.x_peers[i])
                for i in range(3)
            ]
        else:
            self.seconds = []
            for i, step in enumerate((1, 3, 2)):
                source = here.col_from(step)
                self.seconds.append(
                    remote(place(source), place(source), send.at[4 + i], recv.at[4 + i], here.other)
                )

    def start(self):
        self.local.start()
        if self.across_first:
            self.across[0].start()
        for copy in self.lines:
            copy.start()
        if not self.across_first:
            self.across[0].start()

    def middle(self):
        if self.across_first:
            self.across[0].wait_recv()
            for copy in self.seconds:
                copy.start()
        else:
            for copy, second in zip(self.lines, self.seconds):
                copy.wait_recv()
                second.start()

    def end(self):
        self.local.wait()
        if self.across_first:
            for copy in self.lines:
                copy.wait_recv()
        else:
            self.across[0].wait_recv()
        for copy in self.seconds:
            copy.wait_recv()
        for copy in self.lines + self.across + self.seconds:
            copy.wait_send()


class RowSum:
    SEMS = 10

    def __init__(self, here, blocks, paired, relayed, landed, send, recv):
        self.here, self.blocks, self.paired = here, blocks, paired
        self.relayed, self.landed = relayed, landed
        k, half = here.k, TOK // 2
        self.mine, self.half = k * TOK, half
        self.pairs = [
            remote(
                blocks.at[s, ds((1 - k) * TOK, TOK)], paired.at[s], send.at[s], recv.at[s], here.partner
            )
            for s in range(4)
        ]
        self.fars = [
            remote(self.part(2, 0), relayed.at[0], send.at[4], recv.at[4], here.up),
            remote(self.part(2, 1), relayed.at[1], send.at[5], recv.at[5], here.down),
        ]
        self.nears = {}
        for index, (s, a, device) in enumerate(
            [(1, 1, here.up), (3, 0, here.down), (1, 0, here.up), (3, 1, here.down)]
        ):
            slot = 0 if s == 1 else 1
            self.nears[s, a] = remote(
                self.part(s, a),
                landed.at[slot, pl.ds(a * half, half)],
                send.at[6 + index],
                recv.at[6 + index],
                device,
            )

    def part(self, s, a):
        return self.blocks.at[s, ds(self.mine + a * self.half, self.half)]

    def add(self, s, a, other):
        part = self.part(s, a)
        part[...] = (part[...].astype(F32) + other[...].astype(F32)).astype(BF16)

    def pair(self, s):
        self.pairs[s].start()

    def join(self, s):
        self.pairs[s].wait_recv()
        for a in (0, 1):
            self.add(s, a, self.paired.at[s, pl.ds(a * self.half, self.half)])

    def far(self):
        self.join(2)
        self.fars[0].start()
        self.fars[1].start()

    def near(self):
        self.join(1)
        self.nears[1, 1].start()
        self.join(3)
        self.nears[3, 0].start()

    def relay(self):
        self.fars[0].wait_recv()
        self.add(1, 0, self.relayed.at[0])
        self.nears[1, 0].start()
        self.fars[1].wait_recv()
        self.add(3, 1, self.relayed.at[1])
        self.nears[3, 1].start()

    def arrive(self):
        self.pairs[0].wait_recv()
        for copy in self.nears.values():
            copy.wait_recv()

    def total(self, start, rows):
        own = self.blocks[0, pl.ds(pl.multiple_of(self.mine + start, rows), rows)].astype(F32)
        here = pl.ds(pl.multiple_of(start, rows), rows)
        return (
            own
            + self.paired[0, here].astype(F32)
            + self.landed[0, here].astype(F32)
            + self.landed[1, here].astype(F32)
        )

    def sent(self):
        for copy in self.pairs + self.fars + list(self.nears.values()):
            copy.wait_send()


def nn(a, b):
    return jnp.dot(a, b, preferred_element_type=F32)


def nt(a, b):
    return lax.dot_general(a, b, (((1,), (1,)), ((), ())), preferred_element_type=F32)


def tn(a, b):
    return lax.dot_general(a, b, (((0,), (0,)), ((), ())), preferred_element_type=F32)


def swap_halves(values):
    width = values.shape[-1]
    lane = lax.broadcasted_iota(jnp.int32, values.shape, 1)
    return jnp.where(
        lax.rem(lane, HD) < HD // 2, pltpu.roll(values, width - HD // 2, 1), pltpu.roll(values, HD // 2, 1)
    )


def turn(values, cos, sin):
    return values * cos + swap_halves(values) * sin


def gain_row(gains, which):
    return jnp.concatenate([gains[pl.ds(8 * j + which, 1), :] for j in range(8)], axis=1)


def score_bias(seg_col, seg_row, first, rows, keys):
    row = lax.broadcasted_iota(jnp.int32, (rows, keys), 0) + first
    key = lax.broadcasted_iota(jnp.int32, (rows, keys), 1)
    same = seg_col[pl.ds(first, rows), 0:1] == seg_row[0:1, pl.ds(0, keys)]
    return jnp.where(same & (key <= row), 0.0, FLOOR_SCORE)


def forward_kernel(
    x_in,
    g_in,
    wp_in,
    wo_in,
    wg_in,
    wu_in,
    wd_in,
    gain_in,
    cos,
    sin,
    seg_col,
    seg_row,
    normed_out,
    x_mine_out,
    query_out,
    kv_out,
    mixed_out,
    totals_out,
    residual_out,
    normed_two_out,
    gate_out,
    up_out,
    act_out,
    wp_out,
    wo_out,
    wg_out,
    wu_out,
    wd_out,
    g_out,
    gain_out,
    x_all,
    normed,
    wp,
    wo,
    wg,
    wu,
    gains,
    query,
    kv,
    k_low,
    k_high,
    v_low,
    v_high,
    mixed,
    totals,
    blocks,
    paired,
    relayed,
    landed,
    residual,
    normed_two,
    gate,
    up,
    act,
    x_send,
    x_recv,
    g_send,
    g_recv,
    n_send,
    n_recv,
    s_send,
    s_recv,
    w_send,
    w_recv,
    w_local,
    keep_sem,
):
    here = Place()
    meet([here.partner, here.up, here.down, here.other] + here.x_peers)
    half = LEN // 2

    def columns_of(ref):
        def place(row, a):
            lanes = ds(row * FEAT, FEAT)
            return ref.at[:, lanes] if a is None else ref.at[pl.ds(a * half, half), lanes]

        return place

    def halves_of(ref):
        return lambda a: ref if a is None else ref.at[pl.ds(a * half, half)]

    def token_place(row, a):
        if a is None:
            return normed_two.at[ds(row * TOK, TOK)]
        return normed_two.at[ds(row * TOK + a * (TOK // 2), TOK // 2)]

    x_gather = RowGather(here, columns_of(x_all), halves_of(x_in), x_send, x_recv)
    g_gather = RowGather(here, columns_of(g_out), halves_of(g_in), g_send, g_recv)
    n_gather = RowGather(
        here, token_place, functools.partial(token_place, here.r), n_send, n_recv
    )

    def col_gather(index, shard, place, across_first):
        return ColGather(
            here, shard, place, w_send.at[index], w_recv.at[index], w_local.at[index], across_first
        )

    gain_gather = col_gather(0, gain_in, lambda c: gains.at[ds(c * 8, 8)], True)
    wp_gather = col_gather(1, wp_in, lambda c: wp.at[ds(c * FEAT, FEAT)], True)
    wo_gather = col_gather(2, wo_in, lambda c: wo.at[:, ds(c * FEAT, FEAT)], False)
    wg_gather = col_gather(3, wg_in, lambda c: wg.at[ds(c * FEAT, FEAT)], True)
    wu_gather = col_gather(4, wu_in, lambda c: wu.at[ds(c * FEAT, FEAT)], False)
    wd_gather = col_gather(5, wd_in, lambda c: wd_out.at[:, ds(c * FEAT, FEAT)], False)
    kept = []

    def keep(src, dst):
        copy = pltpu.make_async_copy(src, dst, keep_sem.at[len(kept)])
        copy.start()
        kept.append(copy)

    own_x = pltpu.make_async_copy(x_in, x_all.at[:, ds(here.r * FEAT, FEAT)], keep_sem.at[30])
    own_g = pltpu.make_async_copy(g_in, g_out.at[:, ds(here.r * FEAT, FEAT)], keep_sem.at[31])
    own_x.start()
    x_gather.start()
    gain_gather.start()
    wp_gather.start()
    wo_gather.start()
    own_g.start()
    gain_gather.middle()
    wp_gather.middle()
    x_gather.near()
    wo_gather.middle()
    wg_gather.start()
    x_gather.far()
    x_gather.got_own()
    x_gather.got_near()
    x_gather.got_far()
    own_x.wait()
    g_gather.start()
    wu_gather.start()
    gain_gather.end()
    gain_one = gain_row(gains, 0)

    def norm_rows(t, carry):
        rows = ds(t * 16, 16)
        values = x_all[rows, :].astype(F32)
        scale = lax.rsqrt(jnp.sum(values * values, axis=1, keepdims=True) * (1.0 / D) + EPSILON)
        normed[rows, :] = (values * scale * gain_one).astype(BF16)
        return carry

    lax.fori_loop(0, LEN // 16, norm_rows, 0)
    keep(normed, normed_out)
    keep(x_all.at[ds(here.r * TOK, TOK)], x_mine_out)
    wp_gather.end()
    keep(wp, wp_out)

    def project_rows(t, carry):
        rows = ds(t * 256, 256)
        projected = nn(normed[rows, :], wp[...])
        cos_rows, sin_rows = cos[rows, :], sin[rows, :]
        for p in range(2):
            pair = turn(projected[:, p * 128 : (p + 1) * 128], cos_rows, sin_rows)
            query[rows, pl.ds(p * 128, 128)] = (pair * HD**-0.5).astype(BF16)
        key_value = projected[:, 256:384]
        lane = lax.broadcasted_iota(jnp.int32, key_value.shape, 1)
        key = turn(key_value, cos_rows, sin_rows)
        both = jnp.where(lane < HD, key, key_value)
        kv[rows, :] = both.astype(BF16)
        key = jnp.where(lane < HD, both, 0.0)
        value = jnp.where(lane < HD, 0.0, both)
        k_low[rows, :] = key.astype(BF16)
        k_high[rows, :] = pltpu.roll(key, HD, 1).astype(BF16)
        v_high[rows, :] = value.astype(BF16)
        v_low[rows, :] = pltpu.roll(value, HD, 1).astype(BF16)
        return carry

    lax.fori_loop(0, LEN // 256, project_rows, 0)
    keep(query, query_out)
    keep(kv, kv_out)
    wg_gather.middle()

    for block in range(4):
        first, keys = block * 256, (block + 1) * 256
        rows = pl.ds(first, 256)
        bias = score_bias(seg_col, seg_row, first, 256, keys)

        def one_pair(p, carry):
            lanes = ds(p * 128, 128)
            pair = query[rows, lanes]
            lane = lax.broadcasted_iota(jnp.int32, (256, 128), 1)
            out = jnp.zeros((256, 128), F32)
            sums = carry
            for side, (key, value) in enumerate(((k_low, v_low), (k_high, v_high))):
                scores = nt(pair, key[pl.ds(0, keys), :]) + bias
                row_max = jnp.max(scores, axis=1, keepdims=True)
                exps = jnp.exp(scores - row_max)
                row_sum = jnp.sum(exps, axis=1, keepdims=True)
                out = out + nn(exps.astype(BF16), value[pl.ds(0, keys), :]) * (1.0 / row_sum)
                sums = jnp.where(lane == 2 * p + side, row_max + jnp.log(row_sum), sums)
            mixed[rows, lanes] = out.astype(BF16)
            return sums

        totals[rows, :] = lax.fori_loop(0, 2, one_pair, jnp.zeros((256, 128), F32))

    keep(mixed, mixed_out)
    keep(totals, totals_out)
    g_gather.near()
    wu_gather.middle()
    wo_gather.end()
    keep(wo, wo_out)
    row_sum = RowSum(here, blocks, paired, relayed, landed, s_send, s_recv)
    for s in (2, 1, 3, 0):
        rows = ds(lax.rem(here.y + s, CHIPS) * 256, 256)
        blocks[s] = nn(mixed[rows, :], wo[...]).astype(BF16)
        row_sum.pair(s)
    row_sum.far()
    row_sum.near()
    wd_gather.start()
    g_gather.far()
    row_sum.relay()
    row_sum.arrive()
    gain_two = gain_row(gains, 1)

    def residual_rows(t, carry):
        rows = ds(t * 16, 16)
        mine = ds(here.r * TOK + t * 16, 16)
        values = x_all[mine, :].astype(F32) + row_sum.total(t * 16, 16)
        residual[rows, :] = values
        scale = lax.rsqrt(jnp.sum(values * values, axis=1, keepdims=True) * (1.0 / D) + EPSILON)
        normed_two[mine, :] = (values * scale * gain_two).astype(BF16)
        return carry

    lax.fori_loop(0, TOK // 16, residual_rows, 0)
    n_gather.start()
    keep(residual, residual_out)
    wg_gather.end()
    wu_gather.end()
    keep(wg, wg_out)
    keep(wu, wu_out)

    def feed(s):
        rows = ds(lax.rem(here.y + s, CHIPS) * 256, 256)
        values = normed_two[rows, :]
        gate_rows = nn(values, wg[...])
        up_rows = nn(values, wu[...])
        gate[rows, :] = gate_rows.astype(BF16)
        up[rows, :] = up_rows.astype(BF16)
        act[rows, :] = (gate_rows * (1.0 / (1.0 + jnp.exp(-gate_rows))) * up_rows).astype(BF16)

    n_gather.got_own()
    feed(0)
    n_gather.near()
    wd_gather.middle()
    n_gather.got_near()
    feed(1)
    n_gather.far()
    feed(3)
    n_gather.got_far()
    feed(2)
    keep(normed_two, normed_two_out)
    keep(gate, gate_out)
    keep(up, up_out)
    keep(act, act_out)
    keep(gains, gain_out)
    g_gather.got_own()
    g_gather.got_near()
    g_gather.got_far()
    own_g.wait()
    wd_gather.end()
    for gather in (x_gather, g_gather, n_gather, row_sum):
        gather.sent()
    for copy in kept:
        copy.wait()


def forward_call(x, g, wp, wo, wg, wu, wd, gains, cos, sin, seg_col, seg_row):
    ff = wg.shape[1]
    any_space = pl.BlockSpec(memory_space=pl.ANY)
    vmem_space = pl.BlockSpec(memory_space=pltpu.VMEM)
    dma = pltpu.SemaphoreType.DMA

    def low(*shape):
        return jax.ShapeDtypeStruct(shape, BF16)

    def wide(*shape):
        return jax.ShapeDtypeStruct(shape, F32)

    outs = (
        low(LEN, D),
        low(TOK, D),
        low(LEN, 256),
        low(LEN, 128),
        low(LEN, 256),
        wide(LEN, 128),
        wide(TOK, D),
        low(LEN, D),
        low(LEN, ff),
        low(LEN, ff),
        low(LEN, ff),
        low(D, 384),
        low(256, D),
        low(D, ff),
        low(D, ff),
        low(ff, D),
        low(LEN, D),
        wide(64, 256),
    )

    def vmem(*shape, dtype=BF16):
        return pltpu.VMEM(shape, dtype)

    scratch = [
        vmem(LEN, D),
        vmem(LEN, D),
        vmem(D, 384),
        vmem(256, D),
        vmem(D, ff),
        vmem(D, ff),
        vmem(64, 256, dtype=F32),
        vmem(LEN, 256),
        vmem(LEN, 128),
        vmem(LEN, 128),
        vmem(LEN, 128),
        vmem(LEN, 128),
        vmem(LEN, 128),
        vmem(LEN, 256),
        vmem(LEN, 128, dtype=F32),
        vmem(4, 256, D),
        vmem(4, TOK, D),
        vmem(2, TOK // 2, D),
        vmem(2, TOK, D),
        vmem(TOK, D, dtype=F32),
        vmem(LEN, D),
        vmem(LEN, ff),
        vmem(LEN, ff),
        vmem(LEN, ff),
    ]
    scratch += [dma((RowGather.SEMS,))] * 6 + [dma((RowSum.SEMS,))] * 2
    scratch += [dma((6, ColGather.SEMS))] * 2 + [dma((6,)), dma((32,))]
    return pl.pallas_call(
        forward_kernel,
        out_shape=outs,
        in_specs=[any_space] * 8 + [vmem_space] * 4,
        out_specs=tuple(any_space for _ in outs),
        scratch_shapes=scratch,
        compiler_params=pltpu.CompilerParams(
            collective_id=0, has_side_effects=True, vmem_limit_bytes=VMEM_BYTES
        ),
        cost_estimate=pl.CostEstimate(flops=12 * 10**9, bytes_accessed=60 * 10**6, transcendentals=0),
        name="forward_layer",
    )(x, g, wp, wo, wg, wu, wd, gains, cos, sin, seg_col, seg_row)


class WeightSum:
    SEMS = 8

    def __init__(self, here, part, wide_part, rows, z_land, x_land, far_part, send, recv, across_first):
        self.here, self.part, self.across_first, self.rows = here, part, across_first, rows
        self.z_land, self.x_land = z_land, x_land
        self.own = part(here.c)
        steps = (1, 3, 2)
        if across_first:
            self.mine = [part(x * 2 + here.h) for x in range(4)]
            self.across = [
                remote(part(x * 2 + 1 - here.h), z_land.at[x], send.at[x], recv.at[x], here.other)
                for x in range(4)
            ]
            self.lines = [
                remote(
                    part(here.col_of(step)), x_land.at[i], send.at[4 + i], recv.at[4 + i], here.x_peers[i]
                )
                for i, step in enumerate(steps)
            ]
        else:
            self.wide = wide_part(here.x)
            self.across = [
                remote(
                    part(here.x * 2 + 1 - here.h), z_land, send.at[3], recv.at[3], here.other
                )
            ]
            self.lines = [
                remote(
                    wide_part(lax.rem(here.x + step, 4)),
                    x_land.at[i],
                    send.at[i],
                    recv.at[i],
                    here.x_peers[i],
                )
                for i, step in enumerate(steps)
            ]
        self.swap = remote(self.own, far_part, send.at[7], recv.at[7], {"dp": 1 - here.d})

    def add(self, target, others):
        rows = self.rows
        kind = target.dtype

        def step(t, carry):
            at = ds(t * rows, rows)
            total = target[at, :].astype(F32)
            for other in others:
                total = total + other[at, :].astype(F32)
            target[at, :] = total.astype(kind)
            return carry

        lax.fori_loop(0, target.shape[0] // rows, step, 0)

    def start(self):
        for copy in self.across if self.across_first else self.lines:
            copy.start()

    def middle(self):
        if self.across_first:
            for x in range(4):
                self.across[x].wait_recv()
                self.add(self.mine[x], [self.z_land.at[x]])
            for copy in self.lines:
                copy.start()
        else:
            for copy in self.lines:
                copy.wait_recv()
            self.add(self.wide, [self.x_land.at[i] for i in range(3)])
            self.across[0].start()

    def last(self):
        if self.across_first:
            for copy in self.lines:
                copy.wait_recv()
            self.add(self.own, [self.x_land.at[i] for i in range(3)])
        else:
            self.across[0].wait_recv()
            self.add(self.own, [self.z_land])
        self.swap.start()

    def end(self):
        self.swap.wait()
        for copy in self.across + self.lines:
            copy.wait_send()


class Spread:
    def __init__(self, here, source, target, send, recv, local):
        self.here = here
        self.same = here.r == here.c
        self.copies = []
        place = target.at[ds(here.r * TOK, TOK)]
        for j in range(8):
            shard = source.at[:, pl.ds(j * FEAT, FEAT)]
            self.copies.append(
                (
                    remote(shard, place, send.at[j], recv.at[here.r], {"row": here.c, "col": j}),
                    pltpu.make_async_copy(shard, place, local),
                )
            )
        self.arrivals = [
            remote(
                source.at[:, pl.ds(0, FEAT)],
                target.at[pl.ds(i * TOK, TOK)],
                send.at[i],
                recv.at[i],
                {"row": here.c, "col": i},
            )
            for i in range(8)
        ]

    def each(self, index, other, own):
        itself = self.same & (self.here.r == index)
        pl.when(itself)(own)
        pl.when(jnp.logical_not(itself))(other)

    def start(self):
        for j, (copy, local) in enumerate(self.copies):
            self.each(j, copy.start, local.start)

    def end(self):
        for j, (copy, local) in enumerate(self.copies):
            self.each(j, copy.wait_send, local.wait)
        for i, copy in enumerate(self.arrivals):
            self.each(i, copy.wait_recv, lambda: None)


def backward_kernel(
    g_in,
    act_in,
    gate_in,
    up_in,
    wd_in,
    wg_in,
    wu_in,
    n2_in,
    residual_in,
    query_in,
    kv_in,
    mixed_in,
    totals_in,
    wo_in,
    wp_in,
    n1_in,
    x_in,
    gain_in,
    cos,
    sin,
    seg_col,
    seg_row,
    layer_out,
    input_out,
    gd_own,
    gd_far,
    gg_own,
    gg_far,
    gu_own,
    gu_far,
    go_own,
    go_far,
    gp_own,
    gp_far,
    kv_own,
    kv_far,
    gains_out,
    g_all,
    act,
    gate,
    up,
    wd,
    gd,
    wg,
    wu,
    wide_in,
    wo,
    wp,
    blocks,
    paired,
    relayed,
    landed,
    residual,
    d_residual,
    low_rows,
    x_mine,
    gains,
    gain_sums,
    gain_x,
    gain_z,
    gain_far,
    gain_rows,
    query,
    kv,
    k_low,
    k_high,
    v_low,
    v_high,
    mixed,
    totals,
    d_mixed,
    d_projected,
    dk_low,
    dk_high,
    dv_low,
    dv_high,
    gd_z,
    gd_x,
    gg_z,
    gg_x,
    gu_z,
    gu_x,
    go_z,
    go_x,
    gp_z,
    gp_x,
    sums_send,
    sums_recv,
    a_send,
    a_recv,
    w_send,
    w_recv,
    t_send,
    t_recv,
    t_local,
    r_send,
    r_recv,
    p_send,
    p_recv,
    load_sem,
    keep_sem,
    free,
):
    here = Place()
    barrier = pltpu.get_barrier_semaphore()
    row_peers = [{"row": lax.rem(here.r + k, ROWS)} for k in range(1, ROWS)]
    peers = row_peers + [here.other, {"dp": 1 - here.d}] + here.x_peers
    for peer in peers:
        pl.semaphore_signal(barrier, inc=1, device_id=peer, device_id_type=MESH)
    same = here.r == here.c
    for i in range(8):

        @pl.when(jnp.logical_not(same & (here.r == i)))
        def _():
            pl.semaphore_signal(
                barrier, inc=1, device_id={"row": i, "col": here.r}, device_id_type=MESH
            )

    loads = []

    def load(src, dst):
        copy = pltpu.make_async_copy(src, dst, load_sem.at[len(loads)])
        copy.start()
        loads.append(copy)
        return copy

    kept = []

    def keep(src, dst):
        copy = pltpu.make_async_copy(src, dst, keep_sem.at[len(kept)])
        copy.start()
        kept.append(copy)

    first_loads = [
        load(wd_in, wd),
        load(g_in, g_all),
        load(gate_in, gate),
        load(up_in, up),
        load(wg_in, wg),
        load(wu_in, wu),
    ]
    second_loads = [
        load(act_in, act),
        load(n2_in, wide_in),
        load(residual_in, residual),
        load(gain_in, gains),
        load(x_in, x_mine),
        load(wo_in, wo),
        load(wp_in, wp),
        load(query_in, query),
        load(kv_in, kv),
        load(mixed_in, mixed),
        load(totals_in, totals),
    ]
    pl.semaphore_wait(barrier, len(peers) + 8 - same.astype(jnp.int32))

    def token_place(row, a):
        if a is None:
            return g_all.at[ds(row * TOK, TOK)]
        return g_all.at[ds(row * TOK + a * (TOK // 2), TOK // 2)]

    def low_part(a):
        return low_rows if a is None else low_rows.at[pl.ds(a * (TOK // 2), TOK // 2)]

    def row_sum_of(index):
        return RowSum(
            here, blocks, paired, relayed, landed, sums_send.at[index], sums_recv.at[index]
        )

    def credit(index):
        for peer in (here.partner, here.up, here.down):
            pl.semaphore_signal(free.at[index], inc=1, device_id=peer, device_id_type=MESH)

    def rows_of(ref):
        return lambda c: ref.at[ds(c * FEAT, FEAT)], lambda x: ref.at[ds(x * 2 * FEAT, 2 * FEAT)]

    def lanes_of(ref):
        return (
            lambda c: ref.at[:, ds(c * FEAT, FEAT)],
            lambda x: ref.at[:, ds(x * 2 * FEAT, 2 * FEAT)],
        )

    def weight_sum(index, parts, rows, z_land, x_land, far_part, across_first):
        return WeightSum(
            here,
            parts[0],
            parts[1],
            rows,
            z_land,
            x_land,
            far_part,
            w_send.at[index],
            w_recv.at[index],
            across_first,
        )

    d_sum = weight_sum(0, lanes_of(gd), 64, gd_z, gd_x, gd_far, True)
    g_sum = weight_sum(1, rows_of(wg), 32, gg_z, gg_x, gg_far, True)
    u_sum = weight_sum(2, rows_of(wu), 32, gu_z, gu_x, gu_far, False)
    o_sum = weight_sum(3, lanes_of(wo), 32, go_z, go_x, go_far, False)
    p_sum = weight_sum(4, rows_of(wp), 32, gp_z, gp_x, gp_far, False)
    gain_sum = weight_sum(5, lanes_of(gain_sums), 8, gain_z, gain_x, gain_far, False)
    gather = RowGather(here, token_place, low_part, a_send, a_recv)

    for copy in first_loads:
        copy.wait()
    first_sum = row_sum_of(0)
    for s in (2, 1, 3, 0):
        rows = ds(lax.rem(here.y + s, CHIPS) * 256, 256)
        d_act = nt(g_all[rows, :], wd[...])
        gate_rows = gate[rows, :].astype(F32)
        up_rows = up[rows, :].astype(F32)
        sig = 1.0 / (1.0 + jnp.exp(-gate_rows))
        d_up = (d_act * (gate_rows * sig)).astype(BF16)
        d_gate = (d_act * up_rows * (sig * (1.0 + gate_rows * (1.0 - sig)))).astype(BF16)
        gate[rows, :] = d_gate
        up[rows, :] = d_up
        blocks[s] = (nt(d_gate, wg[...]) + nt(d_up, wu[...])).astype(BF16)
        first_sum.pair(s)
        if s == 1:
            first_sum.far()
    first_sum.near()
    for copy in second_loads:
        copy.wait()

    def down_grad(j, carry):
        lanes = ds(j * 512, 512)
        gd[:, lanes] = tn(act[...], g_all[:, lanes]).astype(BF16)
        return carry

    lax.fori_loop(0, 4, down_grad, 0)
    d_sum.start()

    def keep_grad(t, carry):
        rows = ds(t * 16, 16)
        low_rows[rows, :] = g_all[ds(here.r * TOK + t * 16, 16), :]
        return carry

    lax.fori_loop(0, TOK // 16, keep_grad, 0)
    credit(0)
    first_sum.relay()

    def gate_grad(j, carry):
        lanes = ds(j * 512, 512)
        wg[lanes, :] = tn(wide_in[:, lanes], gate[...]).astype(BF16)
        return carry

    lax.fori_loop(0, 4, gate_grad, 0)
    g_sum.start()

    def up_grad(j, carry):
        lanes = ds(j * 512, 512)
        wu[lanes, :] = tn(wide_in[:, lanes], up[...]).astype(BF16)
        return carry

    lax.fori_loop(0, 4, up_grad, 0)
    u_sum.start()
    n1_load = load(n1_in, wide_in)
    first_sum.arrive()
    gain_sums[...] = jnp.zeros_like(gain_sums)

    def norm_back_rows(total, values, gain, which, t):
        scale = lax.rsqrt(jnp.sum(values * values, axis=1, keepdims=True) * (1.0 / D) + EPSILON)
        scaled = total * gain
        inner = jnp.sum(scaled * values, axis=1, keepdims=True) * (1.0 / D)
        part = jnp.sum(total * values * scale, axis=0, keepdims=True)
        gain_sums[pl.ds(which, 1), :] = gain_sums[pl.ds(which, 1), :] + part
        return scale * scaled - values * (scale * scale * scale * inner)

    gain_two = gain_row(gains, 1)

    def residual_rows(t, carry):
        rows = ds(t * 16, 16)
        back = norm_back_rows(first_sum.total(t * 16, 16), residual[rows, :], gain_two, 1, t)
        total = low_rows[rows, :].astype(F32) + back
        d_residual[rows, :] = total
        low_rows[rows, :] = total.astype(BF16)
        return carry

    lax.fori_loop(0, TOK // 16, residual_rows, 0)
    credit(1)
    pl.semaphore_wait(free.at[0], 3)
    own_rows = pltpu.make_async_copy(low_rows, token_place(here.r, None), keep_sem.at[15])
    own_rows.start()
    gather.start()
    first_sum.sent()
    layer_sum = row_sum_of(1)

    def down_block(s):
        rows = ds(lax.rem(here.y + s, CHIPS) * 256, 256)
        blocks[s] = nn(act[rows, :], wd[...]).astype(BF16)

    for s in (2, 1):
        down_block(s)
    gather.near()
    for s in (3, 0):
        down_block(s)
    pl.semaphore_wait(free.at[1], 3)
    for s in (2, 1, 3, 0):
        layer_sum.pair(s)
    gather.far()
    d_sum.middle()
    layer_sum.far()

    def mix_back(s):
        rows = ds(lax.rem(here.y + s, CHIPS) * 256, 256)
        d_mixed[rows, :] = nt(g_all[rows, :], wo[...]).astype(BF16)

    own_rows.wait()
    gather.got_own()
    mix_back(0)
    gather.got_near()
    mix_back(1)
    mix_back(3)
    gather.got_far()
    mix_back(2)

    def out_grad(j, carry):
        lanes = ds(j * 512, 512)
        wo[:, lanes] = tn(mixed[...], g_all[:, lanes]).astype(BF16)
        return carry

    lax.fori_loop(0, 4, out_grad, 0)
    o_sum.start()
    layer_sum.near()
    u_sum.middle()

    lane = lax.broadcasted_iota(jnp.int32, (256, 128), 1)

    def split_rows(t, carry):
        rows = ds(t * 256, 256)
        both = kv[rows, :].astype(F32)
        key = jnp.where(lane < HD, both, 0.0)
        value = jnp.where(lane < HD, 0.0, both)
        k_low[rows, :] = key.astype(BF16)
        k_high[rows, :] = pltpu.roll(key, HD, 1).astype(BF16)
        v_high[rows, :] = value.astype(BF16)
        v_low[rows, :] = pltpu.roll(value, HD, 1).astype(BF16)
        return carry

    lax.fori_loop(0, 4, split_rows, 0)
    for sums in (dk_low, dk_high, dv_low, dv_high):
        sums[...] = jnp.zeros_like(sums)

    def attend_back(block):
        first, keys = block * 256, (block + 1) * 256
        rows = pl.ds(first, 256)
        seen = pl.ds(0, keys)
        bias = score_bias(seg_col, seg_row, first, 256, keys)
        cos_rows, sin_rows = cos[rows, :], sin[rows, :]

        def one_pair(p, carry):
            lanes = ds(p * 128, 128)
            pair = query[rows, lanes]
            grads = d_mixed[rows, lanes]
            product = grads.astype(F32) * mixed[rows, lanes].astype(F32)
            out = jnp.zeros((256, 128), F32)
            for side, (key, value, dk, dv) in enumerate(
                ((k_low, v_low, dk_low, dv_low), (k_high, v_high, dk_high, dv_high))
            ):
                half = (lane < HD) if side == 0 else (lane >= HD)
                inner = jnp.sum(jnp.where(half, product, 0.0), axis=1, keepdims=True)
                total = jnp.sum(
                    jnp.where(lane == 2 * p + side, totals[rows, :], 0.0), axis=1, keepdims=True
                )
                probs = jnp.exp(nt(pair, key[seen, :]) + bias - total)
                d_probs = nt(grads, value[seen, :])
                d_scores = (probs * (d_probs - inner)).astype(BF16)
                out = out + nn(d_scores, key[seen, :])
                dk[seen, :] = dk[seen, :] + tn(d_scores, pair)
                dv[seen, :] = dv[seen, :] + tn(probs.astype(BF16), grads)
            d_projected[rows, lanes] = turn(out * HD**-0.5, cos_rows, -sin_rows).astype(BF16)
            return carry

        lax.fori_loop(0, 2, one_pair, 0)

    attend_back(3)
    layer_sum.relay()
    attend_back(2)
    attend_back(1)
    attend_back(0)

    def key_rows(t, carry):
        rows = ds(t * 256, 256)
        key = dk_low[rows, :] + pltpu.roll(dk_high[rows, :], HD, 1)
        value = dv_high[rows, :] + pltpu.roll(dv_low[rows, :], HD, 1)
        key = turn(key, cos[rows, :], -sin[rows, :])
        d_projected[rows, pl.ds(256, 128)] = jnp.where(lane < HD, key, value).astype(BF16)
        return carry

    lax.fori_loop(0, 4, key_rows, 0)
    layer_sum.arrive()

    def layer_rows(t, carry):
        rows = ds(t * 16, 16)
        low_rows[rows, :] = (residual[rows, :] + layer_sum.total(t * 16, 16)).astype(BF16)
        return carry

    gather.sent()
    lax.fori_loop(0, TOK // 16, layer_rows, 0)
    credit(2)
    layer_spread = Spread(here, low_rows, layer_out, t_send.at[0], t_recv.at[0], t_local.at[0])
    layer_spread.start()
    layer_sum.sent()
    last_sum = row_sum_of(2)
    pl.semaphore_wait(free.at[2], 3)
    for s in (2, 1, 3, 0):
        rows = ds(lax.rem(here.y + s, CHIPS) * 256, 256)
        blocks[s] = nt(d_projected[rows, :], wp[...]).astype(BF16)
        last_sum.pair(s)
    last_sum.far()
    last_sum.near()
    n1_load.wait()

    def project_grad(j, carry):
        lanes = ds(j * 512, 512)
        wp[lanes, :] = tn(wide_in[:, lanes], d_projected[...]).astype(BF16)
        return carry

    lax.fori_loop(0, 4, project_grad, 0)
    p_sum.start()
    g_sum.middle()
    last_sum.relay()
    o_sum.middle()
    d_sum.last()
    u_sum.last()
    layer_spread.end()
    last_sum.arrive()
    gain_one = gain_row(gains, 0)

    def input_rows(t, carry):
        rows = ds(t * 16, 16)
        values = x_mine[rows, :].astype(F32)
        back = norm_back_rows(last_sum.total(t * 16, 16), values, gain_one, 0, t)
        low_rows[rows, :] = (d_residual[rows, :] + back).astype(BF16)
        return carry

    lax.fori_loop(0, TOK // 16, input_rows, 0)
    input_spread = Spread(here, low_rows, input_out, t_send.at[1], t_recv.at[1], t_local.at[1])
    input_spread.start()
    gain_sum.start()
    p_sum.middle()
    gain_sum.middle()
    o_sum.last()
    g_sum.last()
    gain_sum.last()
    p_sum.last()
    gain_sum.end()
    gain_rows[here.r] = gain_sum.own[...] + gain_far[...]
    row_copies = [
        remote(gain_rows.at[here.r], gain_rows.at[here.r], r_send.at[k], r_recv.at[k], row_peers[k])
        for k in range(7)
    ]
    for copy in row_copies:
        copy.start()
    keep(d_sum.own, gd_own)
    keep(g_sum.own, gg_own)
    keep(u_sum.own, gu_own)
    keep(o_sum.own, go_own)
    keep(p_sum.own, gp_own)
    key_lanes = pl.ds(256, 128)
    own_copy = remote(
        p_sum.own.at[:, key_lanes], kv_own, p_send.at[0], p_recv.at[0], here.partner
    )
    own_copy.start()
    p_sum.end()
    far_copy = remote(gp_far.at[:, key_lanes], kv_far, p_send.at[1], p_recv.at[1], here.partner)
    far_copy.start()
    for sums in (d_sum, g_sum, u_sum, o_sum):
        sums.end()
    for copy in row_copies:
        copy.wait()
    total = gain_rows[0]
    for r in range(1, 8):
        total = total + gain_rows[r]
    gain_rows[0] = total
    keep(gain_rows.at[0], gains_out)
    input_spread.end()
    own_copy.wait()
    far_copy.wait()
    last_sum.sent()
    for copy in kept:
        copy.wait()


def backward_call(*args):
    ff = args[1].shape[1]
    any_space = pl.BlockSpec(memory_space=pl.ANY)
    vmem_space = pl.BlockSpec(memory_space=pltpu.VMEM)
    dma = pltpu.SemaphoreType.DMA

    def low(*shape):
        return jax.ShapeDtypeStruct(shape, BF16)

    outs = (
        low(LEN, FEAT),
        low(LEN, FEAT),
        low(ff, FEAT),
        low(ff, FEAT),
        low(FEAT, ff),
        low(FEAT, ff),
        low(FEAT, ff),
        low(FEAT, ff),
        low(256, FEAT),
        low(256, FEAT),
        low(FEAT, 384),
        low(FEAT, 384),
        low(FEAT, 128),
        low(FEAT, 128),
        jax.ShapeDtypeStruct((8, FEAT), F32),
    )

    def vmem(*shape, dtype=BF16):
        return pltpu.VMEM(shape, dtype)

    scratch = [
        vmem(LEN, D),
        vmem(LEN, ff),
        vmem(LEN, ff),
        vmem(LEN, ff),
        vmem(ff, D),
        vmem(ff, D),
        vmem(D, ff),
        vmem(D, ff),
        vmem(LEN, D),
        vmem(256, D),
        vmem(D, 384),
        vmem(4, 256, D),
        vmem(4, TOK, D),
        vmem(2, TOK // 2, D),
        vmem(2, TOK, D),
        vmem(TOK, D, dtype=F32),
        vmem(TOK, D, dtype=F32),
        vmem(TOK, D),
        vmem(TOK, D),
        vmem(64, 256, dtype=F32),
        vmem(8, D, dtype=F32),
        vmem(3, 8, 2 * FEAT, dtype=F32),
        vmem(8, FEAT, dtype=F32),
        vmem(8, FEAT, dtype=F32),
        vmem(8, 8, FEAT, dtype=F32),
        vmem(LEN, 256),
        vmem(LEN, 128),
        vmem(LEN, 128),
        vmem(LEN, 128),
        vmem(LEN, 128),
        vmem(LEN, 128),
        vmem(LEN, 256),
        vmem(LEN, 128, dtype=F32),
        vmem(LEN, 256),
        vmem(LEN, 384),
        vmem(LEN, 128, dtype=F32),
        vmem(LEN, 128, dtype=F32),
        vmem(LEN, 128, dtype=F32),
        vmem(LEN, 128, dtype=F32),
        vmem(4, ff, FEAT),
        vmem(3, ff, FEAT),
        vmem(4, FEAT, ff),
        vmem(3, FEAT, ff),
        vmem(FEAT, ff),
        vmem(3, 2 * FEAT, ff),
        vmem(256, FEAT),
        vmem(3, 256, 2 * FEAT),
        vmem(FEAT, 384),
        vmem(3, 2 * FEAT, 384),
        dma((3, RowSum.SEMS)),
        dma((3, RowSum.SEMS)),
        dma((RowGather.SEMS,)),
        dma((RowGather.SEMS,)),
        dma((6, WeightSum.SEMS)),
        dma((6, WeightSum.SEMS)),
        dma((2, 8)),
        dma((2, 8)),
        dma((2,)),
        dma((7,)),
        dma((7,)),
        dma((2,)),
        dma((2,)),
        dma((18,)),
        dma((16,)),
        pltpu.SemaphoreType.REGULAR((3,)),
    ]
    return pl.pallas_call(
        backward_kernel,
        out_shape=outs,
        in_specs=[any_space] * 18 + [vmem_space] * 4,
        out_specs=tuple(any_space for _ in outs),
        scratch_shapes=scratch,
        compiler_params=pltpu.CompilerParams(
            collective_id=1, has_side_effects=True, vmem_limit_bytes=VMEM_BYTES
        ),
        cost_estimate=pl.CostEstimate(flops=24 * 10**9, bytes_accessed=60 * 10**6, transcendentals=0),
        name="backward_layer",
    )(*args)


def doc_positions(segments):
    places = jnp.arange(segments.shape[0], dtype=jnp.int32)
    change = jnp.concatenate([jnp.ones((1,), jnp.bool_), segments[1:] != segments[:-1]])
    return places - lax.cummax(jnp.where(change, places, 0), axis=0)


def rope_tables(positions):
    frequency = jnp.exp(jnp.arange(0, HD, 2, dtype=F32) * (-math.log(10000.0) / HD))
    angles = positions.astype(F32)[:, None] * frequency
    cos, sin = jnp.cos(angles), jnp.sin(angles)
    return (
        jnp.concatenate([cos, cos, cos, cos], axis=1),
        jnp.concatenate([-sin, sin, -sin, sin], axis=1),
    )


def transposed_blocks(values):
    size = lax.axis_size("row")
    pairs = [(a * size + b, b * size + a) for a in range(size) for b in range(size)]
    return lax.ppermute(values, ("row", "col"), pairs)


def partner_of(values):
    pairs = [(a, a ^ 1) for a in range(lax.axis_size("row"))]
    return lax.ppermute(values, "row", pairs)


def body(
    hidden_in,
    segment_ids,
    attn_gain,
    w_query,
    w_key,
    w_value,
    w_out,
    mlp_gain,
    w_gate,
    w_up,
    w_down,
    grad_output,
):
    upper = lax.axis_index("row") % 2 == 1
    query_width = w_query.shape[1]
    kv_width = w_key.shape[1]
    segments = segment_ids.reshape(-1)
    cos, sin = rope_tables(doc_positions(segments))
    seg_col = jnp.broadcast_to(segments[:, None], (LEN, 128))
    seg_row = jnp.broadcast_to(segments[None, :], (8, LEN))
    gains = jnp.concatenate(
        [attn_gain[None], mlp_gain[None], jnp.zeros((6, attn_gain.shape[0]), F32)], axis=0
    )
    x_block = transposed_blocks(hidden_in)
    g_block = transposed_blocks(grad_output)
    kv_own = jnp.concatenate([w_key, w_value], axis=1)
    kv_other = partner_of(kv_own)
    kv_first = jnp.where(upper, kv_other, kv_own)
    kv_second = jnp.where(upper, kv_own, kv_other)
    w_project = jnp.concatenate(
        [
            w_query,
            kv_first[:, :kv_width],
            kv_second[:, :kv_width],
            kv_first[:, kv_width:],
            kv_second[:, kv_width:],
        ],
        axis=1,
    )
    (
        normed_one,
        x_mine,
        query,
        kv,
        mixed_low,
        totals,
        residual,
        normed_two,
        gate,
        up,
        activated,
        w_project,
        w_out_all,
        w_gate_all,
        w_up_all,
        w_down_all,
        grad_all,
        gains_all,
    ) = forward_call(
        x_block, g_block, w_project, w_out, w_gate, w_up, w_down, gains, cos, sin, seg_col, seg_row
    )
    (
        layer_output,
        grad_input,
        gd_own,
        gd_far,
        gg_own,
        gg_far,
        gu_own,
        gu_far,
        go_own,
        go_far,
        gp_own,
        gp_far,
        kv_other_own,
        kv_other_far,
        d_gains,
    ) = backward_call(
        grad_all,
        activated,
        gate,
        up,
        w_down_all,
        w_gate_all,
        w_up_all,
        normed_two,
        residual,
        query,
        kv,
        mixed_low,
        totals,
        w_out_all,
        w_project,
        normed_one,
        x_mine,
        gains_all,
        cos,
        sin,
        seg_col,
        seg_row,
    )

    def both(own, far):
        return own.astype(F32) + far.astype(F32)

    grad_kv = both(gp_own[:, query_width:], gp_far[:, query_width:]) + both(kv_other_own, kv_other_far)
    grad_kv = grad_kv.reshape(-1, 2, 2, kv_width)
    grad_kv = jnp.where(upper, grad_kv[:, :, 1], grad_kv[:, :, 0])
    return (
        layer_output,
        grad_input.astype(F32),
        d_gains[0],
        both(gp_own[:, :query_width], gp_far[:, :query_width]),
        grad_kv[:, 0],
        grad_kv[:, 1],
        both(go_own, go_far),
        d_gains[1],
        both(gg_own, gg_far),
        both(gu_own, gu_far),
        both(gd_own, gd_far),
    )


def solution(mesh):
    return jax.shard_map(
        body,
        mesh=mesh,
        in_specs=(
            P(("dp", "row"), "col"),
            P(("dp", "col"), None),
            P("col"),
            P("col", "row"),
            P("col", "row"),
            P("col", "row"),
            P("row", "col"),
            P("col"),
            P("col", "row"),
            P("col", "row"),
            P("row", "col"),
            P(("dp", "row"), "col"),
        ),
        out_specs=(
            P(("dp", "row"), "col"),
            P(("dp", "row"), "col"),
            P("col"),
            P("col", "row"),
            P("col", "row"),
            P("col", "row"),
            P("row", "col"),
            P("col"),
            P("col", "row"),
            P("col", "row"),
            P("row", "col"),
        ),
        check_vma=False,
    )
```

```python
import functools
import math

import jax
import jax.numpy as jnp
from jax import lax
from jax.experimental import pallas as pl
from jax.experimental.pallas import tpu as pltpu
from jax.sharding import PartitionSpec as P

D = 2048
HD = 64
LEN = 1024
ROWS = 8
CHIPS = 4
TOK = LEN // ROWS
FEAT = D // 8
EPSILON = 1e-05
FLOOR_SCORE = -1e30
BF16 = jnp.bfloat16
F32 = jnp.float32
MESH = pl.DeviceIdType.MESH
VMEM_BYTES = 62 * 2**20


def remote(src, dst, send, recv, device):
    return pltpu.make_async_remote_copy(
        src_ref=src, dst_ref=dst, send_sem=send, recv_sem=recv, device_id=device, device_id_type=MESH
    )


def meet(peers):
    barrier = pltpu.get_barrier_semaphore()
    for peer in peers:
        pl.semaphore_signal(barrier, inc=1, device_id=peer, device_id_type=MESH)
    pl.semaphore_wait(barrier, len(peers))


def ds(start, size):
    return pl.ds(pl.multiple_of(start, size), size)


class Place:
    def __init__(self):
        self.d = lax.axis_index("dp")
        self.r = lax.axis_index("row")
        self.c = lax.axis_index("col")
        self.y, self.k = self.r // 2, lax.rem(self.r, 2)
        self.x, self.h = self.c // 2, lax.rem(self.c, 2)
        self.partner = {"row": self.y * 2 + 1 - self.k}
        self.up = {"row": self.row_of(1)}
        self.down = {"row": self.row_of(3)}
        self.other = {"dp": 1 - self.d, "col": self.x * 2 + 1 - self.h}
        self.twin = {"dp": 1 - self.d}
        self.half = lax.rem(self.d + self.h, 2)
        self.x_peers = [{"col": self.col_of(s)} for s in (1, 3, 2)]

    def row_of(self, step):
        return lax.rem(self.y + step, CHIPS) * 2 + self.k

    def col_of(self, step):
        return lax.rem(self.x + step, 4) * 2 + self.h

    def col_from(self, step):
        return lax.rem(self.x + 4 - step, 4) * 2 + self.h


class RowGather:
    SEMS = 13

    def __init__(self, here, place, shard, send, recv):
        self.here, self.place = here, place
        y, k = here.y, here.k
        self.low, self.high, self.far_row = here.row_of(3), here.row_of(1), here.row_of(2)
        self.ups = [
            remote(shard(a), place(here.r, a), send.at[a], recv.at[a], here.up) for a in (0, 1)
        ]
        self.downs = [
            remote(shard(a), place(here.r, a), send.at[2 + a], recv.at[2 + a], here.down)
            for a in (0, 1)
        ]
        self.fars = [
            self.hand_on(self.low, 0, send.at[4], recv.at[4], here.up),
            self.hand_on(self.high, 1, send.at[5], recv.at[5], here.down),
        ]
        self.passes = {}
        for index, (row, a) in enumerate(
            [(self.low, 0), (self.low, 1), (self.high, 0), (self.high, 1), (self.far_row, 0), (self.far_row, 1)]
        ):
            self.passes[index] = self.hand_on(
                row, a, send.at[6 + index], recv.at[6 + index], here.partner
            )
        self.own = [
            remote(shard(None), place(here.r, None), send.at[12], recv.at[12], here.partner)
        ]

    def hand_on(self, row, a, send, recv, device):
        return remote(self.place(row, a), self.place(row, a), send, recv, device)

    def start(self):
        for a, b in ((0, 1), (1, 0)):
            self.ups[a].start()
            self.downs[b].start()
        self.own[0].start()

    def near(self):
        for a, b in ((0, 1), (1, 0)):
            self.ups[a].wait_recv()
            if a == 0:
                self.fars[0].start()
            self.passes[a].start()
            self.downs[b].wait_recv()
            if b == 1:
                self.fars[1].start()
            self.passes[2 + b].start()

    def far(self):
        for a in (0, 1):
            self.fars[a].wait_recv()
            self.passes[4 + a].start()

    def got_own(self):
        self.own[0].wait_recv()

    def got_near(self):
        for index in range(4):
            self.passes[index].wait_recv()

    def got_far(self):
        for index in (4, 5):
            self.passes[index].wait_recv()

    def sent(self):
        for copy in self.ups + self.downs + self.fars + self.own + list(self.passes.values()):
            copy.wait_send()


class ColGather:
    SEMS = 7

    def __init__(self, here, shard, place, send, recv, local, across_first):
        self.here, self.place, self.across_first = here, place, across_first
        self.local = pltpu.make_async_copy(shard, place(here.c), local)
        self.lines = [
            remote(shard, place(here.c), send.at[i], recv.at[i], here.x_peers[i]) for i in range(3)
        ]
        self.across = [remote(shard, place(here.c), send.at[3], recv.at[3], here.other)]
        there = here.x * 2 + 1 - here.h
        if across_first:
            self.seconds = [
                remote(place(there), place(there), send.at[4 + i], recv.at[4 + i], here.x_peers[i])
                for i in range(3)
            ]
        else:
            self.seconds = []
            for i, step in enumerate((1, 3, 2)):
                source = here.col_from(step)
                self.seconds.append(
                    remote(place(source), place(source), send.at[4 + i], recv.at[4 + i], here.other)
                )

    def start(self):
        self.start_across()
        self.start_lines()

    def start_across(self):
        self.local.start()
        self.across[0].start()

    def start_lines(self):
        for copy in self.lines:
            copy.start()

    def middle(self):
        if self.across_first:
            self.across[0].wait_recv()
            for copy in self.seconds:
                copy.start()
        else:
            for copy, second in zip(self.lines, self.seconds):
                copy.wait_recv()
                second.start()

    def end(self):
        self.local.wait()
        if self.across_first:
            for copy in self.lines:
                copy.wait_recv()
        else:
            self.across[0].wait_recv()
        for copy in self.seconds:
            copy.wait_recv()
        for copy in self.lines + self.across + self.seconds:
            copy.wait_send()


class SplitGather:
    SEMS = 14

    def __init__(self, here, shard, place, send, recv, local):
        self.here, self.place = here, place
        half = here.half
        self.local = pltpu.make_async_copy(shard(None), place(here.c, None), local)

        def hand_on(c, index, device):
            return remote(place(c, half), place(c, half), send.at[index], recv.at[index], device)

        own = place(here.c, half)
        self.across = remote(shard(half), own, send.at[0], recv.at[0], here.other)
        self.lines = [
            remote(shard(half), own, send.at[1 + i], recv.at[1 + i], here.x_peers[i]) for i in range(3)
        ]
        there = here.x * 2 + 1 - here.h
        self.seconds = [hand_on(there, 4 + i, here.x_peers[i]) for i in range(3)]
        sources = [here.col_from(step) for step in (1, 3, 2)]
        others = [source + 1 - 2 * here.h for source in sources]
        self.swaps = [
            hand_on(c, 7 + i, here.twin) for i, c in enumerate([there] + sources + others)
        ]

    def start_across(self):
        self.local.start()
        self.across.start()

    def start_lines(self):
        for copy in self.lines:
            copy.start()

    def middle(self):
        self.across.wait_recv()
        for copy in self.seconds:
            copy.start()
        self.swaps[0].start()

    def late(self):
        for copy, swap in zip(self.lines + self.seconds, self.swaps[1:]):
            copy.wait_recv()
            swap.start()

    def end(self):
        self.local.wait()
        for swap in self.swaps:
            swap.wait_recv()
        for copy in [self.across] + self.lines + self.seconds + self.swaps:
            copy.wait_send()


class RowSum:
    SEMS = 10

    def __init__(self, here, blocks, paired, relayed, landed, send, recv):
        self.here, self.blocks, self.paired = here, blocks, paired
        self.relayed, self.landed = relayed, landed
        k, half = here.k, TOK // 2
        self.mine, self.half = k * TOK, half
        self.pairs = [
            remote(
                blocks.at[s, ds((1 - k) * TOK, TOK)], paired.at[s], send.at[s], recv.at[s], here.partner
            )
            for s in range(4)
        ]
        self.fars = [
            remote(self.part(2, 0), relayed.at[0], send.at[4], recv.at[4], here.up),
            remote(self.part(2, 1), relayed.at[1], send.at[5], recv.at[5], here.down),
        ]
        self.nears = {}
        for index, (s, a, device) in enumerate(
            [(1, 1, here.up), (3, 0, here.down), (1, 0, here.up), (3, 1, here.down)]
        ):
            slot = 0 if s == 1 else 1
            self.nears[s, a] = remote(
                self.part(s, a),
                landed.at[slot, pl.ds(a * half, half)],
                send.at[6 + index],
                recv.at[6 + index],
                device,
            )

    def part(self, s, a):
        return self.blocks.at[s, ds(self.mine + a * self.half, self.half)]

    def add(self, s, a, other):
        part = self.part(s, a)
        part[...] = (part[...].astype(F32) + other[...].astype(F32)).astype(BF16)

    def pair(self, s):
        self.pairs[s].start()

    def join(self, s):
        self.pairs[s].wait_recv()
        for a in (0, 1):
            self.add(s, a, self.paired.at[s, pl.ds(a * self.half, self.half)])

    def far(self):
        self.join(2)
        self.fars[0].start()
        self.fars[1].start()

    def near(self):
        self.join(1)
        self.nears[1, 1].start()
        self.join(3)
        self.nears[3, 0].start()

    def relay(self):
        self.fars[0].wait_recv()
        self.add(1, 0, self.relayed.at[0])
        self.nears[1, 0].start()
        self.fars[1].wait_recv()
        self.add(3, 1, self.relayed.at[1])
        self.nears[3, 1].start()

    def arrive(self):
        self.pairs[0].wait_recv()
        for copy in self.nears.values():
            copy.wait_recv()

    def total(self, start, rows):
        own = self.blocks[0, pl.ds(pl.multiple_of(self.mine + start, rows), rows)].astype(F32)
        here = pl.ds(pl.multiple_of(start, rows), rows)
        return (
            own
            + self.paired[0, here].astype(F32)
            + self.landed[0, here].astype(F32)
            + self.landed[1, here].astype(F32)
        )

    def sent(self):
        for copy in self.pairs + self.fars + list(self.nears.values()):
            copy.wait_send()


def add_rows(rows, target, others):
    kind = target.dtype

    def step(t, carry):
        at = ds(t * rows, rows)
        total = target[at, :].astype(F32)
        for other in others:
            total = total + other[at, :].astype(F32)
        target[at, :] = total.astype(kind)
        return carry

    lax.fori_loop(0, target.shape[0] // rows, step, 0)


class WeightSum:
    SEMS = 8

    def __init__(self, here, part, wide_part, rows, z_land, x_land, far_part, send, recv, across_first):
        self.here, self.part, self.across_first, self.rows = here, part, across_first, rows
        self.z_land, self.x_land = z_land, x_land
        self.own = part(here.c)
        steps = (1, 3, 2)
        if across_first:
            self.mine = [part(x * 2 + here.h) for x in range(4)]
            self.across = [
                remote(part(x * 2 + 1 - here.h), z_land.at[x], send.at[x], recv.at[x], here.other)
                for x in range(4)
            ]
            self.lines = [
                remote(
                    part(here.col_of(step)), x_land.at[i], send.at[4 + i], recv.at[4 + i], here.x_peers[i]
                )
                for i, step in enumerate(steps)
            ]
        else:
            self.wide = wide_part(here.x)
            self.across = [
                remote(
                    part(here.x * 2 + 1 - here.h), z_land, send.at[3], recv.at[3], here.other
                )
            ]
            self.lines = [
                remote(
                    wide_part(lax.rem(here.x + step, 4)),
                    x_land.at[i],
                    send.at[i],
                    recv.at[i],
                    here.x_peers[i],
                )
                for i, step in enumerate(steps)
            ]
        self.swap = remote(self.own, far_part, send.at[7], recv.at[7], here.twin)

    def add(self, target, others):
        add_rows(self.rows, target, others)

    def start(self):
        for copy in self.across if self.across_first else self.lines:
            copy.start()

    def middle(self):
        if self.across_first:
            for x in range(4):
                self.across[x].wait_recv()
                self.add(self.mine[x], [self.z_land.at[x]])
            for copy in self.lines:
                copy.start()
        else:
            for copy in self.lines:
                copy.wait_recv()
            self.add(self.wide, [self.x_land.at[i] for i in range(3)])
            self.across[0].start()

    def last(self):
        if self.across_first:
            for copy in self.lines:
                copy.wait_recv()
            self.add(self.own, [self.x_land.at[i] for i in range(3)])
        else:
            self.across[0].wait_recv()
            self.add(self.own, [self.z_land])
        self.swap.start()

    def end(self):
        self.swap.wait()
        for copy in self.across + self.lines:
            copy.wait_send()


class SplitSum:
    SEMS = 16

    def __init__(self, here, part, rows, twin_land, x_land, z_land, far_part, send, recv):
        self.here, self.rows = here, rows
        self.twin_land, self.x_land, self.z_land = twin_land, x_land, z_land
        half, x, h = here.half, here.x, here.h
        self.mine = [part(c, half) for c in range(8)]
        self.twins = [
            remote(part(c, 1 - half), twin_land.at[c], send.at[c], recv.at[c], here.twin)
            for c in range(8)
        ]
        self.lines = []
        for i, step in enumerate((1, 3, 2)):
            target = lax.rem(x + step, 4) * 2
            for side in range(2):
                index = 8 + 2 * i + side
                self.lines.append(
                    remote(
                        part(target + side, half),
                        x_land.at[i, side],
                        send.at[index],
                        recv.at[index],
                        here.x_peers[i],
                    )
                )
        self.sides = [part(x * 2 + side, half) for side in range(2)]
        self.across = remote(part(x * 2 + 1 - h, half), z_land, send.at[14], recv.at[14], here.other)
        self.own = part(here.c, half)
        self.swap = remote(self.own, far_part, send.at[15], recv.at[15], here.twin)

    def add(self, target, others):
        add_rows(self.rows, target, others)

    def start(self):
        for copy in self.twins:
            copy.start()

    def middle(self):
        for c in range(8):
            self.twins[c].wait_recv()
            self.add(self.mine[c], [self.twin_land.at[c]])
        for copy in self.lines:
            copy.start()

    def late(self):
        for copy in self.lines:
            copy.wait_recv()
        for side in range(2):
            self.add(self.sides[side], [self.x_land.at[i, side] for i in range(3)])
        self.across.start()

    def last(self):
        self.across.wait_recv()
        self.add(self.own, [self.z_land])
        self.swap.start()

    def end(self):
        self.swap.wait()
        for copy in self.twins + self.lines + [self.across]:
            copy.wait_send()


class Spread:
    def __init__(self, here, source, target, send, recv, local):
        self.here = here
        self.same = here.r == here.c
        self.copies = []
        place = target.at[ds(here.r * TOK, TOK)]
        for j in range(8):
            shard = source.at[:, pl.ds(j * FEAT, FEAT)]
            self.copies.append(
                (
                    remote(shard, place, send.at[j], recv.at[here.r], {"row": here.c, "col": j}),
                    pltpu.make_async_copy(shard, place, local),
                )
            )
        self.arrivals = [
            remote(
                source.at[:, pl.ds(0, FEAT)],
                target.at[pl.ds(i * TOK, TOK)],
                send.at[i],
                recv.at[i],
                {"row": here.c, "col": i},
            )
            for i in range(8)
        ]

    def each(self, index, other, own):
        itself = self.same & (self.here.r == index)
        pl.when(itself)(own)
        pl.when(jnp.logical_not(itself))(other)

    def start(self):
        for j, (copy, local) in enumerate(self.copies):
            self.each(j, copy.start, local.start)

    def end(self):
        for j, (copy, local) in enumerate(self.copies):
            self.each(j, copy.wait_send, local.wait)
        for i, copy in enumerate(self.arrivals):
            self.each(i, copy.wait_recv, lambda: None)


class Collect:
    def __init__(self, here, source, middle, target, send, recv, local):
        self.here = here
        r, c = here.r, here.c
        self.local = pltpu.make_async_copy(source.at[ds(r * TOK, TOK)], middle.at[r], local.at[0])
        self.firsts = []
        self.seconds = []
        lanes = target.at[:, ds(c * FEAT, FEAT)]
        for k in range(1, 8):
            i = lax.rem(r + k, 8)
            self.firsts.append(
                remote(
                    source.at[ds(i * TOK, TOK)], middle.at[r], send.at[k], recv.at[k], {"row": i}
                )
            )
        for k in range(8):
            a = lax.rem(r + 8 - k, 8)
            self.seconds.append(
                (
                    a == c,
                    remote(middle.at[a], lanes, send.at[8 + k], recv.at[8 + c], {"col": a}),
                    pltpu.make_async_copy(middle.at[a], lanes, local.at[1]),
                )
            )
        self.arrivals = [
            (
                c == j,
                remote(
                    middle.at[0],
                    target.at[:, pl.ds(j * FEAT, FEAT)],
                    send.at[8 + j],
                    recv.at[8 + j],
                    {"col": j},
                ),
            )
            for j in range(8)
        ]

    def start(self):
        self.local.start()
        for copy in self.firsts:
            copy.start()

    def turn(self):
        self.local.wait()
        for k, (itself, copy, local) in enumerate(self.seconds):
            if k > 0:
                self.firsts[k - 1].wait_recv()
            pl.when(itself)(local.start)
            pl.when(jnp.logical_not(itself))(copy.start)

    def arrive(self):
        for itself, copy, local in self.seconds:
            pl.when(itself)(local.wait)
        for itself, copy in self.arrivals:
            pl.when(jnp.logical_not(itself))(copy.wait_recv)

    def sent(self):
        for copy in self.firsts:
            copy.wait_send()
        for itself, copy, local in self.seconds:
            pl.when(jnp.logical_not(itself))(copy.wait_send)


def nn(a, b):
    return jnp.dot(a, b, preferred_element_type=F32)


def nt(a, b):
    return lax.dot_general(a, b, (((1,), (1,)), ((), ())), preferred_element_type=F32)


def tn(a, b):
    return lax.dot_general(a, b, (((0,), (0,)), ((), ())), preferred_element_type=F32)


def swap_halves(values):
    width = values.shape[-1]
    lane = lax.broadcasted_iota(jnp.int32, values.shape, 1)
    return jnp.where(
        lax.rem(lane, HD) < HD // 2, pltpu.roll(values, width - HD // 2, 1), pltpu.roll(values, HD // 2, 1)
    )


def turn(values, cos, sin):
    return values * cos + swap_halves(values) * sin


def gain_row(gains, which):
    return jnp.concatenate([gains[pl.ds(8 * j + which, 1), :] for j in range(8)], axis=1)


def layer_kernel(
    x_in,
    g_in,
    wp_in,
    wo_in,
    wg_in,
    wu_in,
    wd_in,
    gain_in,
    seg_in,
    frequency,
    layer_out,
    input_out,
    gd_own,
    gd_far,
    gg_own,
    gg_far,
    gu_own,
    gu_far,
    go_own,
    go_far,
    gp_own,
    gp_far,
    kv_own,
    kv_far,
    gains_out,
    normed_kept,
    g_middle,
    x_middle,
    x_mine,
    low_rows,
    wide,
    g_all,
    act,
    gate,
    up,
    wd,
    gd,
    wg,
    wu,
    wo,
    wp,
    gains,
    cos,
    sin,
    seg_col,
    query,
    k_low,
    k_high,
    v_low,
    v_high,
    mixed,
    totals,
    d_mixed,
    d_projected,
    dk_low,
    dk_high,
    dv_low,
    dv_high,
    blocks,
    paired,
    relayed,
    landed,
    residual,
    d_residual,
    gain_sums,
    gain_x,
    gain_z,
    gain_far,
    gain_rows,
    gd_z,
    gd_x,
    gg_twin,
    gg_x,
    gg_z,
    gu_z,
    gu_x,
    go_z,
    go_x,
    gp_z,
    gp_x,
    collect_send,
    collect_recv,
    collect_local,
    gather_send,
    gather_recv,
    gather_local,
    w_send,
    w_recv,
    w_local,
    rows_send,
    rows_recv,
    sum_send,
    sum_recv,
    spread_send,
    spread_recv,
    spread_local,
    last_send,
    last_recv,
    keep_sem,
    free,
):
    here = Place()
    same = here.r == here.c
    barrier = pltpu.get_barrier_semaphore()
    row_peers = [{"row": lax.rem(here.r + k, ROWS)} for k in range(1, ROWS)]
    col_peers = [{"col": lax.rem(here.c + k, 8)} for k in range(1, 8)]
    peers = row_peers + col_peers + [here.other, here.twin]
    for peer in peers:
        pl.semaphore_signal(barrier, inc=1, device_id=peer, device_id_type=MESH)
    for i in range(8):

        @pl.when(jnp.logical_not(same & (here.r == i)))
        def _():
            pl.semaphore_signal(
                barrier, inc=1, device_id={"row": i, "col": here.r}, device_id_type=MESH
            )

    pl.semaphore_wait(barrier, len(peers) + 8 - same.astype(jnp.int32))

    def token_place(ref):
        def place(row, a):
            if a is None:
                return ref.at[ds(row * TOK, TOK)]
            return ref.at[ds(row * TOK + a * (TOK // 2), TOK // 2)]

        return place

    def own_part(ref):
        place = token_place(ref)
        return lambda a: place(here.r, a)

    def low_part(a):
        return low_rows if a is None else low_rows.at[pl.ds(a * (TOK // 2), TOK // 2)]

    def row_gather(index, ref, shard):
        return RowGather(here, token_place(ref), shard, gather_send.at[index], gather_recv.at[index])

    def row_sum(index):
        return RowSum(here, blocks, paired, relayed, landed, rows_send.at[index], rows_recv.at[index])

    def collect(index, source, middle, target):
        return Collect(
            here,
            source,
            middle,
            target,
            collect_send.at[index],
            collect_recv.at[index],
            collect_local.at[index],
        )

    def spread(index, target):
        return Spread(
            here,
            low_rows,
            target,
            spread_send.at[index],
            spread_recv.at[index],
            spread_local.at[index],
        )

    def col_gather(index, shard, place, across_first):
        return ColGather(
            here, shard, place, w_send.at[index], w_recv.at[index], w_local.at[index], across_first
        )

    def split_gather(index, shard, ref):
        half = FEAT // 2

        def place(c, a):
            if a is None:
                return ref.at[ds(c * FEAT, FEAT)]
            return ref.at[ds(c * FEAT + a * half, half)]

        def part(a):
            return shard if a is None else shard.at[ds(a * half, half)]

        return SplitGather(
            here, part, place, w_send.at[index], w_recv.at[index], w_local.at[index]
        )

    def weight_sum(index, parts, rows, z_land, x_land, far_part, across_first):
        return WeightSum(
            here,
            parts[0],
            parts[1],
            rows,
            z_land,
            x_land,
            far_part,
            sum_send.at[index],
            sum_recv.at[index],
            across_first,
        )

    def rows_of(ref):
        return lambda c: ref.at[ds(c * FEAT, FEAT)], lambda x: ref.at[ds(x * 2 * FEAT, 2 * FEAT)]

    def lanes_of(ref):
        return (
            lambda c: ref.at[:, ds(c * FEAT, FEAT)],
            lambda x: ref.at[:, ds(x * 2 * FEAT, 2 * FEAT)],
        )

    def credit(index):
        for peer in (here.partner, here.up, here.down):
            pl.semaphore_signal(free.at[index], inc=1, device_id=peer, device_id_type=MESH)

    def chip_rows(s):
        return ds(lax.rem(here.y + s, CHIPS) * 256, 256)

    kept = []

    def keep(src, dst):
        copy = pltpu.make_async_copy(src, dst, keep_sem.at[len(kept)])
        copy.start()
        kept.append(copy)
        return copy

    x_collect = collect(0, x_in, x_middle, x_mine)
    g_collect = collect(1, g_in, g_middle, low_rows)
    n1_gather = row_gather(0, wide, own_part(wide))
    g_gather = row_gather(1, g_all, low_part)
    n2_gather = row_gather(2, wide, own_part(wide))
    d_gather = row_gather(3, g_all, low_part)
    gain_gather = col_gather(0, gain_in, lambda c: gains.at[ds(c * 8, 8)], True)
    wp_gather = col_gather(1, wp_in, lambda c: wp.at[ds(c * FEAT, FEAT)], True)
    wo_gather = col_gather(2, wo_in, lambda c: wo.at[:, ds(c * FEAT, FEAT)], False)
    wd_gather = col_gather(3, wd_in, lambda c: wd.at[:, ds(c * FEAT, FEAT)], False)
    wg_gather = split_gather(4, wg_in, wg)
    wu_gather = split_gather(5, wu_in, wu)
    d_sum = weight_sum(0, lanes_of(gd), 64, gd_z, gd_x, gd_far, True)
    u_sum = weight_sum(1, rows_of(wu), 32, gu_z, gu_x, gu_far, False)
    o_sum = weight_sum(2, lanes_of(wo), 32, go_z, go_x, go_far, True)
    p_sum = weight_sum(3, rows_of(wp), 32, gp_z, gp_x, gp_far, True)
    gain_sum = weight_sum(4, lanes_of(gain_sums), 8, gain_z, gain_x, gain_far, False)
    g_sum = SplitSum(
        here,
        lambda c, a: wg.at[ds(c * FEAT + a * (FEAT // 2), FEAT // 2)],
        32,
        gg_twin,
        gg_x,
        gg_z,
        gg_far,
        sum_send.at[5],
        sum_recv.at[5],
    )

    x_collect.start()
    gain_gather.start_across()
    wp_gather.start_across()
    segments = seg_in[0:1, :]
    places = lax.broadcasted_iota(jnp.int32, (1, LEN), 1)
    for number in range(3):
        count = jnp.sum((segments == number).astype(F32), axis=1, keepdims=True).astype(jnp.int32)
        places = places - jnp.where(segments > number, count, 0)
    tall = jnp.transpose(jnp.broadcast_to(places.astype(F32), (128, LEN)))
    angles = tall * frequency[0:1, :]
    sign = jnp.where(
        lax.rem(lax.broadcasted_iota(jnp.int32, (1, 128), 1), HD) < HD // 2, -1.0, 1.0
    )
    cos[...] = jnp.cos(angles)
    sin[...] = jnp.sin(angles) * sign
    seg_col[...] = jnp.transpose(jnp.broadcast_to(segments.astype(F32), (128, LEN)))
    seg_row = segments.astype(F32)
    x_collect.turn()
    g_collect.start()
    gain_gather.start_lines()
    wp_gather.start_lines()
    gain_gather.middle()
    wp_gather.middle()
    wo_gather.start()
    wg_gather.start_across()
    wu_gather.start_across()
    gain_gather.end()
    gain_one = gain_row(gains, 0)
    x_collect.arrive()

    def norm_rows(t, carry):
        values = x_mine[ds(t * 16, 16), :].astype(F32)
        scale = lax.rsqrt(jnp.sum(values * values, axis=1, keepdims=True) * (1.0 / D) + EPSILON)
        wide[ds(here.r * TOK + t * 16, 16), :] = (values * scale * gain_one).astype(BF16)
        return carry

    lax.fori_loop(0, TOK // 16, norm_rows, 0)
    n1_gather.start()
    g_collect.turn()
    wg_gather.start_lines()
    wu_gather.start_lines()
    lane = lax.broadcasted_iota(jnp.int32, (256, 128), 1)

    def project(s):
        rows = chip_rows(s)
        projected = nn(wide[rows, :], wp[...])
        cos_rows, sin_rows = cos[rows, :], sin[rows, :]
        for p in range(2):
            pair = turn(projected[:, p * 128 : (p + 1) * 128], cos_rows, sin_rows)
            query[rows, pl.ds(p * 128, 128)] = (pair * HD**-0.5).astype(BF16)
        key_value = projected[:, 256:384]
        key = jnp.where(lane < HD, turn(key_value, cos_rows, sin_rows), 0.0)
        value = jnp.where(lane < HD, 0.0, key_value)
        k_low[rows, :] = key.astype(BF16)
        k_high[rows, :] = pltpu.roll(key, HD, 1).astype(BF16)
        v_high[rows, :] = value.astype(BF16)
        v_low[rows, :] = pltpu.roll(value, HD, 1).astype(BF16)

    wp_gather.end()
    n1_gather.got_own()
    project(0)
    wo_gather.middle()
    n1_gather.near()
    wg_gather.middle()
    wu_gather.middle()
    n1_gather.got_near()
    project(1)
    n1_gather.far()
    project(3)
    n1_gather.got_far()
    project(2)
    normed_copy = keep(wide, normed_kept)
    g_collect.arrive()
    own_g = pltpu.make_async_copy(low_rows, token_place(g_all)(here.r, None), gather_local.at[0])
    own_g.start()
    g_gather.start()
    wd_gather.start()

    def bias_of(block, keys):
        first = block * 256
        row = lax.broadcasted_iota(jnp.int32, (256, keys), 0) + first
        key = lax.broadcasted_iota(jnp.int32, (256, keys), 1)
        alike = seg_col[pl.ds(first, 256), 0:1] == seg_row[:, :keys]
        return jnp.where(alike & (key <= row), 0.0, FLOOR_SCORE)

    def attend(block):
        keys = (block + 1) * 256
        rows, seen = pl.ds(block * 256, 256), pl.ds(0, keys)
        bias = bias_of(block, keys)

        def one_pair(p, sums):
            lanes = ds(p * 128, 128)
            pair = query[rows, lanes]
            out = jnp.zeros((256, 128), F32)
            for side, (key, value) in enumerate(((k_low, v_low), (k_high, v_high))):
                scores = nt(pair, key[seen, :]) + bias
                row_max = jnp.max(scores, axis=1, keepdims=True)
                exps = jnp.exp(scores - row_max)
                row_sum = jnp.sum(exps, axis=1, keepdims=True)
                out = out + nn(exps.astype(BF16), value[seen, :]) * (1.0 / row_sum)
                sums = jnp.where(lane == 2 * p + side, row_max + jnp.log(row_sum), sums)
            mixed[rows, lanes] = out.astype(BF16)
            return sums

        totals[rows, :] = lax.fori_loop(0, 2, one_pair, jnp.zeros((256, 128), F32))

    attend(0)
    attend(1)
    attend(2)
    wg_gather.late()
    wu_gather.late()
    attend(3)
    wo_gather.end()
    normed_copy.wait()
    n1_gather.sent()
    out_sum = row_sum(0)
    for s in (2, 1, 3, 0):
        blocks[s] = nn(mixed[chip_rows(s), :], wo[...]).astype(BF16)
        out_sum.pair(s)
        if s == 1:
            out_sum.far()
    out_sum.near()
    g_gather.near()
    wd_gather.middle()
    out_sum.relay()
    g_gather.far()
    out_sum.arrive()
    gain_two = gain_row(gains, 1)

    def residual_rows(t, carry):
        rows = ds(t * 16, 16)
        values = x_mine[rows, :].astype(F32) + out_sum.total(t * 16, 16)
        residual[rows, :] = values
        scale = lax.rsqrt(jnp.sum(values * values, axis=1, keepdims=True) * (1.0 / D) + EPSILON)
        wide[ds(here.r * TOK + t * 16, 16), :] = (values * scale * gain_two).astype(BF16)
        return carry

    lax.fori_loop(0, TOK // 16, residual_rows, 0)
    n2_gather.start()
    credit(0)
    out_sum.sent()
    wg_gather.end()
    wu_gather.end()

    def feed(s):
        rows = chip_rows(s)
        values = wide[rows, :]
        gate_rows = nn(values, wg[...])
        up_rows = nn(values, wu[...])
        gate[rows, :] = gate_rows.astype(BF16)
        up[rows, :] = up_rows.astype(BF16)
        act[rows, :] = (gate_rows * (1.0 / (1.0 + jnp.exp(-gate_rows))) * up_rows).astype(BF16)

    n2_gather.got_own()
    feed(0)
    n2_gather.near()
    n2_gather.got_near()
    feed(1)
    n2_gather.far()
    feed(3)
    n2_gather.got_far()
    feed(2)

    g_gather.got_own()
    g_gather.got_near()
    g_gather.got_far()
    own_g.wait()
    wd_gather.end()
    first_sum = row_sum(1)
    pl.semaphore_wait(free.at[0], 3)
    for s in (2, 1, 3, 0):
        rows = chip_rows(s)
        d_act = nt(g_all[rows, :], wd[...])
        gate_rows = gate[rows, :].astype(F32)
        up_rows = up[rows, :].astype(F32)
        sig = 1.0 / (1.0 + jnp.exp(-gate_rows))
        d_up = (d_act * (gate_rows * sig)).astype(BF16)
        d_gate = (d_act * up_rows * (sig * (1.0 + gate_rows * (1.0 - sig)))).astype(BF16)
        gate[rows, :] = d_gate
        up[rows, :] = d_up
        blocks[s] = (nt(d_gate, wg[...]) + nt(d_up, wu[...])).astype(BF16)
        first_sum.pair(s)
        if s == 1:
            first_sum.far()
    first_sum.near()

    def down_grad(j, carry):
        lanes = ds(j * 512, 512)
        gd[:, lanes] = tn(act[...], g_all[:, lanes]).astype(BF16)
        return carry

    lax.fori_loop(0, 4, down_grad, 0)
    d_sum.start()
    g_gather.sent()
    credit(1)
    first_sum.relay()
    n2_gather.sent()

    def gate_grad(j, carry):
        lanes = ds(j * 512, 512)
        wg[lanes, :] = tn(wide[:, lanes], gate[...]).astype(BF16)
        return carry

    lax.fori_loop(0, 4, gate_grad, 0)
    g_sum.start()

    def up_grad(j, carry):
        lanes = ds(j * 512, 512)
        wu[lanes, :] = tn(wide[:, lanes], up[...]).astype(BF16)
        return carry

    lax.fori_loop(0, 4, up_grad, 0)
    u_sum.start()
    normed_again = pltpu.make_async_copy(normed_kept, wide, gather_local.at[1])
    normed_again.start()
    first_sum.arrive()
    gain_sums[...] = jnp.zeros_like(gain_sums)

    def norm_back(total, values, gain, which):
        scale = lax.rsqrt(jnp.sum(values * values, axis=1, keepdims=True) * (1.0 / D) + EPSILON)
        scaled = total * gain
        inner = jnp.sum(scaled * values, axis=1, keepdims=True) * (1.0 / D)
        part = jnp.sum(total * values * scale, axis=0, keepdims=True)
        gain_sums[pl.ds(which, 1), :] = gain_sums[pl.ds(which, 1), :] + part
        return scale * scaled - values * (scale * scale * scale * inner)

    def residual_back_rows(t, carry):
        rows = ds(t * 16, 16)
        back = norm_back(first_sum.total(t * 16, 16), residual[rows, :], gain_two, 1)
        total = low_rows[rows, :].astype(F32) + back
        d_residual[rows, :] = total
        low_rows[rows, :] = total.astype(BF16)
        return carry

    lax.fori_loop(0, TOK // 16, residual_back_rows, 0)
    credit(2)
    pl.semaphore_wait(free.at[1], 3)
    own_rows = pltpu.make_async_copy(low_rows, token_place(g_all)(here.r, None), gather_local.at[2])
    own_rows.start()
    d_gather.start()
    first_sum.sent()
    layer_sum = row_sum(2)

    def down_block(s):
        blocks[s] = nn(act[chip_rows(s), :], wd[...]).astype(BF16)

    for s in (2, 1):
        down_block(s)
    d_gather.near()
    for s in (3, 0):
        down_block(s)
    pl.semaphore_wait(free.at[2], 3)
    for s in (2, 1, 3, 0):
        layer_sum.pair(s)
    d_gather.far()
    layer_sum.far()

    def mix_back(s):
        rows = chip_rows(s)
        d_mixed[rows, :] = nt(g_all[rows, :], wo[...]).astype(BF16)

    own_rows.wait()
    d_gather.got_own()
    mix_back(0)
    d_gather.got_near()
    mix_back(1)
    mix_back(3)
    d_gather.got_far()
    mix_back(2)

    def out_grad(j, carry):
        lanes = ds(j * 512, 512)
        wo[:, lanes] = tn(mixed[...], g_all[:, lanes]).astype(BF16)
        return carry

    lax.fori_loop(0, 4, out_grad, 0)
    o_sum.start()
    layer_sum.near()
    for sums in (dk_low, dk_high, dv_low, dv_high):
        sums[...] = jnp.zeros_like(sums)

    def attend_back(block):
        keys = (block + 1) * 256
        rows, seen = pl.ds(block * 256, 256), pl.ds(0, keys)
        bias = bias_of(block, keys)
        cos_rows, sin_rows = cos[rows, :], sin[rows, :]

        def one_pair(p, carry):
            lanes = ds(p * 128, 128)
            pair = query[rows, lanes]
            grads = d_mixed[rows, lanes]
            product = grads.astype(F32) * mixed[rows, lanes].astype(F32)
            out = jnp.zeros((256, 128), F32)
            for side, (key, value, dk, dv) in enumerate(
                ((k_low, v_low, dk_low, dv_low), (k_high, v_high, dk_high, dv_high))
            ):
                half = (lane < HD) if side == 0 else (lane >= HD)
                inner = jnp.sum(jnp.where(half, product, 0.0), axis=1, keepdims=True)
                total = jnp.sum(
                    jnp.where(lane == 2 * p + side, totals[rows, :], 0.0), axis=1, keepdims=True
                )
                probs = jnp.exp(nt(pair, key[seen, :]) + bias - total)
                d_probs = nt(grads, value[seen, :])
                d_scores = (probs * (d_probs - inner)).astype(BF16)
                out = out + nn(d_scores, key[seen, :])
                dk[seen, :] = dk[seen, :] + tn(d_scores, pair)
                dv[seen, :] = dv[seen, :] + tn(probs.astype(BF16), grads)
            d_projected[rows, lanes] = turn(out * HD**-0.5, cos_rows, -sin_rows).astype(BF16)
            return carry

        lax.fori_loop(0, 2, one_pair, 0)

    attend_back(3)
    layer_sum.relay()
    g_sum.middle()
    attend_back(2)
    u_sum.middle()
    attend_back(1)
    d_sum.middle()
    attend_back(0)

    def key_rows(t, carry):
        rows = ds(t * 256, 256)
        key = dk_low[rows, :] + pltpu.roll(dk_high[rows, :], HD, 1)
        value = dv_high[rows, :] + pltpu.roll(dv_low[rows, :], HD, 1)
        key = turn(key, cos[rows, :], -sin[rows, :])
        d_projected[rows, pl.ds(256, 128)] = jnp.where(lane < HD, key, value).astype(BF16)
        return carry

    lax.fori_loop(0, 4, key_rows, 0)
    layer_sum.arrive()
    d_gather.sent()

    def layer_rows(t, carry):
        rows = ds(t * 16, 16)
        low_rows[rows, :] = (residual[rows, :] + layer_sum.total(t * 16, 16)).astype(BF16)
        return carry

    lax.fori_loop(0, TOK // 16, layer_rows, 0)
    credit(3)
    layer_sum.sent()
    last_sum = row_sum(3)
    pl.semaphore_wait(free.at[3], 3)
    for s in (2, 1, 3, 0):
        blocks[s] = nt(d_projected[chip_rows(s), :], wp[...]).astype(BF16)
        last_sum.pair(s)
        if s == 1:
            last_sum.far()
    last_sum.near()
    layer_spread = spread(0, layer_out)
    layer_spread.start()
    normed_again.wait()

    def project_grad(j, carry):
        lanes = ds(j * 512, 512)
        wp[lanes, :] = tn(wide[:, lanes], d_projected[...]).astype(BF16)
        return carry

    lax.fori_loop(0, 4, project_grad, 0)
    p_sum.start()
    last_sum.relay()
    g_sum.late()
    o_sum.middle()
    u_sum.last()
    layer_spread.end()
    last_sum.arrive()
    gain_one = gain_row(gains, 0)

    def input_rows(t, carry):
        rows = ds(t * 16, 16)
        values = x_mine[rows, :].astype(F32)
        back = norm_back(last_sum.total(t * 16, 16), values, gain_one, 0)
        low_rows[rows, :] = (d_residual[rows, :] + back).astype(BF16)
        return carry

    lax.fori_loop(0, TOK // 16, input_rows, 0)
    input_spread = spread(1, input_out)
    input_spread.start()
    gain_sum.start()
    p_sum.middle()
    gain_sum.middle()
    d_sum.last()
    g_sum.last()
    o_sum.last()
    gain_sum.last()
    p_sum.last()
    gain_sum.end()
    gain_rows[here.r] = gain_sum.own[...] + gain_far[...]
    row_copies = [
        remote(
            gain_rows.at[here.r], gain_rows.at[here.r], last_send.at[k], last_recv.at[k], row_peers[k]
        )
        for k in range(7)
    ]
    for copy in row_copies:
        copy.start()
    keep(d_sum.own, gd_own)
    keep(g_sum.own, gg_own)
    keep(u_sum.own, gu_own)
    keep(o_sum.own, go_own)
    keep(p_sum.own, gp_own)
    key_lanes = pl.ds(256, 128)
    own_copy = remote(
        p_sum.own.at[:, key_lanes], kv_own, last_send.at[7], last_recv.at[7], here.partner
    )
    own_copy.start()
    p_sum.end()
    far_copy = remote(
        gp_far.at[:, key_lanes], kv_far, last_send.at[8], last_recv.at[8], here.partner
    )
    far_copy.start()
    for sums in (d_sum, g_sum, u_sum, o_sum):
        sums.end()
    for copy in row_copies:
        copy.wait()
    total = gain_rows[0]
    for r in range(1, 8):
        total = total + gain_rows[r]
    gain_rows[0] = total
    keep(gain_rows.at[0], gains_out)
    input_spread.end()
    own_copy.wait()
    far_copy.wait()
    last_sum.sent()
    x_collect.sent()
    g_collect.sent()
    for copy in kept:
        if copy is not normed_copy:
            copy.wait()


def layer_call(*args):
    ff = args[4].shape[1]
    any_space = pl.BlockSpec(memory_space=pl.ANY)
    vmem_space = pl.BlockSpec(memory_space=pltpu.VMEM)
    dma = pltpu.SemaphoreType.DMA

    def low(*shape):
        return jax.ShapeDtypeStruct(shape, BF16)

    outs = (
        low(LEN, FEAT),
        low(LEN, FEAT),
        low(ff, FEAT),
        low(ff, FEAT),
        low(FEAT // 2, ff),
        low(FEAT // 2, ff),
        low(FEAT, ff),
        low(FEAT, ff),
        low(256, FEAT),
        low(256, FEAT),
        low(FEAT, 384),
        low(FEAT, 384),
        low(FEAT, 128),
        low(FEAT, 128),
        jax.ShapeDtypeStruct((8, FEAT), F32),
        low(LEN, D),
        low(8, TOK, FEAT),
    )

    def vmem(*shape, dtype=BF16):
        return pltpu.VMEM(shape, dtype)

    scratch = [
        vmem(8, TOK, FEAT),
        vmem(TOK, D),
        vmem(TOK, D),
        vmem(LEN, D),
        vmem(LEN, D),
        vmem(LEN, ff),
        vmem(LEN, ff),
        vmem(LEN, ff),
        vmem(ff, D),
        vmem(ff, D),
        vmem(D, ff),
        vmem(D, ff),
        vmem(256, D),
        vmem(D, 384),
        vmem(64, 256, dtype=F32),
        vmem(LEN, 128, dtype=F32),
        vmem(LEN, 128, dtype=F32),
        vmem(LEN, 128, dtype=F32),
        vmem(LEN, 256),
        vmem(LEN, 128),
        vmem(LEN, 128),
        vmem(LEN, 128),
        vmem(LEN, 128),
        vmem(LEN, 256),
        vmem(LEN, 128, dtype=F32),
        vmem(LEN, 256),
        vmem(LEN, 384),
        vmem(LEN, 128, dtype=F32),
        vmem(LEN, 128, dtype=F32),
        vmem(LEN, 128, dtype=F32),
        vmem(LEN, 128, dtype=F32),
        vmem(4, 256, D),
        vmem(4, TOK, D),
        vmem(2, TOK // 2, D),
        vmem(2, TOK, D),
        vmem(TOK, D, dtype=F32),
        vmem(TOK, D, dtype=F32),
        vmem(8, D, dtype=F32),
        vmem(3, 8, 2 * FEAT, dtype=F32),
        vmem(8, FEAT, dtype=F32),
        vmem(8, FEAT, dtype=F32),
        vmem(8, 8, FEAT, dtype=F32),
        vmem(4, ff, FEAT),
        vmem(3, ff, FEAT),
        vmem(8, FEAT // 2, ff),
        vmem(3, 2, FEAT // 2, ff),
        vmem(FEAT // 2, ff),
        vmem(FEAT, ff),
        vmem(3, 2 * FEAT, ff),
        vmem(4, 256, FEAT),
        vmem(3, 256, FEAT),
        vmem(4, FEAT, 384),
        vmem(3, FEAT, 384),
        dma((2, 16)),
        dma((2, 16)),
        dma((2, 2)),
        dma((4, RowGather.SEMS)),
        dma((4, RowGather.SEMS)),
        dma((3,)),
        dma((6, SplitGather.SEMS)),
        dma((6, SplitGather.SEMS)),
        dma((6,)),
        dma((4, RowSum.SEMS)),
        dma((4, RowSum.SEMS)),
        dma((6, SplitSum.SEMS)),
        dma((6, SplitSum.SEMS)),
        dma((2, 8)),
        dma((2, 8)),
        dma((2,)),
        dma((9,)),
        dma((9,)),
        dma((8,)),
        pltpu.SemaphoreType.REGULAR((4,)),
    ]
    return pl.pallas_call(
        layer_kernel,
        out_shape=outs,
        in_specs=[any_space] * 8 + [vmem_space] * 2,
        out_specs=tuple(any_space for _ in outs),
        scratch_shapes=scratch,
        compiler_params=pltpu.CompilerParams(
            collective_id=0, has_side_effects=True, vmem_limit_bytes=VMEM_BYTES
        ),
        cost_estimate=pl.CostEstimate(flops=36 * 10**9, bytes_accessed=60 * 10**6, transcendentals=0),
        name="decoder_layer",
    )(*args)


def partner_of(values):
    pairs = [(a, a ^ 1) for a in range(lax.axis_size("row"))]
    return lax.ppermute(values, "row", pairs)


def body(
    hidden_in,
    segment_ids,
    attn_gain,
    w_query,
    w_key,
    w_value,
    w_out,
    mlp_gain,
    w_gate,
    w_up,
    w_down,
    grad_output,
):
    upper = lax.axis_index("row") % 2 == 1
    query_width = w_query.shape[1]
    kv_width = w_key.shape[1]
    frequency = jnp.exp(jnp.arange(0, HD, 2, dtype=F32) * (-math.log(10000.0) / HD))
    frequency = jnp.tile(frequency, 4)[None]
    gains = jnp.concatenate(
        [attn_gain[None], mlp_gain[None], jnp.zeros((6, attn_gain.shape[0]), F32)], axis=0
    )
    kv_own = jnp.concatenate([w_key, w_value], axis=1)
    kv_other = partner_of(kv_own)
    kv_first = jnp.where(upper, kv_other, kv_own)
    kv_second = jnp.where(upper, kv_own, kv_other)
    w_project = jnp.concatenate(
        [
            w_query,
            kv_first[:, :kv_width],
            kv_second[:, :kv_width],
            kv_first[:, kv_width:],
            kv_second[:, kv_width:],
        ],
        axis=1,
    )
    (
        layer_output,
        grad_input,
        gd_own,
        gd_far,
        gg_own,
        gg_far,
        gu_own,
        gu_far,
        go_own,
        go_far,
        gp_own,
        gp_far,
        kv_own,
        kv_far,
        d_gains,
        _,
        _,
    ) = layer_call(
        hidden_in,
        grad_output,
        w_project,
        w_out,
        w_gate,
        w_up,
        w_down,
        gains,
        segment_ids,
        frequency,
    )

    def both(own, far):
        return own.astype(F32) + far.astype(F32)

    grad_kv = both(gp_own[:, query_width:], gp_far[:, query_width:]) + both(kv_own, kv_far)
    grad_kv = grad_kv.reshape(-1, 2, 2, kv_width)
    grad_kv = jnp.where(upper, grad_kv[:, :, 1], grad_kv[:, :, 0])
    second = (lax.axis_index("dp") + lax.axis_index("col")) % 2 == 1
    grad_gate = jnp.concatenate(
        [jnp.where(second, gg_far, gg_own), jnp.where(second, gg_own, gg_far)], axis=0
    )
    return (
        layer_output,
        grad_input.astype(F32),
        d_gains[0],
        both(gp_own[:, :query_width], gp_far[:, :query_width]),
        grad_kv[:, 0],
        grad_kv[:, 1],
        both(go_own, go_far),
        d_gains[1],
        grad_gate.astype(F32),
        both(gu_own, gu_far),
        both(gd_own, gd_far),
    )


def solution(mesh):
    return jax.shard_map(
        body,
        mesh=mesh,
        in_specs=(
            P(("dp", "row"), "col"),
            P(("dp", "col"), None),
            P("col"),
            P("col", "row"),
            P("col", "row"),
            P("col", "row"),
            P("row", "col"),
            P("col"),
            P("col", "row"),
            P("col", "row"),
            P("row", "col"),
            P(("dp", "row"), "col"),
        ),
        out_specs=(
            P(("dp", "row"), "col"),
            P(("dp", "row"), "col"),
            P("col"),
            P("col", "row"),
            P("col", "row"),
            P("col", "row"),
            P("row", "col"),
            P("col"),
            P("col", "row"),
            P("col", "row"),
            P("row", "col"),
        ),
        check_vma=False,
    )
```

```python
import functools
import math

import jax
import jax.numpy as jnp
from jax import lax
from jax.experimental import pallas as pl
from jax.experimental.pallas import tpu as pltpu
from jax.sharding import PartitionSpec as P

D = 2048
HD = 64
LEN = 1024
ROWS = 8
CHIPS = 4
TOK = LEN // ROWS
FEAT = D // 8
EPSILON = 1e-05
FLOOR_SCORE = -1e30
BF16 = jnp.bfloat16
F32 = jnp.float32
MESH = pl.DeviceIdType.MESH
VMEM_BYTES = 62 * 2**20


def remote(src, dst, send, recv, device):
    return pltpu.make_async_remote_copy(
        src_ref=src, dst_ref=dst, send_sem=send, recv_sem=recv, device_id=device, device_id_type=MESH
    )


def meet(peers):
    barrier = pltpu.get_barrier_semaphore()
    for peer in peers:
        pl.semaphore_signal(barrier, inc=1, device_id=peer, device_id_type=MESH)
    pl.semaphore_wait(barrier, len(peers))


def ds(start, size):
    return pl.ds(pl.multiple_of(start, size), size)


class Place:
    def __init__(self):
        self.d = lax.axis_index("dp")
        self.r = lax.axis_index("row")
        self.c = lax.axis_index("col")
        self.y, self.k = self.r // 2, lax.rem(self.r, 2)
        self.x, self.h = self.c // 2, lax.rem(self.c, 2)
        self.partner = {"row": self.y * 2 + 1 - self.k}
        self.up = {"row": self.row_of(1)}
        self.down = {"row": self.row_of(3)}
        self.other = {"dp": 1 - self.d, "col": self.x * 2 + 1 - self.h}
        self.twin = {"dp": 1 - self.d}
        self.half = lax.rem(self.d + self.h, 2)
        self.x_peers = [{"col": self.col_of(s)} for s in (1, 3, 2)]

    def row_of(self, step):
        return lax.rem(self.y + step, CHIPS) * 2 + self.k

    def col_of(self, step):
        return lax.rem(self.x + step, 4) * 2 + self.h

    def col_from(self, step):
        return lax.rem(self.x + 4 - step, 4) * 2 + self.h


class RowGather:
    SEMS = 13

    def __init__(self, here, place, shard, send, recv):
        self.here, self.place = here, place
        y, k = here.y, here.k
        self.low, self.high, self.far_row = here.row_of(3), here.row_of(1), here.row_of(2)
        self.ups = [
            remote(shard(a), place(here.r, a), send.at[a], recv.at[a], here.up) for a in (0, 1)
        ]
        self.downs = [
            remote(shard(a), place(here.r, a), send.at[2 + a], recv.at[2 + a], here.down)
            for a in (0, 1)
        ]
        self.fars = [
            self.hand_on(self.low, 0, send.at[4], recv.at[4], here.up),
            self.hand_on(self.high, 1, send.at[5], recv.at[5], here.down),
        ]
        self.passes = {}
        for index, (row, a) in enumerate(
            [(self.low, 0), (self.low, 1), (self.high, 0), (self.high, 1), (self.far_row, 0), (self.far_row, 1)]
        ):
            self.passes[index] = self.hand_on(
                row, a, send.at[6 + index], recv.at[6 + index], here.partner
            )
        self.own = [
            remote(shard(None), place(here.r, None), send.at[12], recv.at[12], here.partner)
        ]

    def hand_on(self, row, a, send, recv, device):
        return remote(self.place(row, a), self.place(row, a), send, recv, device)

    def start(self):
        for a, b in ((0, 1), (1, 0)):
            self.ups[a].start()
            self.downs[b].start()
        self.own[0].start()

    def near(self):
        for a, b in ((0, 1), (1, 0)):
            self.ups[a].wait_recv()
            if a == 0:
                self.fars[0].start()
            self.passes[a].start()
            self.downs[b].wait_recv()
            if b == 1:
                self.fars[1].start()
            self.passes[2 + b].start()

    def far(self):
        for a in (0, 1):
            self.fars[a].wait_recv()
            self.passes[4 + a].start()

    def got_own(self):
        self.own[0].wait_recv()

    def got_near(self):
        for index in range(4):
            self.passes[index].wait_recv()

    def got_far(self):
        for index in (4, 5):
            self.passes[index].wait_recv()

    def sent(self):
        for copy in self.ups + self.downs + self.fars + self.own + list(self.passes.values()):
            copy.wait_send()


class ColGather:
    SEMS = 7

    def __init__(self, here, shard, place, send, recv, local, across_first):
        self.here, self.place, self.across_first = here, place, across_first
        self.local = pltpu.make_async_copy(shard, place(here.c), local)
        self.lines = [
            remote(shard, place(here.c), send.at[i], recv.at[i], here.x_peers[i]) for i in range(3)
        ]
        self.across = [remote(shard, place(here.c), send.at[3], recv.at[3], here.other)]
        there = here.x * 2 + 1 - here.h
        if across_first:
            self.seconds = [
                remote(place(there), place(there), send.at[4 + i], recv.at[4 + i], here.x_peers[i])
                for i in range(3)
            ]
        else:
            self.seconds = []
            for i, step in enumerate((1, 3, 2)):
                source = here.col_from(step)
                self.seconds.append(
                    remote(place(source), place(source), send.at[4 + i], recv.at[4 + i], here.other)
                )

    def start(self):
        self.start_across()
        self.start_lines()

    def start_across(self):
        self.local.start()
        self.across[0].start()

    def start_lines(self):
        for copy in self.lines:
            copy.start()

    def middle(self):
        if self.across_first:
            self.across[0].wait_recv()
            for copy in self.seconds:
                copy.start()
        else:
            for copy, second in zip(self.lines, self.seconds):
                copy.wait_recv()
                second.start()

    def end(self):
        self.local.wait()
        if self.across_first:
            for copy in self.lines:
                copy.wait_recv()
        else:
            self.across[0].wait_recv()
        for copy in self.seconds:
            copy.wait_recv()
        for copy in self.lines + self.across + self.seconds:
            copy.wait_send()


class SplitGather:
    SEMS = 14

    def __init__(self, here, shard, place, send, recv, local):
        self.here, self.place = here, place
        half = here.half
        self.local = pltpu.make_async_copy(shard(None), place(here.c, None), local)

        def hand_on(c, index, device):
            return remote(place(c, half), place(c, half), send.at[index], recv.at[index], device)

        own = place(here.c, half)
        self.across = remote(shard(half), own, send.at[0], recv.at[0], here.other)
        self.lines = [
            remote(shard(half), own, send.at[1 + i], recv.at[1 + i], here.x_peers[i]) for i in range(3)
        ]
        there = here.x * 2 + 1 - here.h
        self.seconds = [hand_on(there, 4 + i, here.x_peers[i]) for i in range(3)]
        sources = [here.col_from(step) for step in (1, 3, 2)]
        others = [source + 1 - 2 * here.h for source in sources]
        self.swaps = [
            hand_on(c, 7 + i, here.twin) for i, c in enumerate([there] + sources + others)
        ]

    def start_across(self):
        self.local.start()
        self.across.start()

    def start_lines(self):
        for copy in self.lines:
            copy.start()

    def middle(self):
        self.across.wait_recv()
        for copy in self.seconds:
            copy.start()
        self.swaps[0].start()

    def late(self, which):
        copies = self.seconds if which else self.lines
        for copy, swap in zip(copies, self.swaps[1 + 3 * which :]):
            copy.wait_recv()
            swap.start()

    def end(self):
        self.local.wait()
        for swap in self.swaps:
            swap.wait_recv()
        for copy in [self.across] + self.lines + self.seconds + self.swaps:
            copy.wait_send()


class RowSum:
    SEMS = 10

    def __init__(self, here, blocks, paired, relayed, landed, send, recv):
        self.here, self.blocks, self.paired = here, blocks, paired
        self.relayed, self.landed = relayed, landed
        k, half = here.k, TOK // 2
        self.mine, self.half = k * TOK, half
        self.pairs = [
            remote(
                blocks.at[s, ds((1 - k) * TOK, TOK)], paired.at[s], send.at[s], recv.at[s], here.partner
            )
            for s in range(4)
        ]
        self.fars = [
            remote(self.part(2, 0), relayed.at[0], send.at[4], recv.at[4], here.up),
            remote(self.part(2, 1), relayed.at[1], send.at[5], recv.at[5], here.down),
        ]
        self.nears = {}
        for index, (s, a, device) in enumerate(
            [(1, 1, here.up), (3, 0, here.down), (1, 0, here.up), (3, 1, here.down)]
        ):
            slot = 0 if s == 1 else 1
            self.nears[s, a] = remote(
                self.part(s, a),
                landed.at[slot, pl.ds(a * half, half)],
                send.at[6 + index],
                recv.at[6 + index],
                device,
            )

    def part(self, s, a):
        return self.blocks.at[s, ds(self.mine + a * self.half, self.half)]

    def add(self, s, a, other):
        part = self.part(s, a)
        part[...] = (part[...].astype(F32) + other[...].astype(F32)).astype(BF16)

    def pair(self, s):
        self.pairs[s].start()

    def join(self, s):
        self.pairs[s].wait_recv()
        for a in (0, 1):
            self.add(s, a, self.paired.at[s, pl.ds(a * self.half, self.half)])

    def far(self):
        self.join(2)
        self.fars[0].start()
        self.fars[1].start()

    def near(self):
        self.join(1)
        self.nears[1, 1].start()
        self.join(3)
        self.nears[3, 0].start()

    def relay(self):
        self.fars[0].wait_recv()
        self.add(1, 0, self.relayed.at[0])
        self.nears[1, 0].start()
        self.fars[1].wait_recv()
        self.add(3, 1, self.relayed.at[1])
        self.nears[3, 1].start()

    def arrive(self):
        self.pairs[0].wait_recv()
        for copy in self.nears.values():
            copy.wait_recv()

    def total(self, start, rows):
        own = self.blocks[0, pl.ds(pl.multiple_of(self.mine + start, rows), rows)].astype(F32)
        here = pl.ds(pl.multiple_of(start, rows), rows)
        return (
            own
            + self.paired[0, here].astype(F32)
            + self.landed[0, here].astype(F32)
            + self.landed[1, here].astype(F32)
        )

    def sent(self):
        for copy in self.pairs + self.fars + list(self.nears.values()):
            copy.wait_send()


def add_rows(rows, target, others):
    kind = target.dtype

    def step(t, carry):
        at = ds(t * rows, rows)
        total = target[at, :].astype(F32)
        for other in others:
            total = total + other[at, :].astype(F32)
        target[at, :] = total.astype(kind)
        return carry

    lax.fori_loop(0, target.shape[0] // rows, step, 0)


class WeightSum:
    SEMS = 8

    def __init__(self, here, part, wide_part, rows, z_land, x_land, far_part, send, recv, across_first):
        self.here, self.part, self.across_first, self.rows = here, part, across_first, rows
        self.z_land, self.x_land = z_land, x_land
        self.own = part(here.c)
        steps = (1, 3, 2)
        if across_first:
            self.mine = [part(x * 2 + here.h) for x in range(4)]
            self.across = [
                remote(part(x * 2 + 1 - here.h), z_land.at[x], send.at[x], recv.at[x], here.other)
                for x in range(4)
            ]
            self.lines = [
                remote(
                    part(here.col_of(step)), x_land.at[i], send.at[4 + i], recv.at[4 + i], here.x_peers[i]
                )
                for i, step in enumerate(steps)
            ]
        else:
            self.wide = wide_part(here.x)
            self.across = [
                remote(
                    part(here.x * 2 + 1 - here.h), z_land, send.at[3], recv.at[3], here.other
                )
            ]
            self.lines = [
                remote(
                    wide_part(lax.rem(here.x + step, 4)),
                    x_land.at[i],
                    send.at[i],
                    recv.at[i],
                    here.x_peers[i],
                )
                for i, step in enumerate(steps)
            ]
        self.swap = remote(self.own, far_part, send.at[7], recv.at[7], here.twin)

    def add(self, target, others):
        add_rows(self.rows, target, others)

    def start(self):
        for copy in self.across if self.across_first else self.lines:
            copy.start()

    def middle(self):
        if self.across_first:
            for x in range(4):
                self.across[x].wait_recv()
                self.add(self.mine[x], [self.z_land.at[x]])
            for copy in self.lines:
                copy.start()
        else:
            for copy in self.lines:
                copy.wait_recv()
            self.add(self.wide, [self.x_land.at[i] for i in range(3)])
            self.across[0].start()

    def last(self):
        if self.across_first:
            for copy in self.lines:
                copy.wait_recv()
            self.add(self.own, [self.x_land.at[i] for i in range(3)])
        else:
            self.across[0].wait_recv()
            self.add(self.own, [self.z_land])
        self.swap.start()

    def end(self):
        self.swap.wait()
        for copy in self.across + self.lines:
            copy.wait_send()


class SplitSum:
    SEMS = 16

    def __init__(self, here, part, rows, twin_land, x_land, z_land, far_part, send, recv):
        self.here, self.rows = here, rows
        self.twin_land, self.x_land, self.z_land = twin_land, x_land, z_land
        half, x, h = here.half, here.x, here.h
        self.mine = [part(c, half) for c in range(8)]
        self.twins = [
            remote(part(c, 1 - half), twin_land.at[c], send.at[c], recv.at[c], here.twin)
            for c in range(8)
        ]
        self.lines = []
        for i, step in enumerate((1, 3, 2)):
            target = lax.rem(x + step, 4) * 2
            for side in range(2):
                index = 8 + 2 * i + side
                self.lines.append(
                    remote(
                        part(target + side, half),
                        x_land.at[i, side],
                        send.at[index],
                        recv.at[index],
                        here.x_peers[i],
                    )
                )
        self.sides = [part(x * 2 + side, half) for side in range(2)]
        self.across = remote(part(x * 2 + 1 - h, half), z_land, send.at[14], recv.at[14], here.other)
        self.own = part(here.c, half)
        self.swap = remote(self.own, far_part, send.at[15], recv.at[15], here.twin)

    def add(self, target, others):
        add_rows(self.rows, target, others)

    def start(self):
        for copy in self.twins:
            copy.start()

    def middle(self):
        for c in range(8):
            self.twins[c].wait_recv()
            self.add(self.mine[c], [self.twin_land.at[c]])
        for copy in self.lines:
            copy.start()

    def late(self):
        for copy in self.lines:
            copy.wait_recv()
        for side in range(2):
            self.add(self.sides[side], [self.x_land.at[i, side] for i in range(3)])
        self.across.start()

    def last(self):
        self.across.wait_recv()
        self.add(self.own, [self.z_land])
        self.swap.start()

    def end(self):
        self.swap.wait()
        for copy in self.twins + self.lines + [self.across]:
            copy.wait_send()


class Spread:
    def __init__(self, here, source, target, send, recv, local):
        self.here = here
        self.same = here.r == here.c
        self.copies = []
        place = target.at[ds(here.r * TOK, TOK)]
        for j in range(8):
            shard = source.at[:, pl.ds(j * FEAT, FEAT)]
            self.copies.append(
                (
                    remote(shard, place, send.at[j], recv.at[here.r], {"row": here.c, "col": j}),
                    pltpu.make_async_copy(shard, place, local),
                )
            )
        self.arrivals = [
            remote(
                source.at[:, pl.ds(0, FEAT)],
                target.at[pl.ds(i * TOK, TOK)],
                send.at[i],
                recv.at[i],
                {"row": here.c, "col": i},
            )
            for i in range(8)
        ]

    def each(self, index, other, own):
        itself = self.same & (self.here.r == index)
        pl.when(itself)(own)
        pl.when(jnp.logical_not(itself))(other)

    def start(self):
        for j, (copy, local) in enumerate(self.copies):
            self.each(j, copy.start, local.start)

    def end(self):
        for j, (copy, local) in enumerate(self.copies):
            self.each(j, copy.wait_send, local.wait)
        for i, copy in enumerate(self.arrivals):
            self.each(i, copy.wait_recv, lambda: None)


class Collect:
    def __init__(self, here, source, middle, target, send, recv, local):
        self.here = here
        r, c = here.r, here.c
        self.local = pltpu.make_async_copy(source.at[ds(r * TOK, TOK)], middle.at[r], local.at[0])
        self.firsts = []
        self.seconds = []
        lanes = target.at[:, ds(c * FEAT, FEAT)]
        for k in range(1, 8):
            i = lax.rem(r + k, 8)
            self.firsts.append(
                remote(
                    source.at[ds(i * TOK, TOK)], middle.at[r], send.at[k], recv.at[k], {"row": i}
                )
            )
        for k in range(8):
            a = lax.rem(r + 8 - k, 8)
            self.seconds.append(
                (
                    a == c,
                    remote(middle.at[a], lanes, send.at[8 + k], recv.at[8 + c], {"col": a}),
                    pltpu.make_async_copy(middle.at[a], lanes, local.at[1]),
                )
            )
        self.arrivals = [
            (
                c == j,
                remote(
                    middle.at[0],
                    target.at[:, pl.ds(j * FEAT, FEAT)],
                    send.at[8 + j],
                    recv.at[8 + j],
                    {"col": j},
                ),
            )
            for j in range(8)
        ]

    def start(self):
        self.local.start()
        for copy in self.firsts:
            copy.start()

    def turn(self):
        self.local.wait()
        for k, (itself, copy, local) in enumerate(self.seconds):
            if k > 0:
                self.firsts[k - 1].wait_recv()
            pl.when(itself)(local.start)
            pl.when(jnp.logical_not(itself))(copy.start)

    def arrive(self):
        for itself, copy, local in self.seconds:
            pl.when(itself)(local.wait)
        for itself, copy in self.arrivals:
            pl.when(jnp.logical_not(itself))(copy.wait_recv)

    def sent(self):
        for copy in self.firsts:
            copy.wait_send()
        for itself, copy, local in self.seconds:
            pl.when(jnp.logical_not(itself))(copy.wait_send)


def nn(a, b):
    return jnp.dot(a, b, preferred_element_type=F32)


def nt(a, b):
    return lax.dot_general(a, b, (((1,), (1,)), ((), ())), preferred_element_type=F32)


def tn(a, b):
    return lax.dot_general(a, b, (((0,), (0,)), ((), ())), preferred_element_type=F32)


def swap_halves(values):
    width = values.shape[-1]
    lane = lax.broadcasted_iota(jnp.int32, values.shape, 1)
    return jnp.where(
        lax.rem(lane, HD) < HD // 2, pltpu.roll(values, width - HD // 2, 1), pltpu.roll(values, HD // 2, 1)
    )


def turn(values, cos, sin):
    return values * cos + swap_halves(values) * sin


def gain_row(gains, which):
    return jnp.concatenate([gains[pl.ds(8 * j + which, 1), :] for j in range(8)], axis=1)


def layer_kernel(
    x_in,
    g_in,
    wq_in,
    wk_in,
    wv_in,
    wo_in,
    wg_in,
    wu_in,
    wd_in,
    gain_in,
    seg_in,
    layer_out,
    input_out,
    gd_own,
    gd_far,
    gg_own,
    gg_far,
    gu_own,
    gu_far,
    go_own,
    go_far,
    gq_own,
    gq_far,
    kv_out,
    gains_out,
    normed_kept,
    g_middle,
    x_middle,
    x_mine,
    low_rows,
    wide,
    g_all,
    act,
    gate,
    up,
    wd,
    gd,
    wg,
    wu,
    wo,
    wq,
    wkv,
    kv_shard,
    kv_far,
    kv_total,
    kv_land,
    kv_final,
    gains,
    cos,
    sin,
    seg_col,
    query,
    k_low,
    k_high,
    v_low,
    v_high,
    mixed,
    totals,
    d_mixed,
    d_projected,
    dk_low,
    dk_high,
    dv_low,
    dv_high,
    blocks,
    paired,
    relayed,
    landed,
    residual,
    d_residual,
    gain_sums,
    gain_x,
    gain_z,
    gain_far,
    gain_rows,
    gd_z,
    gd_x,
    gg_twin,
    gg_x,
    gg_z,
    gu_z,
    gu_x,
    go_z,
    go_x,
    gq_z,
    gq_x,
    kv_z,
    kv_x,
    collect_send,
    collect_recv,
    collect_local,
    gather_send,
    gather_recv,
    gather_local,
    w_send,
    w_recv,
    w_local,
    rows_send,
    rows_recv,
    sum_send,
    sum_recv,
    spread_send,
    spread_recv,
    spread_local,
    last_send,
    last_recv,
    keep_sem,
    free,
):
    here = Place()
    same = here.r == here.c
    barrier = pltpu.get_barrier_semaphore()
    row_peers = [{"row": lax.rem(here.r + k, ROWS)} for k in range(1, ROWS)]
    col_peers = [{"col": lax.rem(here.c + k, 8)} for k in range(1, 8)]
    peers = row_peers + col_peers + [here.other, here.twin]
    for peer in peers:
        pl.semaphore_signal(barrier, inc=1, device_id=peer, device_id_type=MESH)
    for i in range(8):

        @pl.when(jnp.logical_not(same & (here.r == i)))
        def _():
            pl.semaphore_signal(
                barrier, inc=1, device_id={"row": i, "col": here.r}, device_id_type=MESH
            )

    pl.semaphore_wait(barrier, len(peers) + 8 - same.astype(jnp.int32))

    def token_place(ref):
        def place(row, a):
            if a is None:
                return ref.at[ds(row * TOK, TOK)]
            return ref.at[ds(row * TOK + a * (TOK // 2), TOK // 2)]

        return place

    def own_part(ref):
        place = token_place(ref)
        return lambda a: place(here.r, a)

    def low_part(a):
        return low_rows if a is None else low_rows.at[pl.ds(a * (TOK // 2), TOK // 2)]

    def row_gather(index, ref, shard):
        return RowGather(here, token_place(ref), shard, gather_send.at[index], gather_recv.at[index])

    def row_sum(index):
        return RowSum(here, blocks, paired, relayed, landed, rows_send.at[index], rows_recv.at[index])

    def collect(index, source, middle, target):
        return Collect(
            here,
            source,
            middle,
            target,
            collect_send.at[index],
            collect_recv.at[index],
            collect_local.at[index],
        )

    def spread(index, target):
        return Spread(
            here,
            low_rows,
            target,
            spread_send.at[index],
            spread_recv.at[index],
            spread_local.at[index],
        )

    def col_gather(index, shard, place, across_first):
        return ColGather(
            here, shard, place, w_send.at[index], w_recv.at[index], w_local.at[index], across_first
        )

    def split_gather(index, shard, ref):
        half = ref.shape[0] // 2

        def place(c, a):
            lanes = ds(c * FEAT, FEAT)
            return ref.at[:, lanes] if a is None else ref.at[ds(a * half, half), lanes]

        def part(a):
            return shard if a is None else shard.at[ds(a * half, half)]

        return SplitGather(
            here, part, place, w_send.at[index], w_recv.at[index], w_local.at[index]
        )

    def weight_sum(index, parts, rows, z_land, x_land, far_part, across_first):
        return WeightSum(
            here,
            parts[0],
            parts[1],
            rows,
            z_land,
            x_land,
            far_part,
            sum_send.at[index],
            sum_recv.at[index],
            across_first,
        )

    def rows_of(ref):
        return lambda c: ref.at[ds(c * FEAT, FEAT)], lambda x: ref.at[ds(x * 2 * FEAT, 2 * FEAT)]

    def lanes_of(ref):
        return (
            lambda c: ref.at[:, ds(c * FEAT, FEAT)],
            lambda x: ref.at[:, ds(x * 2 * FEAT, 2 * FEAT)],
        )

    def credit(index):
        for peer in (here.partner, here.up, here.down):
            pl.semaphore_signal(free.at[index], inc=1, device_id=peer, device_id_type=MESH)

    def chip_rows(s):
        return ds(lax.rem(here.y + s, CHIPS) * 256, 256)

    kept = []

    def keep(src, dst):
        copy = pltpu.make_async_copy(src, dst, keep_sem.at[len(kept)])
        copy.start()
        kept.append(copy)
        return copy

    x_collect = collect(0, x_in, x_middle, x_mine)
    g_collect = collect(1, g_in, g_middle, low_rows)
    n1_gather = row_gather(0, wide, own_part(wide))
    g_gather = row_gather(1, g_all, low_part)
    n2_gather = row_gather(2, wide, own_part(wide))
    d_gather = row_gather(3, g_all, low_part)
    gain_gather = col_gather(0, gain_in, lambda c: gains.at[ds(c * 8, 8)], True)
    wq_gather = col_gather(1, wq_in, lambda c: wq.at[ds(c * FEAT, FEAT)], True)
    kv_gather = col_gather(2, kv_shard, lambda c: wkv.at[:, ds(c * FEAT, FEAT)], True)
    wo_gather = col_gather(3, wo_in, lambda c: wo.at[:, ds(c * FEAT, FEAT)], False)
    wd_gather = col_gather(4, wd_in, lambda c: wd.at[:, ds(c * FEAT, FEAT)], False)
    wg_gather = split_gather(5, wg_in, wg)
    wu_gather = split_gather(6, wu_in, wu)
    d_sum = weight_sum(0, lanes_of(gd), 32, gd_z, gd_x, gd_far, False)
    u_sum = weight_sum(1, lanes_of(wu), 64, gu_z, gu_x, gu_far, True)
    o_sum = weight_sum(2, lanes_of(wo), 64, go_z, go_x, go_far, True)
    q_sum = weight_sum(3, rows_of(wq), 64, gq_z, gq_x, gq_far, True)
    kv_sum = weight_sum(4, lanes_of(wkv), 32, kv_z, kv_x, kv_far, False)
    gain_sum = weight_sum(5, lanes_of(gain_sums), 8, gain_z, gain_x, gain_far, False)
    g_half = wg.shape[0] // 2
    g_sum = SplitSum(
        here,
        lambda c, a: wg.at[ds(a * g_half, g_half), ds(c * FEAT, FEAT)],
        32,
        gg_twin,
        gg_x,
        gg_z,
        gg_far,
        sum_send.at[6],
        sum_recv.at[6],
    )
    kv_copies = []
    for index, part in enumerate((wk_in, wv_in)):
        rows = ds(index * HD + here.k * (HD // 2), HD // 2)
        local = pltpu.make_async_copy(part, kv_shard.at[rows], gather_local.at[3 + index])
        other = remote(
            part, kv_shard.at[rows], last_send.at[9 + index], last_recv.at[9 + index], here.partner
        )
        kv_copies += [local, other]

    for copy in kv_copies:
        copy.start()
    gain_gather.start()
    wq_gather.start_across()
    x_collect.start()
    wq_gather.start_lines()
    segments = seg_in[0:1, :]
    places = lax.broadcasted_iota(jnp.int32, (1, LEN), 1)
    for number in range(3):
        count = jnp.sum((segments == number).astype(F32), axis=1, keepdims=True).astype(jnp.int32)
        places = places - jnp.where(segments > number, count, 0)
    tall = jnp.transpose(jnp.broadcast_to(places.astype(F32), (128, LEN)))
    lanes = lax.broadcasted_iota(jnp.int32, (1, 128), 1)
    step = (2 * lax.rem(lanes, HD // 2)).astype(F32)
    angles = tall * jnp.exp(step * (-math.log(10000.0) / HD))
    sign = jnp.where(lax.rem(lanes, HD) < HD // 2, -1.0, 1.0)
    cos[...] = jnp.cos(angles)
    sin[...] = jnp.sin(angles) * sign
    seg_col[...] = jnp.transpose(jnp.broadcast_to(segments.astype(F32), (128, LEN)))
    seg_row = segments.astype(F32)
    wg_gather.start_across()
    gain_gather.middle()
    wq_gather.middle()
    for copy in kv_copies:
        copy.wait()
    kv_gather.start_across()
    x_collect.turn()
    g_collect.start()
    wu_gather.start_across()
    gain_gather.end()
    gain_one = gain_row(gains, 0)
    x_collect.arrive()
    kv_gather.start_lines()
    kv_gather.middle()

    def norm_rows(t, carry):
        values = x_mine[ds(t * 16, 16), :].astype(F32)
        scale = lax.rsqrt(jnp.sum(values * values, axis=1, keepdims=True) * (1.0 / D) + EPSILON)
        wide[ds(here.r * TOK + t * 16, 16), :] = (values * scale * gain_one).astype(BF16)
        return carry

    lax.fori_loop(0, TOK // 16, norm_rows, 0)
    wg_gather.start_lines()
    n1_gather.start()
    lane = lax.broadcasted_iota(jnp.int32, (256, 128), 1)

    def project(s):
        rows = chip_rows(s)
        values = wide[rows, :]
        projected = nn(values, wq[...])
        cos_rows, sin_rows = cos[rows, :], sin[rows, :]
        for p in range(2):
            pair = turn(projected[:, p * 128 : (p + 1) * 128], cos_rows, sin_rows)
            query[rows, pl.ds(p * 128, 128)] = (pair * HD**-0.5).astype(BF16)
        key_value = nt(values, wkv[...])
        key = jnp.where(lane < HD, turn(key_value, cos_rows, sin_rows), 0.0)
        value = jnp.where(lane < HD, 0.0, key_value)
        k_low[rows, :] = key.astype(BF16)
        k_high[rows, :] = pltpu.roll(key, HD, 1).astype(BF16)
        v_high[rows, :] = value.astype(BF16)
        v_low[rows, :] = pltpu.roll(value, HD, 1).astype(BF16)

    n1_gather.near()
    wg_gather.middle()
    g_collect.turn()
    n1_gather.far()
    wg_gather.late(0)
    wq_gather.end()
    kv_gather.end()
    n1_gather.got_own()
    project(0)
    n1_gather.got_near()
    project(1)
    project(3)
    n1_gather.got_far()
    project(2)
    wo_gather.start()
    normed_copy = keep(wide, normed_kept)
    g_collect.arrive()
    own_g = pltpu.make_async_copy(low_rows, token_place(g_all)(here.r, None), gather_local.at[0])
    own_g.start()
    g_gather.start()

    def bias_of(block, keys):
        first = block * 256
        row = lax.broadcasted_iota(jnp.int32, (256, keys), 0) + first
        key = lax.broadcasted_iota(jnp.int32, (256, keys), 1)
        alike = seg_col[pl.ds(first, 256), 0:1] == seg_row[:, :keys]
        return jnp.where(alike & (key <= row), 0.0, FLOOR_SCORE)

    def attend(block):
        keys = (block + 1) * 256
        rows, seen = pl.ds(block * 256, 256), pl.ds(0, keys)
        bias = bias_of(block, keys)

        def one_pair(p, sums):
            lanes = ds(p * 128, 128)
            pair = query[rows, lanes]
            out = jnp.zeros((256, 128), F32)
            for side, (key, value) in enumerate(((k_low, v_low), (k_high, v_high))):
                scores = nt(pair, key[seen, :]) + bias
                row_max = jnp.max(scores, axis=1, keepdims=True)
                exps = jnp.exp(scores - row_max)
                row_sum = jnp.sum(exps, axis=1, keepdims=True)
                out = out + nn(exps.astype(BF16), value[seen, :]) * (1.0 / row_sum)
                sums = jnp.where(lane == 2 * p + side, row_max + jnp.log(row_sum), sums)
            mixed[rows, lanes] = out.astype(BF16)
            return sums

        totals[rows, :] = lax.fori_loop(0, 2, one_pair, jnp.zeros((256, 128), F32))

    attend(0)
    attend(1)
    wo_gather.middle()
    wg_gather.late(1)
    wu_gather.start_lines()
    attend(2)
    g_gather.near()
    attend(3)
    wd_gather.start()
    wu_gather.middle()
    wo_gather.end()
    normed_copy.wait()
    n1_gather.sent()
    out_sum = row_sum(0)
    for s in (2, 1, 3, 0):
        blocks[s] = nn(mixed[chip_rows(s), :], wo[...]).astype(BF16)
        out_sum.pair(s)
        if s == 1:
            out_sum.far()
    out_sum.near()
    wu_gather.late(0)
    out_sum.relay()
    wu_gather.late(1)
    out_sum.arrive()
    g_gather.far()
    gain_two = gain_row(gains, 4)

    def residual_rows(t, carry):
        rows = ds(t * 16, 16)
        values = x_mine[rows, :].astype(F32) + out_sum.total(t * 16, 16)
        residual[rows, :] = values
        scale = lax.rsqrt(jnp.sum(values * values, axis=1, keepdims=True) * (1.0 / D) + EPSILON)
        wide[ds(here.r * TOK + t * 16, 16), :] = (values * scale * gain_two).astype(BF16)
        return carry

    lax.fori_loop(0, TOK // 16, residual_rows, 0)
    n2_gather.start()
    wd_gather.middle()
    credit(0)
    out_sum.sent()
    wg_gather.end()
    wu_gather.end()

    def feed(s):
        rows = chip_rows(s)
        values = wide[rows, :]
        gate_rows = nt(values, wg[...])
        up_rows = nt(values, wu[...])
        gate[rows, :] = gate_rows.astype(BF16)
        up[rows, :] = up_rows.astype(BF16)
        act[rows, :] = (gate_rows * (1.0 / (1.0 + jnp.exp(-gate_rows))) * up_rows).astype(BF16)

    n2_gather.got_own()
    feed(0)
    n2_gather.near()
    n2_gather.got_near()
    feed(1)
    n2_gather.far()
    feed(3)
    n2_gather.got_far()
    feed(2)

    g_gather.got_own()
    g_gather.got_near()
    g_gather.got_far()
    own_g.wait()
    wd_gather.end()
    first_sum = row_sum(1)
    pl.semaphore_wait(free.at[0], 3)

    def down_grad(j, carry):
        lanes = ds(j * 512, 512)
        gd[:, lanes] = tn(act[...], g_all[:, lanes]).astype(BF16)
        return carry

    for s in (2, 1, 3, 0):
        rows = chip_rows(s)
        d_act = nt(g_all[rows, :], wd[...])
        gate_rows = gate[rows, :].astype(F32)
        up_rows = up[rows, :].astype(F32)
        sig = 1.0 / (1.0 + jnp.exp(-gate_rows))
        d_up = (d_act * (gate_rows * sig)).astype(BF16)
        d_gate = (d_act * up_rows * (sig * (1.0 + gate_rows * (1.0 - sig)))).astype(BF16)
        gate[rows, :] = d_gate
        up[rows, :] = d_up
        blocks[s] = (nn(d_gate, wg[...]) + nn(d_up, wu[...])).astype(BF16)
        first_sum.pair(s)
        if s == 1:
            first_sum.far()
            lax.fori_loop(0, 4, down_grad, 0)
            d_sum.start()
    first_sum.near()
    g_gather.sent()
    credit(1)
    first_sum.relay()
    n2_gather.sent()

    def gate_grad(j, carry):
        lanes = ds(j * 512, 512)
        wg[:, lanes] = tn(gate[...], wide[:, lanes]).astype(BF16)
        return carry

    lax.fori_loop(0, 4, gate_grad, 0)
    g_sum.start()

    first_sum.arrive()
    gain_sums[...] = jnp.zeros_like(gain_sums)

    def norm_back(total, values, gain, which):
        scale = lax.rsqrt(jnp.sum(values * values, axis=1, keepdims=True) * (1.0 / D) + EPSILON)
        scaled = total * gain
        inner = jnp.sum(scaled * values, axis=1, keepdims=True) * (1.0 / D)
        part = jnp.sum(total * values * scale, axis=0, keepdims=True)
        gain_sums[pl.ds(which, 1), :] = gain_sums[pl.ds(which, 1), :] + part
        return scale * scaled - values * (scale * scale * scale * inner)

    def residual_back_rows(t, carry):
        rows = ds(t * 16, 16)
        back = norm_back(first_sum.total(t * 16, 16), residual[rows, :], gain_two, 1)
        total = low_rows[rows, :].astype(F32) + back
        d_residual[rows, :] = total
        low_rows[rows, :] = total.astype(BF16)
        return carry

    lax.fori_loop(0, TOK // 16, residual_back_rows, 0)
    credit(2)
    pl.semaphore_wait(free.at[1], 3)
    own_rows = pltpu.make_async_copy(low_rows, token_place(g_all)(here.r, None), gather_local.at[2])
    own_rows.start()
    d_gather.start()
    first_sum.sent()
    layer_sum = row_sum(2)

    def up_grad(j, carry):
        lanes = ds(j * 512, 512)
        wu[:, lanes] = tn(up[...], wide[:, lanes]).astype(BF16)
        return carry

    lax.fori_loop(0, 4, up_grad, 0)
    u_sum.start()
    normed_again = pltpu.make_async_copy(normed_kept, wide, gather_local.at[1])
    normed_again.start()


    def down_block(s):
        blocks[s] = nn(act[chip_rows(s), :], wd[...]).astype(BF16)

    for s in (2, 1):
        down_block(s)
    d_gather.near()
    for s in (3, 0):
        down_block(s)
    pl.semaphore_wait(free.at[2], 3)
    for s in (2, 1, 3, 0):
        layer_sum.pair(s)
    d_gather.far()
    d_sum.middle()
    g_sum.middle()
    layer_sum.far()

    def mix_back(s):
        rows = chip_rows(s)
        d_mixed[rows, :] = nt(g_all[rows, :], wo[...]).astype(BF16)

    own_rows.wait()
    d_gather.got_own()
    mix_back(0)
    d_gather.got_near()
    mix_back(1)
    mix_back(3)
    d_gather.got_far()
    mix_back(2)

    def out_grad(j, carry):
        lanes = ds(j * 512, 512)
        wo[:, lanes] = tn(mixed[...], g_all[:, lanes]).astype(BF16)
        return carry

    lax.fori_loop(0, 4, out_grad, 0)
    layer_sum.near()
    for sums in (dk_low, dk_high, dv_low, dv_high):
        sums[...] = jnp.zeros_like(sums)

    def attend_back(block):
        keys = (block + 1) * 256
        rows, seen = pl.ds(block * 256, 256), pl.ds(0, keys)
        bias = bias_of(block, keys)
        cos_rows, sin_rows = cos[rows, :], sin[rows, :]

        def one_pair(p, carry):
            lanes = ds(p * 128, 128)
            pair = query[rows, lanes]
            grads = d_mixed[rows, lanes]
            product = grads.astype(F32) * mixed[rows, lanes].astype(F32)
            out = jnp.zeros((256, 128), F32)
            for side, (key, value, dk, dv) in enumerate(
                ((k_low, v_low, dk_low, dv_low), (k_high, v_high, dk_high, dv_high))
            ):
                half = (lane < HD) if side == 0 else (lane >= HD)
                inner = jnp.sum(jnp.where(half, product, 0.0), axis=1, keepdims=True)
                total = jnp.sum(
                    jnp.where(lane == 2 * p + side, totals[rows, :], 0.0), axis=1, keepdims=True
                )
                probs = jnp.exp(nt(pair, key[seen, :]) + bias - total)
                d_probs = nt(grads, value[seen, :])
                d_scores = (probs * (d_probs - inner)).astype(BF16)
                out = out + nn(d_scores, key[seen, :])
                dk[seen, :] = dk[seen, :] + tn(d_scores, pair)
                dv[seen, :] = dv[seen, :] + tn(probs.astype(BF16), grads)
            d_projected[rows, lanes] = turn(out * HD**-0.5, cos_rows, -sin_rows).astype(BF16)
            return carry

        lax.fori_loop(0, 2, one_pair, 0)

    attend_back(3)
    u_sum.middle()
    layer_sum.relay()
    o_sum.start()
    attend_back(2)
    attend_back(1)
    attend_back(0)
    d_sum.last()
    g_sum.late()

    def key_rows(t, carry):
        rows = ds(t * 256, 256)
        key = dk_low[rows, :] + pltpu.roll(dk_high[rows, :], HD, 1)
        value = dv_high[rows, :] + pltpu.roll(dv_low[rows, :], HD, 1)
        key = turn(key, cos[rows, :], -sin[rows, :])
        d_projected[rows, pl.ds(256, 128)] = jnp.where(lane < HD, key, value).astype(BF16)
        return carry

    lax.fori_loop(0, 4, key_rows, 0)
    layer_sum.arrive()
    d_gather.sent()

    def layer_rows(t, carry):
        rows = ds(t * 16, 16)
        low_rows[rows, :] = (residual[rows, :] + layer_sum.total(t * 16, 16)).astype(BF16)
        return carry

    lax.fori_loop(0, TOK // 16, layer_rows, 0)
    credit(3)
    layer_sum.sent()
    last_sum = row_sum(3)
    pl.semaphore_wait(free.at[3], 3)
    for s in (2, 1, 3, 0):
        rows = chip_rows(s)
        back = nt(d_projected[rows, pl.ds(0, 256)], wq[...])
        back = back + nn(d_projected[rows, pl.ds(256, 128)], wkv[...])
        blocks[s] = back.astype(BF16)
        last_sum.pair(s)
        if s == 1:
            last_sum.far()
    last_sum.near()
    layer_spread = spread(0, layer_out)
    layer_spread.start()
    normed_again.wait()

    def project_grad(j, carry):
        lanes = ds(j * 512, 512)
        values = wide[:, lanes]
        wq[lanes, :] = tn(values, d_projected[:, pl.ds(0, 256)]).astype(BF16)
        wkv[:, lanes] = tn(d_projected[:, pl.ds(256, 128)], values).astype(BF16)
        return carry

    lax.fori_loop(0, 4, project_grad, 0)
    q_sum.start()
    kv_sum.start()
    u_sum.last()
    g_sum.last()
    last_sum.relay()
    o_sum.middle()
    kv_sum.middle()
    layer_spread.end()
    last_sum.arrive()
    gain_one = gain_row(gains, 0)

    def input_rows(t, carry):
        rows = ds(t * 16, 16)
        values = x_mine[rows, :].astype(F32)
        back = norm_back(last_sum.total(t * 16, 16), values, gain_one, 0)
        low_rows[rows, :] = (d_residual[rows, :] + back).astype(BF16)
        return carry

    lax.fori_loop(0, TOK // 16, input_rows, 0)
    input_spread = spread(1, input_out)
    input_spread.start()
    gain_sum.start()
    kv_sum.last()
    o_sum.last()
    q_sum.middle()
    gain_sum.middle()
    gain_sum.last()
    kv_sum.end()
    kv_total[...] = kv_sum.own[...].astype(F32) + kv_far[...].astype(F32)
    kv_swaps = []
    for index in range(2):
        theirs = ds(index * HD + (1 - here.k) * (HD // 2), HD // 2)
        land = kv_land.at[pl.ds(index * (HD // 2), HD // 2)]
        kv_swaps.append(
            remote(
                kv_total.at[theirs], land, last_send.at[7 + index], last_recv.at[7 + index], here.partner
            )
        )
        kv_swaps[index].start()
    gain_sum.end()
    gain_rows[here.r] = gain_sum.own[...] + gain_far[...]
    row_copies = [
        remote(
            gain_rows.at[here.r], gain_rows.at[here.r], last_send.at[k], last_recv.at[k], row_peers[k]
        )
        for k in range(7)
    ]
    for copy in row_copies:
        copy.start()
    q_sum.last()
    keep(d_sum.own, gd_own)
    keep(g_sum.own, gg_own)
    keep(u_sum.own, gu_own)
    keep(o_sum.own, go_own)
    keep(q_sum.own, gq_own)
    for index in range(2):
        kv_swaps[index].wait()
        mine = kv_total[ds(index * HD + here.k * (HD // 2), HD // 2), :]
        there = pl.ds(index * (HD // 2), HD // 2)
        kv_final[there, :] = mine + kv_land[there, :]
    keep(kv_final, kv_out)
    for sums in (d_sum, g_sum, u_sum, o_sum, q_sum):
        sums.end()
    for copy in row_copies:
        copy.wait()
    total = gain_rows[0]
    for r in range(1, 8):
        total = total + gain_rows[r]
    gain_rows[0] = total
    keep(gain_rows.at[0], gains_out)
    input_spread.end()
    last_sum.sent()
    x_collect.sent()
    g_collect.sent()
    for copy in kept:
        if copy is not normed_copy:
            copy.wait()


def layer_call(*args):
    ff = args[6].shape[0]
    any_space = pl.BlockSpec(memory_space=pl.ANY)
    vmem_space = pl.BlockSpec(memory_space=pltpu.VMEM)
    dma = pltpu.SemaphoreType.DMA

    def low(*shape):
        return jax.ShapeDtypeStruct(shape, BF16)

    outs = (
        low(LEN, FEAT),
        low(LEN, FEAT),
        low(ff, FEAT),
        low(ff, FEAT),
        low(ff // 2, FEAT),
        low(ff // 2, FEAT),
        low(ff, FEAT),
        low(ff, FEAT),
        low(256, FEAT),
        low(256, FEAT),
        low(FEAT, 256),
        low(FEAT, 256),
        jax.ShapeDtypeStruct((HD, FEAT), F32),
        jax.ShapeDtypeStruct((8, FEAT), F32),
        low(LEN, D),
        low(8, TOK, FEAT),
    )

    def vmem(*shape, dtype=BF16):
        return pltpu.VMEM(shape, dtype)

    scratch = [
        vmem(8, TOK, FEAT),
        vmem(TOK, D),
        vmem(TOK, D),
        vmem(LEN, D),
        vmem(LEN, D),
        vmem(LEN, ff),
        vmem(LEN, ff),
        vmem(LEN, ff),
        vmem(ff, D),
        vmem(ff, D),
        vmem(ff, D),
        vmem(ff, D),
        vmem(256, D),
        vmem(D, 256),
        vmem(128, D),
        vmem(128, FEAT),
        vmem(128, FEAT),
        vmem(128, FEAT, dtype=F32),
        vmem(HD, FEAT, dtype=F32),
        vmem(HD, FEAT, dtype=F32),
        vmem(64, 256, dtype=F32),
        vmem(LEN, 128, dtype=F32),
        vmem(LEN, 128, dtype=F32),
        vmem(LEN, 128, dtype=F32),
        vmem(LEN, 256),
        vmem(LEN, 128),
        vmem(LEN, 128),
        vmem(LEN, 128),
        vmem(LEN, 128),
        vmem(LEN, 256),
        vmem(LEN, 128, dtype=F32),
        vmem(LEN, 256),
        vmem(LEN, 384),
        vmem(LEN, 128, dtype=F32),
        vmem(LEN, 128, dtype=F32),
        vmem(LEN, 128, dtype=F32),
        vmem(LEN, 128, dtype=F32),
        vmem(4, 256, D),
        vmem(4, TOK, D),
        vmem(2, TOK // 2, D),
        vmem(2, TOK, D),
        vmem(TOK, D, dtype=F32),
        vmem(TOK, D, dtype=F32),
        vmem(8, D, dtype=F32),
        vmem(3, 8, 2 * FEAT, dtype=F32),
        vmem(8, FEAT, dtype=F32),
        vmem(8, FEAT, dtype=F32),
        vmem(8, 8, FEAT, dtype=F32),
        vmem(ff, FEAT),
        vmem(3, ff, 2 * FEAT),
        vmem(8, ff // 2, FEAT),
        vmem(3, 2, ff // 2, FEAT),
        vmem(ff // 2, FEAT),
        vmem(4, ff, FEAT),
        vmem(3, ff, FEAT),
        vmem(4, 256, FEAT),
        vmem(3, 256, FEAT),
        vmem(4, FEAT, 256),
        vmem(3, FEAT, 256),
        vmem(128, FEAT),
        vmem(3, 128, 2 * FEAT),
        dma((2, 16)),
        dma((2, 16)),
        dma((2, 2)),
        dma((4, RowGather.SEMS)),
        dma((4, RowGather.SEMS)),
        dma((5,)),
        dma((7, SplitGather.SEMS)),
        dma((7, SplitGather.SEMS)),
        dma((7,)),
        dma((4, RowSum.SEMS)),
        dma((4, RowSum.SEMS)),
        dma((7, SplitSum.SEMS)),
        dma((7, SplitSum.SEMS)),
        dma((2, 8)),
        dma((2, 8)),
        dma((2,)),
        dma((11,)),
        dma((11,)),
        dma((8,)),
        pltpu.SemaphoreType.REGULAR((4,)),
    ]
    return pl.pallas_call(
        layer_kernel,
        out_shape=outs,
        in_specs=[any_space] * 10 + [vmem_space],
        out_specs=tuple(any_space for _ in outs),
        scratch_shapes=scratch,
        compiler_params=pltpu.CompilerParams(
            collective_id=0, has_side_effects=True, vmem_limit_bytes=VMEM_BYTES
        ),
        cost_estimate=pl.CostEstimate(flops=36 * 10**9, bytes_accessed=60 * 10**6, transcendentals=0),
        name="decoder_layer",
    )(*args)


def body(
    hidden_in,
    segment_ids,
    attn_gain,
    w_query,
    w_key,
    w_value,
    w_out,
    mlp_gain,
    w_gate,
    w_up,
    w_down,
    grad_output,
):
    row = lax.broadcasted_iota(jnp.int32, (8, attn_gain.shape[0]), 0)
    gains = jnp.where(row < 4, attn_gain[None], mlp_gain[None])
    (
        layer_output,
        grad_input,
        gd_own,
        gd_far,
        gg_own,
        gg_far,
        gu_own,
        gu_far,
        go_own,
        go_far,
        gq_own,
        gq_far,
        grad_kv,
        d_gains,
        _,
        _,
    ) = layer_call(
        hidden_in,
        grad_output,
        w_query,
        w_key.T,
        w_value.T,
        w_out,
        w_gate.T,
        w_up.T,
        w_down,
        gains,
        segment_ids,
    )

    def both(own, far):
        return own.astype(F32) + far.astype(F32)

    second = (lax.axis_index("dp") + lax.axis_index("col")) % 2 == 1
    grad_gate = jnp.concatenate(
        [jnp.where(second, gg_far, gg_own), jnp.where(second, gg_own, gg_far)], axis=0
    )
    kv_width = w_key.shape[1]
    return (
        layer_output,
        grad_input.astype(F32),
        d_gains[0],
        both(gq_own, gq_far),
        grad_kv[:kv_width].T,
        grad_kv[kv_width:].T,
        both(go_own, go_far),
        d_gains[1],
        grad_gate.astype(F32).T,
        both(gu_own, gu_far).T,
        both(gd_own, gd_far),
    )


def solution(mesh):
    return jax.shard_map(
        body,
        mesh=mesh,
        in_specs=(
            P(("dp", "row"), "col"),
            P(("dp", "col"), None),
            P("col"),
            P("col", "row"),
            P("col", "row"),
            P("col", "row"),
            P("row", "col"),
            P("col"),
            P("col", "row"),
            P("col", "row"),
            P("row", "col"),
            P(("dp", "row"), "col"),
        ),
        out_specs=(
            P(("dp", "row"), "col"),
            P(("dp", "row"), "col"),
            P("col"),
            P("col", "row"),
            P("col", "row"),
            P("col", "row"),
            P("row", "col"),
            P("col"),
            P("col", "row"),
            P("col", "row"),
            P("row", "col"),
        ),
        check_vma=False,
    )
```

```python
import functools
import math

import jax
import jax.numpy as jnp
from jax import lax
from jax.experimental import pallas as pl
from jax.experimental.pallas import tpu as pltpu
from jax.sharding import PartitionSpec as P

D = 2048
HD = 64
LEN = 1024
ROWS = 8
CHIPS = 4
TOK = LEN // ROWS
FEAT = D // 8
EPSILON = 1e-05
FLOOR_SCORE = -1e30
BF16 = jnp.bfloat16
F32 = jnp.float32
MESH = pl.DeviceIdType.MESH
VMEM_BYTES = 62 * 2**20


def remote(src, dst, send, recv, device):
    return pltpu.make_async_remote_copy(
        src_ref=src, dst_ref=dst, send_sem=send, recv_sem=recv, device_id=device, device_id_type=MESH
    )


def meet(peers):
    barrier = pltpu.get_barrier_semaphore()
    for peer in peers:
        pl.semaphore_signal(barrier, inc=1, device_id=peer, device_id_type=MESH)
    pl.semaphore_wait(barrier, len(peers))


def ds(start, size):
    return pl.ds(pl.multiple_of(start, size), size)


class Place:
    def __init__(self):
        self.d = lax.axis_index("dp")
        self.r = lax.axis_index("row")
        self.c = lax.axis_index("col")
        self.y, self.k = self.r // 2, lax.rem(self.r, 2)
        self.x, self.h = self.c // 2, lax.rem(self.c, 2)
        self.partner = {"row": self.y * 2 + 1 - self.k}
        self.up = {"row": self.row_of(1)}
        self.down = {"row": self.row_of(3)}
        self.other = {"dp": 1 - self.d, "col": self.x * 2 + 1 - self.h}
        self.twin = {"dp": 1 - self.d}
        self.half = lax.rem(self.d + self.h, 2)
        self.x_peers = [{"col": self.col_of(s)} for s in (1, 3, 2)]

    def row_of(self, step):
        return lax.rem(self.y + step, CHIPS) * 2 + self.k

    def col_of(self, step):
        return lax.rem(self.x + step, 4) * 2 + self.h

    def col_from(self, step):
        return lax.rem(self.x + 4 - step, 4) * 2 + self.h


class RowGather:
    SEMS = 13

    def __init__(self, here, place, shard, send, recv):
        self.here, self.place = here, place
        y, k = here.y, here.k
        self.low, self.high, self.far_row = here.row_of(3), here.row_of(1), here.row_of(2)
        self.ups = [
            remote(shard(a), place(here.r, a), send.at[a], recv.at[a], here.up) for a in (0, 1)
        ]
        self.downs = [
            remote(shard(a), place(here.r, a), send.at[2 + a], recv.at[2 + a], here.down)
            for a in (0, 1)
        ]
        self.fars = [
            self.hand_on(self.low, 0, send.at[4], recv.at[4], here.up),
            self.hand_on(self.high, 1, send.at[5], recv.at[5], here.down),
        ]
        self.passes = {}
        for index, (row, a) in enumerate(
            [(self.low, 0), (self.low, 1), (self.high, 0), (self.high, 1), (self.far_row, 0), (self.far_row, 1)]
        ):
            self.passes[index] = self.hand_on(
                row, a, send.at[6 + index], recv.at[6 + index], here.partner
            )
        self.own = [
            remote(shard(None), place(here.r, None), send.at[12], recv.at[12], here.partner)
        ]

    def hand_on(self, row, a, send, recv, device):
        return remote(self.place(row, a), self.place(row, a), send, recv, device)

    def start(self):
        for a, b in ((0, 1), (1, 0)):
            self.ups[a].start()
            self.downs[b].start()
        self.own[0].start()

    def near(self):
        for a, b in ((0, 1), (1, 0)):
            self.ups[a].wait_recv()
            if a == 0:
                self.fars[0].start()
            self.passes[a].start()
            self.downs[b].wait_recv()
            if b == 1:
                self.fars[1].start()
            self.passes[2 + b].start()

    def far(self):
        for a in (0, 1):
            self.fars[a].wait_recv()
            self.passes[4 + a].start()

    def got_own(self):
        self.own[0].wait_recv()

    def got_near(self):
        for index in range(4):
            self.passes[index].wait_recv()

    def got_far(self):
        for index in (4, 5):
            self.passes[index].wait_recv()

    def sent(self):
        for copy in self.ups + self.downs + self.fars + self.own + list(self.passes.values()):
            copy.wait_send()


class ColGather:
    SEMS = 7

    def __init__(self, here, shard, place, send, recv, local, across_first):
        self.here, self.place, self.across_first = here, place, across_first
        self.local = pltpu.make_async_copy(shard, place(here.c), local)
        self.lines = [
            remote(shard, place(here.c), send.at[i], recv.at[i], here.x_peers[i]) for i in range(3)
        ]
        self.across = [remote(shard, place(here.c), send.at[3], recv.at[3], here.other)]
        there = here.x * 2 + 1 - here.h
        if across_first:
            self.seconds = [
                remote(place(there), place(there), send.at[4 + i], recv.at[4 + i], here.x_peers[i])
                for i in range(3)
            ]
        else:
            self.seconds = []
            for i, step in enumerate((1, 3, 2)):
                source = here.col_from(step)
                self.seconds.append(
                    remote(place(source), place(source), send.at[4 + i], recv.at[4 + i], here.other)
                )

    def start(self):
        self.start_across()
        self.start_lines()

    def start_across(self):
        self.local.start()
        self.across[0].start()

    def start_lines(self):
        for copy in self.lines:
            copy.start()

    def middle(self):
        if self.across_first:
            self.across[0].wait_recv()
            for copy in self.seconds:
                copy.start()
        else:
            for copy, second in zip(self.lines, self.seconds):
                copy.wait_recv()
                second.start()

    def end(self):
        self.local.wait()
        if self.across_first:
            for copy in self.lines:
                copy.wait_recv()
        else:
            self.across[0].wait_recv()
        for copy in self.seconds:
            copy.wait_recv()
        for copy in self.lines + self.across + self.seconds:
            copy.wait_send()


class SplitGather:
    SEMS = 14

    def __init__(self, here, shard, place, send, recv, local):
        self.here, self.place = here, place
        half = here.half
        self.local = pltpu.make_async_copy(shard(None), place(here.c, None), local)

        def hand_on(c, index, device):
            return remote(place(c, half), place(c, half), send.at[index], recv.at[index], device)

        own = place(here.c, half)
        self.across = remote(shard(half), own, send.at[0], recv.at[0], here.other)
        self.lines = [
            remote(shard(half), own, send.at[1 + i], recv.at[1 + i], here.x_peers[i]) for i in range(3)
        ]
        there = here.x * 2 + 1 - here.h
        self.seconds = [hand_on(there, 4 + i, here.x_peers[i]) for i in range(3)]
        sources = [here.col_from(step) for step in (1, 3, 2)]
        others = [source + 1 - 2 * here.h for source in sources]
        self.swaps = [
            hand_on(c, 7 + i, here.twin) for i, c in enumerate([there] + sources + others)
        ]

    def start_across(self):
        self.local.start()
        self.across.start()

    def start_lines(self):
        for copy in self.lines:
            copy.start()

    def middle(self):
        self.across.wait_recv()
        for copy in self.seconds:
            copy.start()
        self.swaps[0].start()

    def late(self, which):
        copies = self.seconds if which else self.lines
        for copy, swap in zip(copies, self.swaps[1 + 3 * which :]):
            copy.wait_recv()
            swap.start()

    def end(self):
        self.local.wait()
        for swap in self.swaps:
            swap.wait_recv()
        for copy in [self.across] + self.lines + self.seconds + self.swaps:
            copy.wait_send()


class RowSum:
    SEMS = 10

    def __init__(self, here, blocks, paired, relayed, landed, send, recv):
        self.here, self.blocks, self.paired = here, blocks, paired
        self.relayed, self.landed = relayed, landed
        k, half = here.k, TOK // 2
        self.mine, self.half = k * TOK, half
        self.pairs = [
            remote(
                blocks.at[s, ds((1 - k) * TOK, TOK)], paired.at[s], send.at[s], recv.at[s], here.partner
            )
            for s in range(4)
        ]
        self.fars = [
            remote(self.part(2, 0), relayed.at[0], send.at[4], recv.at[4], here.up),
            remote(self.part(2, 1), relayed.at[1], send.at[5], recv.at[5], here.down),
        ]
        self.nears = {}
        for index, (s, a, device) in enumerate(
            [(1, 1, here.up), (3, 0, here.down), (1, 0, here.up), (3, 1, here.down)]
        ):
            slot = 0 if s == 1 else 1
            self.nears[s, a] = remote(
                self.part(s, a),
                landed.at[slot, pl.ds(a * half, half)],
                send.at[6 + index],
                recv.at[6 + index],
                device,
            )

    def part(self, s, a):
        return self.blocks.at[s, ds(self.mine + a * self.half, self.half)]

    def add(self, s, a, other):
        part = self.part(s, a)
        part[...] = (part[...].astype(F32) + other[...].astype(F32)).astype(BF16)

    def pair(self, s):
        self.pairs[s].start()

    def join(self, s):
        self.pairs[s].wait_recv()
        for a in (0, 1):
            self.add(s, a, self.paired.at[s, pl.ds(a * self.half, self.half)])

    def far(self):
        self.join(2)
        self.fars[0].start()
        self.fars[1].start()

    def near(self):
        self.join(1)
        self.nears[1, 1].start()
        self.join(3)
        self.nears[3, 0].start()

    def relay(self):
        self.fars[0].wait_recv()
        self.add(1, 0, self.relayed.at[0])
        self.nears[1, 0].start()
        self.fars[1].wait_recv()
        self.add(3, 1, self.relayed.at[1])
        self.nears[3, 1].start()

    def arrive(self):
        self.pairs[0].wait_recv()
        for copy in self.nears.values():
            copy.wait_recv()

    def total(self, start, rows):
        own = self.blocks[0, pl.ds(pl.multiple_of(self.mine + start, rows), rows)].astype(F32)
        here = pl.ds(pl.multiple_of(start, rows), rows)
        return (
            own
            + self.paired[0, here].astype(F32)
            + self.landed[0, here].astype(F32)
            + self.landed[1, here].astype(F32)
        )

    def sent(self):
        for copy in self.pairs + self.fars + list(self.nears.values()):
            copy.wait_send()


def add_rows(rows, target, others):
    kind = target.dtype

    def step(t, carry):
        at = ds(t * rows, rows)
        total = target[at, :].astype(F32)
        for other in others:
            total = total + other[at, :].astype(F32)
        target[at, :] = total.astype(kind)
        return carry

    lax.fori_loop(0, target.shape[0] // rows, step, 0)


class WeightSum:
    SEMS = 8

    def __init__(self, here, part, wide_part, rows, z_land, x_land, far_part, send, recv, across_first):
        self.here, self.part, self.across_first, self.rows = here, part, across_first, rows
        self.z_land, self.x_land = z_land, x_land
        self.own = part(here.c)
        steps = (1, 3, 2)
        if across_first:
            self.mine = [part(x * 2 + here.h) for x in range(4)]
            self.across = [
                remote(part(x * 2 + 1 - here.h), z_land.at[x], send.at[x], recv.at[x], here.other)
                for x in range(4)
            ]
            self.lines = [
                remote(
                    part(here.col_of(step)), x_land.at[i], send.at[4 + i], recv.at[4 + i], here.x_peers[i]
                )
                for i, step in enumerate(steps)
            ]
        else:
            self.wide = wide_part(here.x)
            self.across = [
                remote(
                    part(here.x * 2 + 1 - here.h), z_land, send.at[3], recv.at[3], here.other
                )
            ]
            self.lines = [
                remote(
                    wide_part(lax.rem(here.x + step, 4)),
                    x_land.at[i],
                    send.at[i],
                    recv.at[i],
                    here.x_peers[i],
                )
                for i, step in enumerate(steps)
            ]
        self.swap = remote(self.own, far_part, send.at[7], recv.at[7], here.twin)

    def add(self, target, others):
        add_rows(self.rows, target, others)

    def start(self):
        for copy in self.across if self.across_first else self.lines:
            copy.start()

    def middle(self):
        if self.across_first:
            for x in range(4):
                self.across[x].wait_recv()
                self.add(self.mine[x], [self.z_land.at[x]])
            for copy in self.lines:
                copy.start()
        else:
            for copy in self.lines:
                copy.wait_recv()
            self.add(self.wide, [self.x_land.at[i] for i in range(3)])
            self.across[0].start()

    def last(self):
        if self.across_first:
            for copy in self.lines:
                copy.wait_recv()
            self.add(self.own, [self.x_land.at[i] for i in range(3)])
        else:
            self.across[0].wait_recv()
            self.add(self.own, [self.z_land])
        self.swap.start()

    def end(self):
        self.swap.wait()
        for copy in self.across + self.lines:
            copy.wait_send()


class SplitSum:
    SEMS = 16

    def __init__(self, here, part, rows, twin_land, x_land, z_land, far_part, send, recv):
        self.here, self.rows = here, rows
        self.twin_land, self.x_land, self.z_land = twin_land, x_land, z_land
        half, x, h = here.half, here.x, here.h
        self.mine = [part(c, half) for c in range(8)]
        self.twins = [
            remote(part(c, 1 - half), twin_land.at[c], send.at[c], recv.at[c], here.twin)
            for c in range(8)
        ]
        self.lines = []
        for i, step in enumerate((1, 3, 2)):
            target = lax.rem(x + step, 4) * 2
            for side in range(2):
                index = 8 + 2 * i + side
                self.lines.append(
                    remote(
                        part(target + side, half),
                        x_land.at[i, side],
                        send.at[index],
                        recv.at[index],
                        here.x_peers[i],
                    )
                )
        self.sides = [part(x * 2 + side, half) for side in range(2)]
        self.across = remote(part(x * 2 + 1 - h, half), z_land, send.at[14], recv.at[14], here.other)
        self.own = part(here.c, half)
        self.swap = remote(self.own, far_part, send.at[15], recv.at[15], here.twin)

    def add(self, target, others):
        add_rows(self.rows, target, others)

    def start(self):
        for copy in self.twins:
            copy.start()

    def middle(self):
        for c in range(8):
            self.twins[c].wait_recv()
            self.add(self.mine[c], [self.twin_land.at[c]])
        for copy in self.lines:
            copy.start()

    def late(self):
        for copy in self.lines:
            copy.wait_recv()
        for side in range(2):
            self.add(self.sides[side], [self.x_land.at[i, side] for i in range(3)])
        self.across.start()

    def last(self):
        self.across.wait_recv()
        self.add(self.own, [self.z_land])
        self.swap.start()

    def end(self):
        self.swap.wait()
        for copy in self.twins + self.lines + [self.across]:
            copy.wait_send()


class Spread:
    def __init__(self, here, source, target, send, recv, local):
        self.here = here
        self.same = here.r == here.c
        self.copies = []
        place = target.at[ds(here.r * TOK, TOK)]
        for j in range(8):
            shard = source.at[:, pl.ds(j * FEAT, FEAT)]
            self.copies.append(
                (
                    remote(shard, place, send.at[j], recv.at[here.r], {"row": here.c, "col": j}),
                    pltpu.make_async_copy(shard, place, local),
                )
            )
        self.arrivals = [
            remote(
                source.at[:, pl.ds(0, FEAT)],
                target.at[pl.ds(i * TOK, TOK)],
                send.at[i],
                recv.at[i],
                {"row": here.c, "col": i},
            )
            for i in range(8)
        ]

    def each(self, index, other, own):
        itself = self.same & (self.here.r == index)
        pl.when(itself)(own)
        pl.when(jnp.logical_not(itself))(other)

    def start(self):
        for j, (copy, local) in enumerate(self.copies):
            self.each(j, copy.start, local.start)

    def end(self):
        for j, (copy, local) in enumerate(self.copies):
            self.each(j, copy.wait_send, local.wait)
        for i, copy in enumerate(self.arrivals):
            self.each(i, copy.wait_recv, lambda: None)


class Collect:
    def __init__(self, here, source, middle, target, send, recv, local):
        self.here = here
        r, c = here.r, here.c
        self.local = pltpu.make_async_copy(source.at[ds(r * TOK, TOK)], middle.at[r], local.at[0])
        self.firsts = []
        self.seconds = []
        lanes = target.at[:, ds(c * FEAT, FEAT)]
        for k in range(1, 8):
            i = lax.rem(r + k, 8)
            self.firsts.append(
                remote(
                    source.at[ds(i * TOK, TOK)], middle.at[r], send.at[k], recv.at[k], {"row": i}
                )
            )
        for k in range(8):
            a = lax.rem(r + 8 - k, 8)
            self.seconds.append(
                (
                    a == c,
                    remote(middle.at[a], lanes, send.at[8 + k], recv.at[8 + c], {"col": a}),
                    pltpu.make_async_copy(middle.at[a], lanes, local.at[1]),
                )
            )
        self.arrivals = [
            (
                c == j,
                remote(
                    middle.at[0],
                    target.at[:, pl.ds(j * FEAT, FEAT)],
                    send.at[8 + j],
                    recv.at[8 + j],
                    {"col": j},
                ),
            )
            for j in range(8)
        ]

    def start(self):
        self.local.start()
        for copy in self.firsts:
            copy.start()

    def turn(self):
        self.local.wait()
        for k, (itself, copy, local) in enumerate(self.seconds):
            if k > 0:
                self.firsts[k - 1].wait_recv()
            pl.when(itself)(local.start)
            pl.when(jnp.logical_not(itself))(copy.start)

    def arrive(self):
        for itself, copy, local in self.seconds:
            pl.when(itself)(local.wait)
        for itself, copy in self.arrivals:
            pl.when(jnp.logical_not(itself))(copy.wait_recv)

    def sent(self):
        for copy in self.firsts:
            copy.wait_send()
        for itself, copy, local in self.seconds:
            pl.when(jnp.logical_not(itself))(copy.wait_send)


def nn(a, b):
    return jnp.dot(a, b, preferred_element_type=F32)


def nt(a, b):
    return lax.dot_general(a, b, (((1,), (1,)), ((), ())), preferred_element_type=F32)


def tn(a, b):
    return lax.dot_general(a, b, (((0,), (0,)), ((), ())), preferred_element_type=F32)


def swap_halves(values):
    width = values.shape[-1]
    lane = lax.broadcasted_iota(jnp.int32, values.shape, 1)
    return jnp.where(
        lax.rem(lane, HD) < HD // 2, pltpu.roll(values, width - HD // 2, 1), pltpu.roll(values, HD // 2, 1)
    )


def turn(values, cos, sin):
    return values * cos + swap_halves(values) * sin


def gain_row(gains, which):
    return jnp.concatenate([gains[pl.ds(8 * j + which, 1), :] for j in range(8)], axis=1)


def layer_kernel(
    x_in,
    g_in,
    wq_in,
    wk_in,
    wv_in,
    wo_in,
    wg_in,
    wu_in,
    wd_in,
    attn_in,
    mlp_in,
    seg_in,
    layer_out,
    input_out,
    gd_own,
    gd_far,
    gg_own,
    gg_far,
    gu_own,
    gu_far,
    go_own,
    go_far,
    gq_own,
    gq_far,
    kv_out,
    gains_out,
    normed_kept,
    g_middle,
    x_middle,
    x_mine,
    low_rows,
    wide,
    g_all,
    act,
    gate,
    up,
    wd,
    gd,
    wg,
    wu,
    wo,
    wq,
    wkv,
    kv_shard,
    kv_far,
    kv_total,
    kv_land,
    kv_final,
    gain_shard,
    gains,
    cos,
    sin,
    seg_col,
    query,
    k_low,
    k_high,
    v_low,
    v_high,
    mixed,
    totals,
    d_mixed,
    d_projected,
    dk_low,
    dk_high,
    dv_low,
    dv_high,
    blocks,
    paired,
    relayed,
    landed,
    residual,
    d_residual,
    gain_sums,
    gain_cols,
    gain_far,
    gain_rows,
    gd_z,
    gd_x,
    gg_twin,
    gg_x,
    gg_z,
    gu_z,
    gu_x,
    go_z,
    go_x,
    gq_z,
    gq_x,
    kv_z,
    kv_x,
    collect_send,
    collect_recv,
    collect_local,
    gather_send,
    gather_recv,
    gather_local,
    w_send,
    w_recv,
    w_local,
    rows_send,
    rows_recv,
    sum_send,
    sum_recv,
    spread_send,
    spread_recv,
    spread_local,
    last_send,
    last_recv,
    gain_send,
    gain_recv,
    keep_sem,
    free,
):
    here = Place()
    same = here.r == here.c
    barrier = pltpu.get_barrier_semaphore()
    row_peers = [{"row": lax.rem(here.r + k, ROWS)} for k in range(1, ROWS)]
    col_peers = [{"col": lax.rem(here.c + k, 8)} for k in range(1, 8)]
    peers = row_peers + col_peers + [here.other, here.twin]
    for peer in peers:
        pl.semaphore_signal(barrier, inc=1, device_id=peer, device_id_type=MESH)
    for i in range(8):

        @pl.when(jnp.logical_not(same & (here.r == i)))
        def _():
            pl.semaphore_signal(
                barrier, inc=1, device_id={"row": i, "col": here.r}, device_id_type=MESH
            )

    pl.semaphore_wait(barrier, len(peers) + 8 - same.astype(jnp.int32))

    def token_place(ref):
        def place(row, a):
            if a is None:
                return ref.at[ds(row * TOK, TOK)]
            return ref.at[ds(row * TOK + a * (TOK // 2), TOK // 2)]

        return place

    def own_part(ref):
        place = token_place(ref)
        return lambda a: place(here.r, a)

    def low_part(a):
        return low_rows if a is None else low_rows.at[pl.ds(a * (TOK // 2), TOK // 2)]

    def row_gather(index, ref, shard):
        return RowGather(here, token_place(ref), shard, gather_send.at[index], gather_recv.at[index])

    def row_sum(index):
        return RowSum(here, blocks, paired, relayed, landed, rows_send.at[index], rows_recv.at[index])

    def collect(index, source, middle, target):
        return Collect(
            here,
            source,
            middle,
            target,
            collect_send.at[index],
            collect_recv.at[index],
            collect_local.at[index],
        )

    def spread(index, target):
        return Spread(
            here,
            low_rows,
            target,
            spread_send.at[index],
            spread_recv.at[index],
            spread_local.at[index],
        )

    def col_gather(index, shard, place, across_first):
        return ColGather(
            here, shard, place, w_send.at[index], w_recv.at[index], w_local.at[index], across_first
        )

    def split_gather(index, shard, ref):
        half = ref.shape[0] // 2

        def place(c, a):
            lanes = ds(c * FEAT, FEAT)
            return ref.at[:, lanes] if a is None else ref.at[ds(a * half, half), lanes]

        def part(a):
            return shard if a is None else shard.at[ds(a * half, half)]

        return SplitGather(
            here, part, place, w_send.at[index], w_recv.at[index], w_local.at[index]
        )

    def weight_sum(index, parts, rows, z_land, x_land, far_part, across_first):
        return WeightSum(
            here,
            parts[0],
            parts[1],
            rows,
            z_land,
            x_land,
            far_part,
            sum_send.at[index],
            sum_recv.at[index],
            across_first,
        )

    def rows_of(ref):
        return lambda c: ref.at[ds(c * FEAT, FEAT)], lambda x: ref.at[ds(x * 2 * FEAT, 2 * FEAT)]

    def lanes_of(ref):
        return (
            lambda c: ref.at[:, ds(c * FEAT, FEAT)],
            lambda x: ref.at[:, ds(x * 2 * FEAT, 2 * FEAT)],
        )

    def credit(index):
        for peer in (here.partner, here.up, here.down):
            pl.semaphore_signal(free.at[index], inc=1, device_id=peer, device_id_type=MESH)

    def chip_rows(s):
        return ds(lax.rem(here.y + s, CHIPS) * 256, 256)

    kept = []

    def keep(src, dst):
        copy = pltpu.make_async_copy(src, dst, keep_sem.at[len(kept)])
        copy.start()
        kept.append(copy)
        return copy

    x_collect = collect(0, x_in, x_middle, x_mine)
    g_collect = collect(1, g_in, g_middle, low_rows)
    n1_gather = row_gather(0, wide, own_part(wide))
    g_gather = row_gather(1, g_all, low_part)
    n2_gather = row_gather(2, wide, own_part(wide))
    d_gather = row_gather(3, g_all, low_part)
    gain_gather = col_gather(0, gain_shard, lambda c: gains.at[ds(c * 8, 8)], True)
    wq_gather = col_gather(1, wq_in, lambda c: wq.at[ds(c * FEAT, FEAT)], False)
    kv_gather = col_gather(2, kv_shard, lambda c: wkv.at[:, ds(c * FEAT, FEAT)], False)
    wo_gather = col_gather(3, wo_in, lambda c: wo.at[:, ds(c * FEAT, FEAT)], False)
    wd_gather = col_gather(4, wd_in, lambda c: wd.at[:, ds(c * FEAT, FEAT)], False)
    wg_gather = split_gather(5, wg_in, wg)
    wu_gather = split_gather(6, wu_in, wu)
    d_sum = weight_sum(0, lanes_of(gd), 32, gd_z, gd_x, gd_far, False)
    u_sum = weight_sum(1, lanes_of(wu), 64, gu_z, gu_x, gu_far, True)
    o_sum = weight_sum(2, lanes_of(wo), 64, go_z, go_x, go_far, True)
    q_sum = weight_sum(3, rows_of(wq), 64, gq_z, gq_x, gq_far, True)
    kv_sum = weight_sum(4, lanes_of(wkv), 32, kv_z, kv_x, kv_far, False)
    g_half = wg.shape[0] // 2
    g_sum = SplitSum(
        here,
        lambda c, a: wg.at[ds(a * g_half, g_half), ds(c * FEAT, FEAT)],
        32,
        gg_twin,
        gg_x,
        gg_z,
        gg_far,
        sum_send.at[5],
        sum_recv.at[5],
    )
    kv_copies = []
    for index, part in enumerate((wk_in, wv_in)):
        rows = ds(index * HD + here.k * (HD // 2), HD // 2)
        local = pltpu.make_async_copy(part, kv_shard.at[rows], gather_local.at[3 + index])
        other = remote(
            part, kv_shard.at[rows], last_send.at[9 + index], last_recv.at[9 + index], here.partner
        )
        kv_copies += [local, other]

    for copy in kv_copies:
        copy.start()
    gain_shard[pl.ds(0, 4), :] = jnp.broadcast_to(attn_in[...], (4, FEAT))
    gain_shard[pl.ds(4, 4), :] = jnp.broadcast_to(mlp_in[...], (4, FEAT))
    gain_gather.start()
    wq_gather.start_across()
    wq_gather.start_lines()
    x_collect.start()
    wu_gather.start_across()
    segments = seg_in[0:1, :]
    places = lax.broadcasted_iota(jnp.int32, (1, LEN), 1)
    for number in range(3):
        count = jnp.sum((segments == number).astype(F32), axis=1, keepdims=True).astype(jnp.int32)
        places = places - jnp.where(segments > number, count, 0)
    tall = jnp.transpose(jnp.broadcast_to(places.astype(F32), (128, LEN)))
    lanes = lax.broadcasted_iota(jnp.int32, (1, 128), 1)
    step = (2 * lax.rem(lanes, HD // 2)).astype(F32)
    angles = tall * jnp.exp(step * (-math.log(10000.0) / HD))
    sign = jnp.where(lax.rem(lanes, HD) < HD // 2, -1.0, 1.0)
    cos[...] = jnp.cos(angles)
    sin[...] = jnp.sin(angles) * sign
    seg_col[...] = jnp.transpose(jnp.broadcast_to(segments.astype(F32), (128, LEN)))
    seg_row = segments.astype(F32)
    for copy in kv_copies:
        copy.wait()
    gain_gather.middle()
    x_collect.turn()
    g_collect.start()
    kv_gather.start_across()
    gain_gather.end()
    gain_one = gain_row(gains, 0)
    x_collect.arrive()
    wq_gather.middle()
    wo_gather.start()
    kv_gather.start_lines()

    def norm_rows(t, carry):
        values = x_mine[ds(t * 16, 16), :].astype(F32)
        scale = lax.rsqrt(jnp.sum(values * values, axis=1, keepdims=True) * (1.0 / D) + EPSILON)
        wide[ds(here.r * TOK + t * 16, 16), :] = (values * scale * gain_one).astype(BF16)
        return carry

    lax.fori_loop(0, TOK // 16, norm_rows, 0)
    n1_gather.start()
    kv_gather.middle()
    g_collect.turn()
    lane = lax.broadcasted_iota(jnp.int32, (256, 128), 1)

    def project(s):
        rows = chip_rows(s)
        values = wide[rows, :]
        projected = nn(values, wq[...])
        cos_rows, sin_rows = cos[rows, :], sin[rows, :]
        for p in range(2):
            pair = turn(projected[:, p * 128 : (p + 1) * 128], cos_rows, sin_rows)
            query[rows, pl.ds(p * 128, 128)] = (pair * HD**-0.5).astype(BF16)
        key_value = nt(values, wkv[...])
        key = jnp.where(lane < HD, turn(key_value, cos_rows, sin_rows), 0.0)
        value = jnp.where(lane < HD, 0.0, key_value)
        k_low[rows, :] = key.astype(BF16)
        k_high[rows, :] = pltpu.roll(key, HD, 1).astype(BF16)
        v_high[rows, :] = value.astype(BF16)
        v_low[rows, :] = pltpu.roll(value, HD, 1).astype(BF16)

    n1_gather.near()
    wu_gather.start_lines()
    wq_gather.end()
    kv_gather.end()
    n1_gather.got_own()
    project(0)
    n1_gather.got_near()
    project(1)
    wu_gather.middle()
    n1_gather.far()
    wg_gather.start_across()
    project(3)
    n1_gather.got_far()
    project(2)
    normed_copy = keep(wide, normed_kept)
    g_collect.arrive()
    own_g = pltpu.make_async_copy(low_rows, token_place(g_all)(here.r, None), gather_local.at[0])
    own_g.start()
    g_gather.start()
    wu_gather.late(0)
    wo_gather.middle()

    def bias_of(block, keys):
        first = block * 256
        row = lax.broadcasted_iota(jnp.int32, (256, keys), 0) + first
        key = lax.broadcasted_iota(jnp.int32, (256, keys), 1)
        alike = seg_col[pl.ds(first, 256), 0:1] == seg_row[:, :keys]
        return jnp.where(alike & (key <= row), 0.0, FLOOR_SCORE)

    def attend(block):
        keys = (block + 1) * 256
        rows, seen = pl.ds(block * 256, 256), pl.ds(0, keys)
        bias = bias_of(block, keys)

        def one_pair(p, sums):
            lanes = ds(p * 128, 128)
            pair = query[rows, lanes]
            out = jnp.zeros((256, 128), F32)
            for side, (key, value) in enumerate(((k_low, v_low), (k_high, v_high))):
                scores = nt(pair, key[seen, :]) + bias
                row_max = jnp.max(scores, axis=1, keepdims=True)
                exps = jnp.exp(scores - row_max)
                row_sum = jnp.sum(exps, axis=1, keepdims=True)
                out = out + nn(exps.astype(BF16), value[seen, :]) * (1.0 / row_sum)
                sums = jnp.where(lane == 2 * p + side, row_max + jnp.log(row_sum), sums)
            mixed[rows, lanes] = out.astype(BF16)
            return sums

        totals[rows, :] = lax.fori_loop(0, 2, one_pair, jnp.zeros((256, 128), F32))

    attend(0)
    wu_gather.late(1)
    attend(1)
    attend(2)
    wg_gather.start_lines()
    attend(3)
    g_gather.near()
    wg_gather.middle()
    wo_gather.end()
    normed_copy.wait()
    n1_gather.sent()
    out_sum = row_sum(0)
    for s in (2, 1, 3, 0):
        blocks[s] = nn(mixed[chip_rows(s), :], wo[...]).astype(BF16)
        out_sum.pair(s)
        if s == 1:
            out_sum.far()
    out_sum.near()
    wg_gather.late(0)
    wd_gather.start()
    wg_gather.late(1)
    out_sum.relay()
    out_sum.arrive()
    gain_two = gain_row(gains, 4)

    def residual_rows(t, carry):
        rows = ds(t * 16, 16)
        values = x_mine[rows, :].astype(F32) + out_sum.total(t * 16, 16)
        residual[rows, :] = values
        scale = lax.rsqrt(jnp.sum(values * values, axis=1, keepdims=True) * (1.0 / D) + EPSILON)
        wide[ds(here.r * TOK + t * 16, 16), :] = (values * scale * gain_two).astype(BF16)
        return carry

    lax.fori_loop(0, TOK // 16, residual_rows, 0)
    n2_gather.start()
    wd_gather.middle()
    credit(0)
    out_sum.sent()
    wg_gather.end()
    wu_gather.end()

    def feed(s):
        rows = chip_rows(s)
        values = wide[rows, :]
        gate_rows = nt(values, wg[...])
        up_rows = nt(values, wu[...])
        gate[rows, :] = gate_rows.astype(BF16)
        up[rows, :] = up_rows.astype(BF16)
        act[rows, :] = (gate_rows * (1.0 / (1.0 + jnp.exp(-gate_rows))) * up_rows).astype(BF16)

    n2_gather.got_own()
    feed(0)
    n2_gather.near()
    n2_gather.got_near()
    feed(1)
    g_gather.far()
    feed(3)
    n2_gather.far()
    n2_gather.got_far()
    feed(2)

    g_gather.got_own()
    g_gather.got_near()
    g_gather.got_far()
    own_g.wait()
    wd_gather.end()
    first_sum = row_sum(1)
    pl.semaphore_wait(free.at[0], 3)

    def down_grad(j, carry):
        lanes = ds(j * 512, 512)
        gd[:, lanes] = tn(act[...], g_all[:, lanes]).astype(BF16)
        return carry

    for s in (2, 1, 3, 0):
        rows = chip_rows(s)
        d_act = nt(g_all[rows, :], wd[...])
        gate_rows = gate[rows, :].astype(F32)
        up_rows = up[rows, :].astype(F32)
        sig = 1.0 / (1.0 + jnp.exp(-gate_rows))
        d_up = (d_act * (gate_rows * sig)).astype(BF16)
        d_gate = (d_act * up_rows * (sig * (1.0 + gate_rows * (1.0 - sig)))).astype(BF16)
        gate[rows, :] = d_gate
        up[rows, :] = d_up
        blocks[s] = (nn(d_gate, wg[...]) + nn(d_up, wu[...])).astype(BF16)
        first_sum.pair(s)
        if s == 1:
            first_sum.far()
    first_sum.near()
    lax.fori_loop(0, 4, down_grad, 0)
    g_gather.sent()
    credit(1)
    first_sum.relay()
    n2_gather.sent()

    def gate_grad(j, carry):
        lanes = ds(j * 512, 512)
        wg[:, lanes] = tn(gate[...], wide[:, lanes]).astype(BF16)
        return carry

    lax.fori_loop(0, 4, gate_grad, 0)
    g_sum.start()
    d_sum.start()

    first_sum.arrive()
    gain_sums[...] = jnp.zeros_like(gain_sums)

    def norm_back(total, values, gain, which):
        scale = lax.rsqrt(jnp.sum(values * values, axis=1, keepdims=True) * (1.0 / D) + EPSILON)
        scaled = total * gain
        inner = jnp.sum(scaled * values, axis=1, keepdims=True) * (1.0 / D)
        part = jnp.sum(total * values * scale, axis=0, keepdims=True)
        gain_sums[pl.ds(which, 1), :] = gain_sums[pl.ds(which, 1), :] + part
        return scale * scaled - values * (scale * scale * scale * inner)

    def residual_back_rows(t, carry):
        rows = ds(t * 16, 16)
        back = norm_back(first_sum.total(t * 16, 16), residual[rows, :], gain_two, 1)
        total = low_rows[rows, :].astype(F32) + back
        d_residual[rows, :] = total
        low_rows[rows, :] = total.astype(BF16)
        return carry

    lax.fori_loop(0, TOK // 16, residual_back_rows, 0)
    credit(2)
    pl.semaphore_wait(free.at[1], 3)
    own_rows = pltpu.make_async_copy(low_rows, token_place(g_all)(here.r, None), gather_local.at[2])
    own_rows.start()
    d_gather.start()
    first_sum.sent()
    layer_sum = row_sum(2)

    def up_grad(j, carry):
        lanes = ds(j * 512, 512)
        wu[:, lanes] = tn(up[...], wide[:, lanes]).astype(BF16)
        return carry

    lax.fori_loop(0, 4, up_grad, 0)
    u_sum.start()
    normed_again = pltpu.make_async_copy(normed_kept, wide, gather_local.at[1])
    normed_again.start()


    def down_block(s):
        blocks[s] = nn(act[chip_rows(s), :], wd[...]).astype(BF16)

    for s in (2, 1):
        down_block(s)
    d_gather.near()
    for s in (3, 0):
        down_block(s)
    pl.semaphore_wait(free.at[2], 3)
    for s in (2, 1, 3, 0):
        layer_sum.pair(s)
    d_gather.far()
    layer_sum.far()
    g_sum.middle()
    d_sum.middle()

    def mix_back(s):
        rows = chip_rows(s)
        d_mixed[rows, :] = nt(g_all[rows, :], wo[...]).astype(BF16)

    own_rows.wait()
    d_gather.got_own()
    mix_back(0)
    d_gather.got_near()
    mix_back(1)
    mix_back(3)
    d_gather.got_far()
    mix_back(2)

    def out_grad(j, carry):
        lanes = ds(j * 512, 512)
        wo[:, lanes] = tn(mixed[...], g_all[:, lanes]).astype(BF16)
        return carry

    lax.fori_loop(0, 4, out_grad, 0)
    layer_sum.near()
    for sums in (dk_low, dk_high, dv_low, dv_high):
        sums[...] = jnp.zeros_like(sums)

    def attend_back(block):
        keys = (block + 1) * 256
        rows, seen = pl.ds(block * 256, 256), pl.ds(0, keys)
        bias = bias_of(block, keys)
        cos_rows, sin_rows = cos[rows, :], sin[rows, :]

        def one_pair(p, carry):
            lanes = ds(p * 128, 128)
            pair = query[rows, lanes]
            grads = d_mixed[rows, lanes]
            product = grads.astype(F32) * mixed[rows, lanes].astype(F32)
            out = jnp.zeros((256, 128), F32)
            for side, (key, value, dk, dv) in enumerate(
                ((k_low, v_low, dk_low, dv_low), (k_high, v_high, dk_high, dv_high))
            ):
                half = (lane < HD) if side == 0 else (lane >= HD)
                inner = jnp.sum(jnp.where(half, product, 0.0), axis=1, keepdims=True)
                total = jnp.sum(
                    jnp.where(lane == 2 * p + side, totals[rows, :], 0.0), axis=1, keepdims=True
                )
                probs = jnp.exp(nt(pair, key[seen, :]) + bias - total)
                d_probs = nt(grads, value[seen, :])
                d_scores = (probs * (d_probs - inner)).astype(BF16)
                out = out + nn(d_scores, key[seen, :])
                dk[seen, :] = dk[seen, :] + tn(d_scores, pair)
                dv[seen, :] = dv[seen, :] + tn(probs.astype(BF16), grads)
            d_projected[rows, lanes] = turn(out * HD**-0.5, cos_rows, -sin_rows).astype(BF16)
            return carry

        lax.fori_loop(0, 2, one_pair, 0)

    attend_back(3)
    layer_sum.relay()
    attend_back(2)
    u_sum.middle()
    o_sum.start()
    attend_back(1)
    attend_back(0)
    d_sum.last()

    def key_rows(t, carry):
        rows = ds(t * 256, 256)
        key = dk_low[rows, :] + pltpu.roll(dk_high[rows, :], HD, 1)
        value = dv_high[rows, :] + pltpu.roll(dv_low[rows, :], HD, 1)
        key = turn(key, cos[rows, :], -sin[rows, :])
        d_projected[rows, pl.ds(256, 128)] = jnp.where(lane < HD, key, value).astype(BF16)
        return carry

    lax.fori_loop(0, 4, key_rows, 0)
    layer_sum.arrive()
    d_gather.sent()

    def layer_rows(t, carry):
        rows = ds(t * 16, 16)
        low_rows[rows, :] = (residual[rows, :] + layer_sum.total(t * 16, 16)).astype(BF16)
        return carry

    lax.fori_loop(0, TOK // 16, layer_rows, 0)
    g_sum.late()
    credit(3)
    layer_sum.sent()
    last_sum = row_sum(3)
    pl.semaphore_wait(free.at[3], 3)
    for s in (2, 1, 3, 0):
        rows = chip_rows(s)
        back = nt(d_projected[rows, pl.ds(0, 256)], wq[...])
        back = back + nn(d_projected[rows, pl.ds(256, 128)], wkv[...])
        blocks[s] = back.astype(BF16)
        last_sum.pair(s)
        if s == 1:
            last_sum.far()
    last_sum.near()
    layer_spread = spread(0, layer_out)
    layer_spread.start()
    normed_again.wait()

    def project_grad(j, carry):
        lanes = ds(j * 512, 512)
        values = wide[:, lanes]
        wq[lanes, :] = tn(values, d_projected[:, pl.ds(0, 256)]).astype(BF16)
        wkv[:, lanes] = tn(d_projected[:, pl.ds(256, 128)], values).astype(BF16)
        return carry

    lax.fori_loop(0, 4, project_grad, 0)
    q_sum.start()
    kv_sum.start()
    g_sum.last()
    u_sum.last()
    o_sum.middle()
    last_sum.relay()
    q_sum.middle()
    o_sum.last()
    layer_spread.end()
    last_sum.arrive()
    kv_sum.middle()
    kv_sum.last()
    gain_one = gain_row(gains, 0)

    def input_rows(t, carry):
        rows = ds(t * 16, 16)
        values = x_mine[rows, :].astype(F32)
        back = norm_back(last_sum.total(t * 16, 16), values, gain_one, 0)
        low_rows[rows, :] = (d_residual[rows, :] + back).astype(BF16)
        return carry

    lax.fori_loop(0, TOK // 16, input_rows, 0)
    input_spread = spread(1, input_out)
    input_spread.start()
    col_copies = []
    for k in range(7):
        target = lax.rem(here.c + k + 1, 8)
        col_copies.append(
            remote(
                gain_sums.at[:, ds(target * FEAT, FEAT)],
                gain_cols.at[here.c],
                gain_send.at[k],
                gain_recv.at[k],
                col_peers[k],
            )
        )
        col_copies[k].start()
    gain_cols[here.c] = gain_sums[:, ds(here.c * FEAT, FEAT)]
    for copy in col_copies:
        copy.wait()
    total = gain_cols[0]
    for c in range(1, 8):
        total = total + gain_cols[c]
    gain_rows[here.r] = total
    row_copies = [
        remote(
            gain_rows.at[here.r], gain_rows.at[here.r], last_send.at[k], last_recv.at[k], row_peers[k]
        )
        for k in range(7)
    ]
    for copy in row_copies:
        copy.start()
    q_sum.last()
    kv_sum.end()
    kv_total[...] = kv_sum.own[...].astype(F32) + kv_far[...].astype(F32)
    kv_swaps = []
    for index in range(2):
        theirs = ds(index * HD + (1 - here.k) * (HD // 2), HD // 2)
        land = kv_land.at[pl.ds(index * (HD // 2), HD // 2)]
        kv_swaps.append(
            remote(
                kv_total.at[theirs], land, last_send.at[7 + index], last_recv.at[7 + index], here.partner
            )
        )
        kv_swaps[index].start()
    keep(d_sum.own, gd_own)
    keep(g_sum.own, gg_own)
    keep(u_sum.own, gu_own)
    keep(o_sum.own, go_own)
    keep(q_sum.own, gq_own)
    for index in range(2):
        kv_swaps[index].wait()
        mine = kv_total[ds(index * HD + here.k * (HD // 2), HD // 2), :]
        there = pl.ds(index * (HD // 2), HD // 2)
        kv_final[there, :] = mine + kv_land[there, :]
    keep(kv_final, kv_out)
    for sums in (d_sum, g_sum, u_sum, o_sum, q_sum):
        sums.end()
    for copy in row_copies:
        copy.wait()
    total = gain_rows[0]
    for r in range(1, 8):
        total = total + gain_rows[r]
    gain_cols[0] = total
    twin_copy = remote(gain_cols.at[0], gain_far, gain_send.at[7], gain_recv.at[7], here.twin)
    twin_copy.start()
    twin_copy.wait()
    gain_cols[0] = total + gain_far[...]
    keep(gain_cols.at[0], gains_out)
    input_spread.end()
    last_sum.sent()
    x_collect.sent()
    g_collect.sent()
    for copy in kept:
        if copy is not normed_copy:
            copy.wait()


def layer_call(*args):
    ff = args[6].shape[0]
    any_space = pl.BlockSpec(memory_space=pl.ANY)
    vmem_space = pl.BlockSpec(memory_space=pltpu.VMEM)
    dma = pltpu.SemaphoreType.DMA

    def low(*shape):
        return jax.ShapeDtypeStruct(shape, BF16)

    outs = (
        low(LEN, FEAT),
        low(LEN, FEAT),
        low(ff, FEAT),
        low(ff, FEAT),
        low(ff // 2, FEAT),
        low(ff // 2, FEAT),
        low(ff, FEAT),
        low(ff, FEAT),
        low(256, FEAT),
        low(256, FEAT),
        low(FEAT, 256),
        low(FEAT, 256),
        jax.ShapeDtypeStruct((HD, FEAT), F32),
        jax.ShapeDtypeStruct((8, FEAT), F32),
        low(LEN, D),
        low(8, TOK, FEAT),
    )

    def vmem(*shape, dtype=BF16):
        return pltpu.VMEM(shape, dtype)

    scratch = [
        vmem(8, TOK, FEAT),
        vmem(TOK, D),
        vmem(TOK, D),
        vmem(LEN, D),
        vmem(LEN, D),
        vmem(LEN, ff),
        vmem(LEN, ff),
        vmem(LEN, ff),
        vmem(ff, D),
        vmem(ff, D),
        vmem(ff, D),
        vmem(ff, D),
        vmem(256, D),
        vmem(D, 256),
        vmem(128, D),
        vmem(128, FEAT),
        vmem(128, FEAT),
        vmem(128, FEAT, dtype=F32),
        vmem(HD, FEAT, dtype=F32),
        vmem(HD, FEAT, dtype=F32),
        vmem(8, FEAT, dtype=F32),
        vmem(64, 256, dtype=F32),
        vmem(LEN, 128, dtype=F32),
        vmem(LEN, 128, dtype=F32),
        vmem(LEN, 128, dtype=F32),
        vmem(LEN, 256),
        vmem(LEN, 128),
        vmem(LEN, 128),
        vmem(LEN, 128),
        vmem(LEN, 128),
        vmem(LEN, 256),
        vmem(LEN, 128, dtype=F32),
        vmem(LEN, 256),
        vmem(LEN, 384),
        vmem(LEN, 128, dtype=F32),
        vmem(LEN, 128, dtype=F32),
        vmem(LEN, 128, dtype=F32),
        vmem(LEN, 128, dtype=F32),
        vmem(4, 256, D),
        vmem(4, TOK, D),
        vmem(2, TOK // 2, D),
        vmem(2, TOK, D),
        vmem(TOK, D, dtype=F32),
        vmem(TOK, D, dtype=F32),
        vmem(8, D, dtype=F32),
        vmem(8, 8, FEAT, dtype=F32),
        vmem(8, FEAT, dtype=F32),
        vmem(8, 8, FEAT, dtype=F32),
        vmem(ff, FEAT),
        vmem(3, ff, 2 * FEAT),
        vmem(8, ff // 2, FEAT),
        vmem(3, 2, ff // 2, FEAT),
        vmem(ff // 2, FEAT),
        vmem(4, ff, FEAT),
        vmem(3, ff, FEAT),
        vmem(4, 256, FEAT),
        vmem(3, 256, FEAT),
        vmem(4, FEAT, 256),
        vmem(3, FEAT, 256),
        vmem(128, FEAT),
        vmem(3, 128, 2 * FEAT),
        dma((2, 16)),
        dma((2, 16)),
        dma((2, 2)),
        dma((4, RowGather.SEMS)),
        dma((4, RowGather.SEMS)),
        dma((5,)),
        dma((7, SplitGather.SEMS)),
        dma((7, SplitGather.SEMS)),
        dma((7,)),
        dma((4, RowSum.SEMS)),
        dma((4, RowSum.SEMS)),
        dma((6, SplitSum.SEMS)),
        dma((6, SplitSum.SEMS)),
        dma((2, 8)),
        dma((2, 8)),
        dma((2,)),
        dma((11,)),
        dma((11,)),
        dma((8,)),
        dma((8,)),
        dma((8,)),
        pltpu.SemaphoreType.REGULAR((4,)),
    ]
    return pl.pallas_call(
        layer_kernel,
        out_shape=outs,
        in_specs=[any_space] * 9 + [vmem_space] * 3,
        out_specs=tuple(any_space for _ in outs),
        scratch_shapes=scratch,
        compiler_params=pltpu.CompilerParams(
            collective_id=0, has_side_effects=True, vmem_limit_bytes=VMEM_BYTES
        ),
        cost_estimate=pl.CostEstimate(flops=36 * 10**9, bytes_accessed=60 * 10**6, transcendentals=0),
        name="decoder_layer",
    )(*args)


def finish_kernel(
    layer,
    inner,
    d_own,
    d_far,
    g_own,
    g_far,
    u_own,
    u_far,
    o_own,
    o_far,
    q_own,
    q_far,
    kv,
    gains,
    layer_output,
    grad_input,
    grad_down,
    grad_gate,
    grad_up,
    grad_out,
    grad_query,
    grad_key,
    grad_value,
    grad_attn_gain,
    grad_mlp_gain,
):
    layer_output[...] = layer[...]
    grad_input[...] = inner[...].astype(F32)
    for total, own, far in (
        (grad_down, d_own, d_far),
        (grad_up, u_own, u_far),
        (grad_out, o_own, o_far),
        (grad_query, q_own, q_far),
    ):
        total[...] = own[...].astype(F32) + far[...].astype(F32)
    half = lax.rem(lax.axis_index("dp") + lax.axis_index("col"), 2)
    mine = pl.program_id(0) // 2 == half

    @pl.when(mine)
    def _():
        grad_gate[...] = g_own[...].astype(F32)

    @pl.when(jnp.logical_not(mine))
    def _():
        grad_gate[...] = g_far[...].astype(F32)

    width = grad_key.shape[0]
    grad_key[...] = kv[pl.ds(0, width), :]
    grad_value[...] = kv[pl.ds(width, width), :]
    grad_attn_gain[...] = gains[pl.ds(0, 1), :]
    grad_mlp_gain[...] = gains[pl.ds(1, 1), :]


def finish_call(*args):
    steps = 4
    ff = args[2].shape[0]

    def block(rows, index=lambda i: (i, 0)):
        return pl.BlockSpec((rows, FEAT), index)

    tall, wide, square = block(LEN // steps), block(ff // steps), block(256 // steps)
    halves = block(ff // steps, lambda i: (i % 2, 0))
    whole = block(HD, lambda i: (0, 0))
    kept = block(HD // 2, lambda i: (0, 0))
    gain_block, row = block(8, lambda i: (0, 0)), block(1, lambda i: (0, 0))

    def full(rows, dtype=F32):
        return jax.ShapeDtypeStruct((rows, FEAT), dtype)

    return pl.pallas_call(
        finish_kernel,
        grid=(steps,),
        out_shape=(
            full(LEN, BF16),
            full(LEN),
            full(ff),
            full(ff),
            full(ff),
            full(256),
            full(256),
            full(HD // 2),
            full(HD // 2),
            full(1),
            full(1),
        ),
        in_specs=[tall, tall, wide, wide, halves, halves, wide, wide] + [square] * 4 + [whole, gain_block],
        out_specs=(tall, tall, wide, wide, wide, square, square, kept, kept, row, row),
        name="finish_outputs",
    )(*args)


def body(
    hidden_in,
    segment_ids,
    attn_gain,
    w_query,
    w_key,
    w_value,
    w_out,
    mlp_gain,
    w_gate,
    w_up,
    w_down,
    grad_output,
):
    (
        layer_output,
        grad_input,
        gd_own,
        gd_far,
        gg_own,
        gg_far,
        gu_own,
        gu_far,
        go_own,
        go_far,
        gq_own,
        gq_far,
        grad_kv,
        d_gains,
        _,
        _,
    ) = layer_call(
        hidden_in,
        grad_output,
        w_query,
        w_key.T,
        w_value.T,
        w_out,
        w_gate.T,
        w_up.T,
        w_down,
        attn_gain[None],
        mlp_gain[None],
        segment_ids,
    )

    (
        layer_output,
        grad_input,
        grad_down,
        grad_gate,
        grad_up,
        grad_out_proj,
        grad_query,
        grad_key,
        grad_value,
        grad_attn_gain,
        grad_mlp_gain,
    ) = finish_call(
        layer_output,
        grad_input,
        gd_own,
        gd_far,
        gg_own,
        gg_far,
        gu_own,
        gu_far,
        go_own,
        go_far,
        gq_own,
        gq_far,
        grad_kv,
        d_gains,
    )
    return (
        layer_output,
        grad_input,
        grad_attn_gain[0],
        grad_query,
        grad_key.T,
        grad_value.T,
        grad_out_proj,
        grad_mlp_gain[0],
        grad_gate.T,
        grad_up.T,
        grad_down,
    )


def solution(mesh):
    return jax.shard_map(
        body,
        mesh=mesh,
        in_specs=(
            P(("dp", "row"), "col"),
            P(("dp", "col"), None),
            P("col"),
            P("col", "row"),
            P("col", "row"),
            P("col", "row"),
            P("row", "col"),
            P("col"),
            P("col", "row"),
            P("col", "row"),
            P("row", "col"),
            P(("dp", "row"), "col"),
        ),
        out_specs=(
            P(("dp", "row"), "col"),
            P(("dp", "row"), "col"),
            P("col"),
            P("col", "row"),
            P("col", "row"),
            P("col", "row"),
            P("row", "col"),
            P("col"),
            P("col", "row"),
            P("col", "row"),
            P("row", "col"),
        ),
        check_vma=False,
    )
```

```python
import functools
import math

import jax
import jax.numpy as jnp
from jax import lax
from jax.experimental import pallas as pl
from jax.experimental.pallas import tpu as pltpu
from jax.sharding import PartitionSpec as P

D = 2048
HD = 64
LEN = 1024
ROWS = 8
CHIPS = 4
TOK = LEN // ROWS
FEAT = D // 8
EPSILON = 1e-05
FLOOR_SCORE = -1e30
BF16 = jnp.bfloat16
F32 = jnp.float32
MESH = pl.DeviceIdType.MESH
VMEM_BYTES = 62 * 2**20


def remote(src, dst, send, recv, device):
    return pltpu.make_async_remote_copy(
        src_ref=src, dst_ref=dst, send_sem=send, recv_sem=recv, device_id=device, device_id_type=MESH
    )


def meet(peers):
    barrier = pltpu.get_barrier_semaphore()
    for peer in peers:
        pl.semaphore_signal(barrier, inc=1, device_id=peer, device_id_type=MESH)
    pl.semaphore_wait(barrier, len(peers))


def ds(start, size):
    return pl.ds(pl.multiple_of(start, size), size)


class Place:
    def __init__(self):
        self.d = lax.axis_index("dp")
        self.r = lax.axis_index("row")
        self.c = lax.axis_index("col")
        self.y, self.k = self.r // 2, lax.rem(self.r, 2)
        self.x, self.h = self.c // 2, lax.rem(self.c, 2)
        self.partner = {"row": self.y * 2 + 1 - self.k}
        self.up = {"row": self.row_of(1)}
        self.down = {"row": self.row_of(3)}
        self.other = {"dp": 1 - self.d, "col": self.x * 2 + 1 - self.h}
        self.twin = {"dp": 1 - self.d}
        self.half = lax.rem(self.d + self.h, 2)
        self.x_peers = [{"col": self.col_of(s)} for s in (1, 3, 2)]

    def row_of(self, step):
        return lax.rem(self.y + step, CHIPS) * 2 + self.k

    def col_of(self, step):
        return lax.rem(self.x + step, 4) * 2 + self.h

    def col_from(self, step):
        return lax.rem(self.x + 4 - step, 4) * 2 + self.h


class RowGather:
    SEMS = 13

    def __init__(self, here, place, shard, send, recv):
        self.here, self.place = here, place
        y, k = here.y, here.k
        self.low, self.high, self.far_row = here.row_of(3), here.row_of(1), here.row_of(2)
        self.ups = [
            remote(shard(a), place(here.r, a), send.at[a], recv.at[a], here.up) for a in (0, 1)
        ]
        self.downs = [
            remote(shard(a), place(here.r, a), send.at[2 + a], recv.at[2 + a], here.down)
            for a in (0, 1)
        ]
        self.fars = [
            self.hand_on(self.low, 0, send.at[4], recv.at[4], here.up),
            self.hand_on(self.high, 1, send.at[5], recv.at[5], here.down),
        ]
        self.passes = {}
        for index, (row, a) in enumerate(
            [(self.low, 0), (self.low, 1), (self.high, 0), (self.high, 1), (self.far_row, 0), (self.far_row, 1)]
        ):
            self.passes[index] = self.hand_on(
                row, a, send.at[6 + index], recv.at[6 + index], here.partner
            )
        self.own = [
            remote(shard(None), place(here.r, None), send.at[12], recv.at[12], here.partner)
        ]

    def hand_on(self, row, a, send, recv, device):
        return remote(self.place(row, a), self.place(row, a), send, recv, device)

    def start(self):
        for a, b in ((0, 1), (1, 0)):
            self.ups[a].start()
            self.downs[b].start()
        self.own[0].start()

    def near(self):
        for a, b in ((0, 1), (1, 0)):
            self.ups[a].wait_recv()
            if a == 0:
                self.fars[0].start()
            self.passes[a].start()
            self.downs[b].wait_recv()
            if b == 1:
                self.fars[1].start()
            self.passes[2 + b].start()

    def far(self):
        for a in (0, 1):
            self.fars[a].wait_recv()
            self.passes[4 + a].start()

    def got_own(self):
        self.own[0].wait_recv()

    def got_near(self):
        for index in range(4):
            self.passes[index].wait_recv()

    def got_far(self):
        for index in (4, 5):
            self.passes[index].wait_recv()

    def sent(self):
        for copy in self.ups + self.downs + self.fars + self.own + list(self.passes.values()):
            copy.wait_send()


class ColGather:
    SEMS = 7

    def __init__(self, here, shard, place, send, recv, local, across_first):
        self.here, self.place, self.across_first = here, place, across_first
        self.local = pltpu.make_async_copy(shard, place(here.c), local)
        self.lines = [
            remote(shard, place(here.c), send.at[i], recv.at[i], here.x_peers[i]) for i in range(3)
        ]
        self.across = [remote(shard, place(here.c), send.at[3], recv.at[3], here.other)]
        there = here.x * 2 + 1 - here.h
        if across_first:
            self.seconds = [
                remote(place(there), place(there), send.at[4 + i], recv.at[4 + i], here.x_peers[i])
                for i in range(3)
            ]
        else:
            self.seconds = []
            for i, step in enumerate((1, 3, 2)):
                source = here.col_from(step)
                self.seconds.append(
                    remote(place(source), place(source), send.at[4 + i], recv.at[4 + i], here.other)
                )

    def start(self):
        self.start_across()
        self.start_lines()

    def start_across(self):
        self.local.start()
        self.across[0].start()

    def start_lines(self):
        for copy in self.lines:
            copy.start()

    def middle(self):
        if self.across_first:
            self.across[0].wait_recv()
            for copy in self.seconds:
                copy.start()
        else:
            for copy, second in zip(self.lines, self.seconds):
                copy.wait_recv()
                second.start()

    def end(self):
        self.local.wait()
        if self.across_first:
            for copy in self.lines:
                copy.wait_recv()
        else:
            self.across[0].wait_recv()
        for copy in self.seconds:
            copy.wait_recv()
        for copy in self.lines + self.across + self.seconds:
            copy.wait_send()


class SplitGather:
    SEMS = 14

    def __init__(self, here, shard, place, send, recv, local):
        self.here, self.place = here, place
        half = here.half
        self.local = pltpu.make_async_copy(shard(None), place(here.c, None), local)

        def hand_on(c, index, device):
            return remote(place(c, half), place(c, half), send.at[index], recv.at[index], device)

        own = place(here.c, half)
        self.across = remote(shard(half), own, send.at[0], recv.at[0], here.other)
        self.lines = [
            remote(shard(half), own, send.at[1 + i], recv.at[1 + i], here.x_peers[i]) for i in range(3)
        ]
        there = here.x * 2 + 1 - here.h
        self.seconds = [hand_on(there, 4 + i, here.x_peers[i]) for i in range(3)]
        sources = [here.col_from(step) for step in (1, 3, 2)]
        others = [source + 1 - 2 * here.h for source in sources]
        self.swaps = [
            hand_on(c, 7 + i, here.twin) for i, c in enumerate([there] + sources + others)
        ]

    def start_across(self):
        self.local.start()
        self.across.start()

    def start_lines(self):
        for copy in self.lines:
            copy.start()

    def middle(self):
        self.across.wait_recv()
        for copy in self.seconds:
            copy.start()
        self.swaps[0].start()

    def late(self, which):
        copies = self.seconds if which else self.lines
        for copy, swap in zip(copies, self.swaps[1 + 3 * which :]):
            copy.wait_recv()
            swap.start()

    def end(self):
        self.local.wait()
        for swap in self.swaps:
            swap.wait_recv()
        for copy in [self.across] + self.lines + self.seconds + self.swaps:
            copy.wait_send()


class RowSum:
    SEMS = 10

    def __init__(self, here, blocks, paired, relayed, landed, send, recv):
        self.here, self.blocks, self.paired = here, blocks, paired
        self.relayed, self.landed = relayed, landed
        k, half = here.k, TOK // 2
        self.mine, self.half = k * TOK, half
        self.pairs = [
            remote(
                blocks.at[s, ds((1 - k) * TOK, TOK)], paired.at[s], send.at[s], recv.at[s], here.partner
            )
            for s in range(4)
        ]
        self.fars = [
            remote(self.part(2, 0), relayed.at[0], send.at[4], recv.at[4], here.up),
            remote(self.part(2, 1), relayed.at[1], send.at[5], recv.at[5], here.down),
        ]
        self.nears = {}
        for index, (s, a, device) in enumerate(
            [(1, 1, here.up), (3, 0, here.down), (1, 0, here.up), (3, 1, here.down)]
        ):
            slot = 0 if s == 1 else 1
            self.nears[s, a] = remote(
                self.part(s, a),
                landed.at[slot, pl.ds(a * half, half)],
                send.at[6 + index],
                recv.at[6 + index],
                device,
            )

    def part(self, s, a):
        return self.blocks.at[s, ds(self.mine + a * self.half, self.half)]

    def add(self, s, a, other):
        part = self.part(s, a)
        part[...] = (part[...].astype(F32) + other[...].astype(F32)).astype(BF16)

    def pair(self, s):
        self.pairs[s].start()

    def join(self, s):
        self.pairs[s].wait_recv()
        for a in (0, 1):
            self.add(s, a, self.paired.at[s, pl.ds(a * self.half, self.half)])

    def far(self):
        self.join(2)
        self.fars[0].start()
        self.fars[1].start()

    def near(self):
        self.join(1)
        self.nears[1, 1].start()
        self.join(3)
        self.nears[3, 0].start()

    def relay(self):
        self.fars[0].wait_recv()
        self.add(1, 0, self.relayed.at[0])
        self.nears[1, 0].start()
        self.fars[1].wait_recv()
        self.add(3, 1, self.relayed.at[1])
        self.nears[3, 1].start()

    def arrive(self):
        self.pairs[0].wait_recv()
        for copy in self.nears.values():
            copy.wait_recv()

    def total(self, start, rows):
        own = self.blocks[0, pl.ds(pl.multiple_of(self.mine + start, rows), rows)].astype(F32)
        here = pl.ds(pl.multiple_of(start, rows), rows)
        return (
            own
            + self.paired[0, here].astype(F32)
            + self.landed[0, here].astype(F32)
            + self.landed[1, here].astype(F32)
        )

    def sent(self):
        for copy in self.pairs + self.fars + list(self.nears.values()):
            copy.wait_send()


def add_rows(rows, target, others):
    kind = target.dtype

    def step(t, carry):
        at = ds(t * rows, rows)
        total = target[at, :].astype(F32)
        for other in others:
            total = total + other[at, :].astype(F32)
        target[at, :] = total.astype(kind)
        return carry

    lax.fori_loop(0, target.shape[0] // rows, step, 0)


class WeightSum:
    SEMS = 8

    def __init__(self, here, part, wide_part, rows, z_land, x_land, far_part, send, recv, across_first):
        self.here, self.part, self.across_first, self.rows = here, part, across_first, rows
        self.z_land, self.x_land = z_land, x_land
        self.own = part(here.c)
        steps = (1, 3, 2)
        if across_first:
            self.mine = [part(x * 2 + here.h) for x in range(4)]
            self.across = [
                remote(part(x * 2 + 1 - here.h), z_land.at[x], send.at[x], recv.at[x], here.other)
                for x in range(4)
            ]
            self.lines = [
                remote(
                    part(here.col_of(step)), x_land.at[i], send.at[4 + i], recv.at[4 + i], here.x_peers[i]
                )
                for i, step in enumerate(steps)
            ]
        else:
            self.wide = wide_part(here.x)
            self.across = [
                remote(
                    part(here.x * 2 + 1 - here.h), z_land, send.at[3], recv.at[3], here.other
                )
            ]
            self.lines = [
                remote(
                    wide_part(lax.rem(here.x + step, 4)),
                    x_land.at[i],
                    send.at[i],
                    recv.at[i],
                    here.x_peers[i],
                )
                for i, step in enumerate(steps)
            ]
        self.swap = remote(self.own, far_part, send.at[7], recv.at[7], here.twin)

    def add(self, target, others):
        add_rows(self.rows, target, others)

    def start(self):
        for copy in self.across if self.across_first else self.lines:
            copy.start()

    def middle(self):
        if self.across_first:
            for x in range(4):
                self.across[x].wait_recv()
                self.add(self.mine[x], [self.z_land.at[x]])
            for copy in self.lines:
                copy.start()
        else:
            for copy in self.lines:
                copy.wait_recv()
            self.add(self.wide, [self.x_land.at[i] for i in range(3)])
            self.across[0].start()

    def last(self):
        if self.across_first:
            for copy in self.lines:
                copy.wait_recv()
            self.add(self.own, [self.x_land.at[i] for i in range(3)])
        else:
            self.across[0].wait_recv()
            self.add(self.own, [self.z_land])
        self.swap.start()

    def end(self):
        self.swap.wait()
        for copy in self.across + self.lines:
            copy.wait_send()


class SplitSum:
    SEMS = 16

    def __init__(self, here, part, rows, twin_land, x_land, z_land, far_part, send, recv):
        self.here, self.rows = here, rows
        self.twin_land, self.x_land, self.z_land = twin_land, x_land, z_land
        half, x, h = here.half, here.x, here.h
        self.mine = [part(c, half) for c in range(8)]
        self.twins = [
            remote(part(c, 1 - half), twin_land.at[c], send.at[c], recv.at[c], here.twin)
            for c in range(8)
        ]
        self.lines = []
        for i, step in enumerate((1, 3, 2)):
            target = lax.rem(x + step, 4) * 2
            for side in range(2):
                index = 8 + 2 * i + side
                self.lines.append(
                    remote(
                        part(target + side, half),
                        x_land.at[i, side],
                        send.at[index],
                        recv.at[index],
                        here.x_peers[i],
                    )
                )
        self.sides = [part(x * 2 + side, half) for side in range(2)]
        self.across = remote(part(x * 2 + 1 - h, half), z_land, send.at[14], recv.at[14], here.other)
        self.own = part(here.c, half)
        self.swap = remote(self.own, far_part, send.at[15], recv.at[15], here.twin)

    def add(self, target, others):
        add_rows(self.rows, target, others)

    def start(self):
        for copy in self.twins:
            copy.start()

    def middle(self):
        for c in range(8):
            self.twins[c].wait_recv()
            self.add(self.mine[c], [self.twin_land.at[c]])
        for copy in self.lines:
            copy.start()

    def late(self):
        for copy in self.lines:
            copy.wait_recv()
        for side in range(2):
            self.add(self.sides[side], [self.x_land.at[i, side] for i in range(3)])
        self.across.start()

    def last(self):
        self.across.wait_recv()
        self.add(self.own, [self.z_land])
        self.swap.start()

    def end(self):
        self.swap.wait()
        for copy in self.twins + self.lines + [self.across]:
            copy.wait_send()


class Spread:
    def __init__(self, here, source, target, send, recv, local):
        self.here = here
        self.same = here.r == here.c
        self.copies = []
        place = target.at[ds(here.r * TOK, TOK)]
        for j in range(8):
            shard = source.at[:, pl.ds(j * FEAT, FEAT)]
            self.copies.append(
                (
                    remote(shard, place, send.at[j], recv.at[here.r], {"row": here.c, "col": j}),
                    pltpu.make_async_copy(shard, place, local),
                )
            )
        self.arrivals = [
            remote(
                source.at[:, pl.ds(0, FEAT)],
                target.at[pl.ds(i * TOK, TOK)],
                send.at[i],
                recv.at[i],
                {"row": here.c, "col": i},
            )
            for i in range(8)
        ]

    def each(self, index, other, own):
        itself = self.same & (self.here.r == index)
        pl.when(itself)(own)
        pl.when(jnp.logical_not(itself))(other)

    def start(self):
        for j, (copy, local) in enumerate(self.copies):
            self.each(j, copy.start, local.start)

    def end(self):
        for j, (copy, local) in enumerate(self.copies):
            self.each(j, copy.wait_send, local.wait)
        for i, copy in enumerate(self.arrivals):
            self.each(i, copy.wait_recv, lambda: None)


class Collect:
    def __init__(self, here, source, middle, target, send, recv, local):
        self.here = here
        r, c = here.r, here.c
        self.local = pltpu.make_async_copy(source.at[ds(r * TOK, TOK)], middle.at[r], local.at[0])
        self.firsts = []
        self.seconds = []
        lanes = target.at[:, ds(c * FEAT, FEAT)]
        for k in range(1, 8):
            i = lax.rem(r + k, 8)
            self.firsts.append(
                remote(
                    source.at[ds(i * TOK, TOK)], middle.at[r], send.at[k], recv.at[k], {"row": i}
                )
            )
        for k in range(8):
            a = lax.rem(r + 8 - k, 8)
            self.seconds.append(
                (
                    a == c,
                    remote(middle.at[a], lanes, send.at[8 + k], recv.at[8 + c], {"col": a}),
                    pltpu.make_async_copy(middle.at[a], lanes, local.at[1]),
                )
            )
        self.arrivals = [
            (
                c == j,
                remote(
                    middle.at[0],
                    target.at[:, pl.ds(j * FEAT, FEAT)],
                    send.at[8 + j],
                    recv.at[8 + j],
                    {"col": j},
                ),
            )
            for j in range(8)
        ]

    def start(self):
        self.local.start()
        for copy in self.firsts:
            copy.start()

    def turn(self):
        self.local.wait()
        for k, (itself, copy, local) in enumerate(self.seconds):
            if k > 0:
                self.firsts[k - 1].wait_recv()
            pl.when(itself)(local.start)
            pl.when(jnp.logical_not(itself))(copy.start)

    def arrive(self):
        for itself, copy, local in self.seconds:
            pl.when(itself)(local.wait)
        for itself, copy in self.arrivals:
            pl.when(jnp.logical_not(itself))(copy.wait_recv)

    def sent(self):
        for copy in self.firsts:
            copy.wait_send()
        for itself, copy, local in self.seconds:
            pl.when(jnp.logical_not(itself))(copy.wait_send)


def nn(a, b):
    return jnp.dot(a, b, preferred_element_type=F32)


def nt(a, b):
    return lax.dot_general(a, b, (((1,), (1,)), ((), ())), preferred_element_type=F32)


def tn(a, b):
    return lax.dot_general(a, b, (((0,), (0,)), ((), ())), preferred_element_type=F32)


def swap_halves(values):
    width = values.shape[-1]
    lane = lax.broadcasted_iota(jnp.int32, values.shape, 1)
    return jnp.where(
        lax.rem(lane, HD) < HD // 2, pltpu.roll(values, width - HD // 2, 1), pltpu.roll(values, HD // 2, 1)
    )


def turn(values, cos, sin):
    return values * cos + swap_halves(values) * sin


def gain_row(gains, which):
    return jnp.concatenate([gains[pl.ds(8 * j + which, 1), :] for j in range(8)], axis=1)


def layer_kernel(
    x_in,
    g_in,
    wq_in,
    wk_in,
    wv_in,
    wo_in,
    wg_in,
    wu_in,
    wd_in,
    attn_in,
    mlp_in,
    seg_in,
    layer_out,
    input_out,
    gd_own,
    gd_far,
    gg_own,
    gg_far,
    gu_own,
    gu_far,
    go_own,
    go_far,
    gq_own,
    gq_far,
    kv_out,
    gains_out,
    normed_kept,
    g_middle,
    x_middle,
    x_mine,
    low_rows,
    wide,
    g_all,
    act,
    gate,
    up,
    wd,
    gd,
    wg,
    wu,
    wo,
    wq,
    wkv,
    kv_shard,
    kv_far,
    kv_total,
    kv_land,
    kv_final,
    gain_shard,
    gains,
    cos,
    sin,
    seg_col,
    query,
    k_low,
    k_high,
    v_low,
    v_high,
    mixed,
    totals,
    d_mixed,
    d_projected,
    dk_low,
    dk_high,
    dv_low,
    dv_high,
    blocks,
    paired,
    relayed,
    landed,
    residual,
    d_residual,
    gain_sums,
    gain_cols,
    gain_far,
    gain_rows,
    gd_z,
    gd_x,
    gg_twin,
    gg_x,
    gg_z,
    gu_z,
    gu_x,
    go_z,
    go_x,
    gq_z,
    gq_x,
    kv_z,
    kv_x,
    collect_send,
    collect_recv,
    collect_local,
    gather_send,
    gather_recv,
    gather_local,
    w_send,
    w_recv,
    w_local,
    rows_send,
    rows_recv,
    sum_send,
    sum_recv,
    spread_send,
    spread_recv,
    spread_local,
    last_send,
    last_recv,
    gain_send,
    gain_recv,
    keep_sem,
    free,
):
    here = Place()
    same = here.r == here.c
    barrier = pltpu.get_barrier_semaphore()
    row_peers = [{"row": lax.rem(here.r + k, ROWS)} for k in range(1, ROWS)]
    col_peers = [{"col": lax.rem(here.c + k, 8)} for k in range(1, 8)]
    peers = row_peers + col_peers + [here.other, here.twin]
    for peer in peers:
        pl.semaphore_signal(barrier, inc=1, device_id=peer, device_id_type=MESH)
    for i in range(8):

        @pl.when(jnp.logical_not(same & (here.r == i)))
        def _():
            pl.semaphore_signal(
                barrier, inc=1, device_id={"row": i, "col": here.r}, device_id_type=MESH
            )

    pl.semaphore_wait(barrier, len(peers) + 8 - same.astype(jnp.int32))

    def token_place(ref):
        def place(row, a):
            if a is None:
                return ref.at[ds(row * TOK, TOK)]
            return ref.at[ds(row * TOK + a * (TOK // 2), TOK // 2)]

        return place

    def own_part(ref):
        place = token_place(ref)
        return lambda a: place(here.r, a)

    def low_part(a):
        return low_rows if a is None else low_rows.at[pl.ds(a * (TOK // 2), TOK // 2)]

    def row_gather(index, ref, shard):
        return RowGather(here, token_place(ref), shard, gather_send.at[index], gather_recv.at[index])

    def row_sum(index):
        return RowSum(here, blocks, paired, relayed, landed, rows_send.at[index], rows_recv.at[index])

    def collect(index, source, middle, target):
        return Collect(
            here,
            source,
            middle,
            target,
            collect_send.at[index],
            collect_recv.at[index],
            collect_local.at[index],
        )

    def spread(index, target):
        return Spread(
            here,
            low_rows,
            target,
            spread_send.at[index],
            spread_recv.at[index],
            spread_local.at[index],
        )

    def col_gather(index, shard, place, across_first):
        return ColGather(
            here, shard, place, w_send.at[index], w_recv.at[index], w_local.at[index], across_first
        )

    def split_gather(index, shard, ref):
        half = ref.shape[0] // 2

        def place(c, a):
            lanes = ds(c * FEAT, FEAT)
            return ref.at[:, lanes] if a is None else ref.at[ds(a * half, half), lanes]

        def part(a):
            return shard if a is None else shard.at[ds(a * half, half)]

        return SplitGather(
            here, part, place, w_send.at[index], w_recv.at[index], w_local.at[index]
        )

    def weight_sum(index, parts, rows, z_land, x_land, far_part, across_first):
        return WeightSum(
            here,
            parts[0],
            parts[1],
            rows,
            z_land,
            x_land,
            far_part,
            sum_send.at[index],
            sum_recv.at[index],
            across_first,
        )

    def rows_of(ref):
        return lambda c: ref.at[ds(c * FEAT, FEAT)], lambda x: ref.at[ds(x * 2 * FEAT, 2 * FEAT)]

    def lanes_of(ref):
        return (
            lambda c: ref.at[:, ds(c * FEAT, FEAT)],
            lambda x: ref.at[:, ds(x * 2 * FEAT, 2 * FEAT)],
        )

    def credit(index):
        for peer in (here.partner, here.up, here.down):
            pl.semaphore_signal(free.at[index], inc=1, device_id=peer, device_id_type=MESH)

    def chip_rows(s):
        return ds(lax.rem(here.y + s, CHIPS) * 256, 256)

    kept = []

    def keep(src, dst):
        copy = pltpu.make_async_copy(src, dst, keep_sem.at[len(kept)])
        copy.start()
        kept.append(copy)
        return copy

    x_collect = collect(0, x_in, x_middle, x_mine)
    g_collect = collect(1, g_in, g_middle, low_rows)
    n1_gather = row_gather(0, wide, own_part(wide))
    g_gather = row_gather(1, g_all, low_part)
    n2_gather = row_gather(2, wide, own_part(wide))
    d_gather = row_gather(3, g_all, low_part)
    gain_gather = col_gather(0, gain_shard, lambda c: gains.at[ds(c * 8, 8)], True)
    wq_gather = col_gather(1, wq_in, lambda c: wq.at[ds(c * FEAT, FEAT)], False)
    kv_gather = col_gather(2, kv_shard, lambda c: wkv.at[:, ds(c * FEAT, FEAT)], False)
    wo_gather = col_gather(3, wo_in, lambda c: wo.at[:, ds(c * FEAT, FEAT)], False)
    wd_gather = col_gather(4, wd_in, lambda c: wd.at[:, ds(c * FEAT, FEAT)], False)
    wg_gather = split_gather(5, wg_in, wg)
    wu_gather = split_gather(6, wu_in, wu)
    d_sum = weight_sum(0, lanes_of(gd), 32, gd_z, gd_x, gd_far, False)
    u_sum = weight_sum(1, lanes_of(wu), 64, gu_z, gu_x, gu_far, True)
    o_sum = weight_sum(2, lanes_of(wo), 64, go_z, go_x, go_far, True)
    q_sum = weight_sum(3, rows_of(wq), 64, gq_z, gq_x, gq_far, True)
    kv_sum = weight_sum(4, lanes_of(wkv), 32, kv_z, kv_x, kv_far, False)
    g_half = wg.shape[0] // 2
    g_sum = SplitSum(
        here,
        lambda c, a: wg.at[ds(a * g_half, g_half), ds(c * FEAT, FEAT)],
        32,
        gg_twin,
        gg_x,
        gg_z,
        gg_far,
        sum_send.at[5],
        sum_recv.at[5],
    )
    kv_copies = []
    for index, part in enumerate((wk_in, wv_in)):
        rows = ds(index * HD + here.k * (HD // 2), HD // 2)
        local = pltpu.make_async_copy(part, kv_shard.at[rows], gather_local.at[3 + index])
        other = remote(
            part, kv_shard.at[rows], last_send.at[9 + index], last_recv.at[9 + index], here.partner
        )
        kv_copies += [local, other]

    for copy in kv_copies:
        copy.start()
    gain_shard[pl.ds(0, 4), :] = jnp.broadcast_to(attn_in[...], (4, FEAT))
    gain_shard[pl.ds(4, 4), :] = jnp.broadcast_to(mlp_in[...], (4, FEAT))
    gain_gather.start()
    wu_gather.start_across()
    x_collect.start()
    wq_gather.start_across()
    wg_gather.start_across()
    wq_gather.start_lines()
    segments = seg_in[0:1, :]
    places = lax.broadcasted_iota(jnp.int32, (1, LEN), 1)
    for number in range(3):
        count = jnp.sum((segments == number).astype(F32), axis=1, keepdims=True).astype(jnp.int32)
        places = places - jnp.where(segments > number, count, 0)
    tall = jnp.transpose(jnp.broadcast_to(places.astype(F32), (128, LEN)))
    lanes = lax.broadcasted_iota(jnp.int32, (1, 128), 1)
    step = (2 * lax.rem(lanes, HD // 2)).astype(F32)
    angles = tall * jnp.exp(step * (-math.log(10000.0) / HD))
    sign = jnp.where(lax.rem(lanes, HD) < HD // 2, -1.0, 1.0)
    cos[...] = jnp.cos(angles)
    sin[...] = jnp.sin(angles) * sign
    seg_col[...] = jnp.transpose(jnp.broadcast_to(segments.astype(F32), (128, LEN)))
    seg_row = segments.astype(F32)
    for copy in kv_copies:
        copy.wait()
    gain_gather.middle()
    kv_gather.start_across()
    kv_gather.start_lines()
    x_collect.turn()
    g_collect.start()
    wq_gather.middle()
    wo_gather.start()
    gain_gather.end()
    gain_one = gain_row(gains, 0)
    x_collect.arrive()

    def norm_rows(t, carry):
        values = x_mine[ds(t * 16, 16), :].astype(F32)
        scale = lax.rsqrt(jnp.sum(values * values, axis=1, keepdims=True) * (1.0 / D) + EPSILON)
        wide[ds(here.r * TOK + t * 16, 16), :] = (values * scale * gain_one).astype(BF16)
        return carry

    lax.fori_loop(0, TOK // 16, norm_rows, 0)
    wu_gather.start_lines()
    n1_gather.start()
    kv_gather.middle()
    wo_gather.middle()
    wu_gather.middle()
    lane = lax.broadcasted_iota(jnp.int32, (256, 128), 1)

    def project(s):
        rows = chip_rows(s)
        values = wide[rows, :]
        projected = nn(values, wq[...])
        cos_rows, sin_rows = cos[rows, :], sin[rows, :]
        for p in range(2):
            pair = turn(projected[:, p * 128 : (p + 1) * 128], cos_rows, sin_rows)
            query[rows, pl.ds(p * 128, 128)] = (pair * HD**-0.5).astype(BF16)
        key_value = nt(values, wkv[...])
        key = jnp.where(lane < HD, turn(key_value, cos_rows, sin_rows), 0.0)
        value = jnp.where(lane < HD, 0.0, key_value)
        k_low[rows, :] = key.astype(BF16)
        k_high[rows, :] = pltpu.roll(key, HD, 1).astype(BF16)
        v_high[rows, :] = value.astype(BF16)
        v_low[rows, :] = pltpu.roll(value, HD, 1).astype(BF16)

    n1_gather.near()
    g_collect.turn()
    wu_gather.late(0)
    wq_gather.end()
    kv_gather.end()
    n1_gather.got_own()
    project(0)
    n1_gather.got_near()
    project(1)
    n1_gather.far()
    project(3)
    n1_gather.got_far()
    project(2)
    normed_copy = keep(wide, normed_kept)
    g_collect.arrive()
    own_g = pltpu.make_async_copy(low_rows, token_place(g_all)(here.r, None), gather_local.at[0])
    own_g.start()
    g_gather.start()

    def bias_of(block, keys):
        first = block * 256
        row = lax.broadcasted_iota(jnp.int32, (256, keys), 0) + first
        key = lax.broadcasted_iota(jnp.int32, (256, keys), 1)
        alike = seg_col[pl.ds(first, 256), 0:1] == seg_row[:, :keys]
        return jnp.where(alike & (key <= row), 0.0, FLOOR_SCORE)

    def attend(block):
        keys = (block + 1) * 256
        rows, seen = pl.ds(block * 256, 256), pl.ds(0, keys)
        bias = bias_of(block, keys)

        def one_pair(p, sums):
            lanes = ds(p * 128, 128)
            pair = query[rows, lanes]
            out = jnp.zeros((256, 128), F32)
            for side, (key, value) in enumerate(((k_low, v_low), (k_high, v_high))):
                scores = nt(pair, key[seen, :]) + bias
                row_max = jnp.max(scores, axis=1, keepdims=True)
                exps = jnp.exp(scores - row_max)
                row_sum = jnp.sum(exps, axis=1, keepdims=True)
                out = out + nn(exps.astype(BF16), value[seen, :]) * (1.0 / row_sum)
                sums = jnp.where(lane == 2 * p + side, row_max + jnp.log(row_sum), sums)
            mixed[rows, lanes] = out.astype(BF16)
            return sums

        totals[rows, :] = lax.fori_loop(0, 2, one_pair, jnp.zeros((256, 128), F32))

    attend(0)
    wg_gather.start_lines()
    attend(1)
    wg_gather.middle()
    attend(2)
    attend(3)
    wu_gather.late(1)
    wo_gather.end()
    normed_copy.wait()
    n1_gather.sent()
    out_sum = row_sum(0)
    for s in (2, 1, 3, 0):
        blocks[s] = nn(mixed[chip_rows(s), :], wo[...]).astype(BF16)
        out_sum.pair(s)
        if s == 1:
            out_sum.far()
    out_sum.near()
    wg_gather.late(0)
    out_sum.relay()
    wd_gather.start()
    out_sum.arrive()
    wg_gather.late(1)
    gain_two = gain_row(gains, 4)

    def residual_rows(t, carry):
        rows = ds(t * 16, 16)
        values = x_mine[rows, :].astype(F32) + out_sum.total(t * 16, 16)
        residual[rows, :] = values
        scale = lax.rsqrt(jnp.sum(values * values, axis=1, keepdims=True) * (1.0 / D) + EPSILON)
        wide[ds(here.r * TOK + t * 16, 16), :] = (values * scale * gain_two).astype(BF16)
        return carry

    lax.fori_loop(0, TOK // 16, residual_rows, 0)
    n2_gather.start()
    wd_gather.middle()
    g_gather.near()
    credit(0)
    out_sum.sent()

    def feed(s):
        rows = chip_rows(s)
        values = wide[rows, :]
        gate_rows = nt(values, wg[...])
        up_rows = nt(values, wu[...])
        gate[rows, :] = gate_rows.astype(BF16)
        up[rows, :] = up_rows.astype(BF16)
        act[rows, :] = (gate_rows * (1.0 / (1.0 + jnp.exp(-gate_rows))) * up_rows).astype(BF16)

    n2_gather.near()
    wg_gather.end()
    wu_gather.end()
    n2_gather.got_own()
    feed(0)
    n2_gather.got_near()
    feed(1)
    g_gather.far()
    feed(3)
    n2_gather.far()
    n2_gather.got_far()
    feed(2)

    g_gather.got_own()
    g_gather.got_near()
    g_gather.got_far()
    own_g.wait()
    wd_gather.end()
    first_sum = row_sum(1)
    pl.semaphore_wait(free.at[0], 3)

    def down_grad(j, carry):
        lanes = ds(j * 512, 512)
        gd[:, lanes] = tn(act[...], g_all[:, lanes]).astype(BF16)
        return carry

    for s in (2, 1, 3, 0):
        rows = chip_rows(s)
        d_act = nt(g_all[rows, :], wd[...])
        gate_rows = gate[rows, :].astype(F32)
        up_rows = up[rows, :].astype(F32)
        sig = 1.0 / (1.0 + jnp.exp(-gate_rows))
        d_up = (d_act * (gate_rows * sig)).astype(BF16)
        d_gate = (d_act * up_rows * (sig * (1.0 + gate_rows * (1.0 - sig)))).astype(BF16)
        gate[rows, :] = d_gate
        up[rows, :] = d_up
        blocks[s] = (nn(d_gate, wg[...]) + nn(d_up, wu[...])).astype(BF16)
        first_sum.pair(s)
        if s == 1:
            first_sum.far()
    first_sum.near()
    lax.fori_loop(0, 4, down_grad, 0)
    d_sum.start()
    g_gather.sent()
    credit(1)
    first_sum.relay()
    n2_gather.sent()

    def gate_grad(j, carry):
        lanes = ds(j * 512, 512)
        wg[:, lanes] = tn(gate[...], wide[:, lanes]).astype(BF16)
        return carry

    lax.fori_loop(0, 4, gate_grad, 0)
    g_sum.start()

    first_sum.arrive()
    gain_sums[...] = jnp.zeros_like(gain_sums)

    def norm_back(total, values, gain, which):
        scale = lax.rsqrt(jnp.sum(values * values, axis=1, keepdims=True) * (1.0 / D) + EPSILON)
        scaled = total * gain
        inner = jnp.sum(scaled * values, axis=1, keepdims=True) * (1.0 / D)
        part = jnp.sum(total * values * scale, axis=0, keepdims=True)
        gain_sums[pl.ds(which, 1), :] = gain_sums[pl.ds(which, 1), :] + part
        return scale * scaled - values * (scale * scale * scale * inner)

    def residual_back_rows(t, carry):
        rows = ds(t * 16, 16)
        back = norm_back(first_sum.total(t * 16, 16), residual[rows, :], gain_two, 1)
        total = low_rows[rows, :].astype(F32) + back
        d_residual[rows, :] = total
        low_rows[rows, :] = total.astype(BF16)
        return carry

    lax.fori_loop(0, TOK // 16, residual_back_rows, 0)
    credit(2)
    pl.semaphore_wait(free.at[1], 3)
    own_rows = pltpu.make_async_copy(low_rows, token_place(g_all)(here.r, None), gather_local.at[2])
    own_rows.start()
    d_gather.start()
    first_sum.sent()
    layer_sum = row_sum(2)

    def up_grad(j, carry):
        lanes = ds(j * 512, 512)
        wu[:, lanes] = tn(up[...], wide[:, lanes]).astype(BF16)
        return carry

    lax.fori_loop(0, 4, up_grad, 0)
    u_sum.start()
    normed_again = pltpu.make_async_copy(normed_kept, wide, gather_local.at[1])
    normed_again.start()


    def down_block(s):
        blocks[s] = nn(act[chip_rows(s), :], wd[...]).astype(BF16)

    for s in (2, 1):
        down_block(s)
    d_gather.near()
    for s in (3, 0):
        down_block(s)
    pl.semaphore_wait(free.at[2], 3)
    for s in (2, 1, 3, 0):
        layer_sum.pair(s)
    d_gather.far()
    layer_sum.far()
    g_sum.middle()

    def mix_back(s):
        rows = chip_rows(s)
        d_mixed[rows, :] = nt(g_all[rows, :], wo[...]).astype(BF16)

    own_rows.wait()
    d_gather.got_own()
    mix_back(0)
    d_gather.got_near()
    mix_back(1)
    mix_back(3)
    d_gather.got_far()
    mix_back(2)
    d_sum.middle()

    def out_grad(j, carry):
        lanes = ds(j * 512, 512)
        wo[:, lanes] = tn(mixed[...], g_all[:, lanes]).astype(BF16)
        return carry

    lax.fori_loop(0, 4, out_grad, 0)
    layer_sum.near()
    for sums in (dk_low, dk_high, dv_low, dv_high):
        sums[...] = jnp.zeros_like(sums)

    def attend_back(block):
        keys = (block + 1) * 256
        rows, seen = pl.ds(block * 256, 256), pl.ds(0, keys)
        bias = bias_of(block, keys)
        cos_rows, sin_rows = cos[rows, :], sin[rows, :]

        def one_pair(p, carry):
            lanes = ds(p * 128, 128)
            pair = query[rows, lanes]
            grads = d_mixed[rows, lanes]
            product = grads.astype(F32) * mixed[rows, lanes].astype(F32)
            out = jnp.zeros((256, 128), F32)
            for side, (key, value, dk, dv) in enumerate(
                ((k_low, v_low, dk_low, dv_low), (k_high, v_high, dk_high, dv_high))
            ):
                half = (lane < HD) if side == 0 else (lane >= HD)
                inner = jnp.sum(jnp.where(half, product, 0.0), axis=1, keepdims=True)
                total = jnp.sum(
                    jnp.where(lane == 2 * p + side, totals[rows, :], 0.0), axis=1, keepdims=True
                )
                probs = jnp.exp(nt(pair, key[seen, :]) + bias - total)
                d_probs = nt(grads, value[seen, :])
                d_scores = (probs * (d_probs - inner)).astype(BF16)
                out = out + nn(d_scores, key[seen, :])
                dk[seen, :] = dk[seen, :] + tn(d_scores, pair)
                dv[seen, :] = dv[seen, :] + tn(probs.astype(BF16), grads)
            d_projected[rows, lanes] = turn(out * HD**-0.5, cos_rows, -sin_rows).astype(BF16)
            return carry

        lax.fori_loop(0, 2, one_pair, 0)

    attend_back(3)
    layer_sum.relay()
    attend_back(2)
    u_sum.middle()
    o_sum.start()
    attend_back(1)
    attend_back(0)
    g_sum.late()

    def key_rows(t, carry):
        rows = ds(t * 256, 256)
        key = dk_low[rows, :] + pltpu.roll(dk_high[rows, :], HD, 1)
        value = dv_high[rows, :] + pltpu.roll(dv_low[rows, :], HD, 1)
        key = turn(key, cos[rows, :], -sin[rows, :])
        d_projected[rows, pl.ds(256, 128)] = jnp.where(lane < HD, key, value).astype(BF16)
        return carry

    lax.fori_loop(0, 4, key_rows, 0)
    layer_sum.arrive()
    d_gather.sent()

    def layer_rows(t, carry):
        rows = ds(t * 16, 16)
        low_rows[rows, :] = (residual[rows, :] + layer_sum.total(t * 16, 16)).astype(BF16)
        return carry

    lax.fori_loop(0, TOK // 16, layer_rows, 0)
    d_sum.last()
    credit(3)
    layer_sum.sent()
    last_sum = row_sum(3)
    pl.semaphore_wait(free.at[3], 3)
    for s in (2, 1, 3, 0):
        rows = chip_rows(s)
        back = nt(d_projected[rows, pl.ds(0, 256)], wq[...])
        back = back + nn(d_projected[rows, pl.ds(256, 128)], wkv[...])
        blocks[s] = back.astype(BF16)
        last_sum.pair(s)
        if s == 1:
            last_sum.far()
    last_sum.near()
    layer_spread = spread(0, layer_out)
    layer_spread.start()
    normed_again.wait()

    def project_grad(j, carry):
        lanes = ds(j * 512, 512)
        values = wide[:, lanes]
        wq[lanes, :] = tn(values, d_projected[:, pl.ds(0, 256)]).astype(BF16)
        wkv[:, lanes] = tn(d_projected[:, pl.ds(256, 128)], values).astype(BF16)
        return carry

    lax.fori_loop(0, 4, project_grad, 0)
    q_sum.start()
    g_sum.last()
    o_sum.middle()
    u_sum.last()
    kv_sum.start()
    last_sum.relay()
    q_sum.middle()
    kv_sum.middle()
    o_sum.last()
    layer_spread.end()
    last_sum.arrive()
    kv_sum.last()
    gain_one = gain_row(gains, 0)

    def input_rows(t, carry):
        rows = ds(t * 16, 16)
        values = x_mine[rows, :].astype(F32)
        back = norm_back(last_sum.total(t * 16, 16), values, gain_one, 0)
        low_rows[rows, :] = (d_residual[rows, :] + back).astype(BF16)
        return carry

    lax.fori_loop(0, TOK // 16, input_rows, 0)
    input_spread = spread(1, input_out)
    input_spread.start()
    col_copies = []
    for k in range(7):
        target = lax.rem(here.c + k + 1, 8)
        col_copies.append(
            remote(
                gain_sums.at[:, ds(target * FEAT, FEAT)],
                gain_cols.at[here.c],
                gain_send.at[k],
                gain_recv.at[k],
                col_peers[k],
            )
        )
        col_copies[k].start()
    gain_cols[here.c] = gain_sums[:, ds(here.c * FEAT, FEAT)]
    for copy in col_copies:
        copy.wait()
    total = gain_cols[0]
    for c in range(1, 8):
        total = total + gain_cols[c]
    gain_rows[here.r] = total
    row_copies = [
        remote(
            gain_rows.at[here.r], gain_rows.at[here.r], last_send.at[k], last_recv.at[k], row_peers[k]
        )
        for k in range(7)
    ]
    for copy in row_copies:
        copy.start()
    q_sum.last()
    kv_sum.end()
    kv_total[...] = kv_sum.own[...].astype(F32) + kv_far[...].astype(F32)
    kv_swaps = []
    for index in range(2):
        theirs = ds(index * HD + (1 - here.k) * (HD // 2), HD // 2)
        land = kv_land.at[pl.ds(index * (HD // 2), HD // 2)]
        kv_swaps.append(
            remote(
                kv_total.at[theirs], land, last_send.at[7 + index], last_recv.at[7 + index], here.partner
            )
        )
        kv_swaps[index].start()
    keep(d_sum.own, gd_own)
    keep(g_sum.own, gg_own)
    keep(u_sum.own, gu_own)
    keep(o_sum.own, go_own)
    keep(q_sum.own, gq_own)
    for index in range(2):
        kv_swaps[index].wait()
        mine = kv_total[ds(index * HD + here.k * (HD // 2), HD // 2), :]
        there = pl.ds(index * (HD // 2), HD // 2)
        kv_final[there, :] = mine + kv_land[there, :]
    keep(kv_final, kv_out)
    for sums in (d_sum, g_sum, u_sum, o_sum, q_sum):
        sums.end()
    for copy in row_copies:
        copy.wait()
    total = gain_rows[0]
    for r in range(1, 8):
        total = total + gain_rows[r]
    gain_cols[0] = total
    twin_copy = remote(gain_cols.at[0], gain_far, gain_send.at[7], gain_recv.at[7], here.twin)
    twin_copy.start()
    twin_copy.wait()
    gain_cols[0] = total + gain_far[...]
    keep(gain_cols.at[0], gains_out)
    input_spread.end()
    last_sum.sent()
    x_collect.sent()
    g_collect.sent()
    for copy in kept:
        if copy is not normed_copy:
            copy.wait()


def layer_call(*args):
    ff = args[6].shape[0]
    any_space = pl.BlockSpec(memory_space=pl.ANY)
    vmem_space = pl.BlockSpec(memory_space=pltpu.VMEM)
    dma = pltpu.SemaphoreType.DMA

    def low(*shape):
        return jax.ShapeDtypeStruct(shape, BF16)

    outs = (
        low(LEN, FEAT),
        low(LEN, FEAT),
        low(ff, FEAT),
        low(ff, FEAT),
        low(ff // 2, FEAT),
        low(ff // 2, FEAT),
        low(ff, FEAT),
        low(ff, FEAT),
        low(256, FEAT),
        low(256, FEAT),
        low(FEAT, 256),
        low(FEAT, 256),
        jax.ShapeDtypeStruct((HD, FEAT), F32),
        jax.ShapeDtypeStruct((8, FEAT), F32),
        low(LEN, D),
        low(8, TOK, FEAT),
    )

    def vmem(*shape, dtype=BF16):
        return pltpu.VMEM(shape, dtype)

    scratch = [
        vmem(8, TOK, FEAT),
        vmem(TOK, D),
        vmem(TOK, D),
        vmem(LEN, D),
        vmem(LEN, D),
        vmem(LEN, ff),
        vmem(LEN, ff),
        vmem(LEN, ff),
        vmem(ff, D),
        vmem(ff, D),
        vmem(ff, D),
        vmem(ff, D),
        vmem(256, D),
        vmem(D, 256),
        vmem(128, D),
        vmem(128, FEAT),
        vmem(128, FEAT),
        vmem(128, FEAT, dtype=F32),
        vmem(HD, FEAT, dtype=F32),
        vmem(HD, FEAT, dtype=F32),
        vmem(8, FEAT, dtype=F32),
        vmem(64, 256, dtype=F32),
        vmem(LEN, 128, dtype=F32),
        vmem(LEN, 128, dtype=F32),
        vmem(LEN, 128, dtype=F32),
        vmem(LEN, 256),
        vmem(LEN, 128),
        vmem(LEN, 128),
        vmem(LEN, 128),
        vmem(LEN, 128),
        vmem(LEN, 256),
        vmem(LEN, 128, dtype=F32),
        vmem(LEN, 256),
        vmem(LEN, 384),
        vmem(LEN, 128, dtype=F32),
        vmem(LEN, 128, dtype=F32),
        vmem(LEN, 128, dtype=F32),
        vmem(LEN, 128, dtype=F32),
        vmem(4, 256, D),
        vmem(4, TOK, D),
        vmem(2, TOK // 2, D),
        vmem(2, TOK, D),
        vmem(TOK, D, dtype=F32),
        vmem(TOK, D, dtype=F32),
        vmem(8, D, dtype=F32),
        vmem(8, 8, FEAT, dtype=F32),
        vmem(8, FEAT, dtype=F32),
        vmem(8, 8, FEAT, dtype=F32),
        vmem(ff, FEAT),
        vmem(3, ff, 2 * FEAT),
        vmem(8, ff // 2, FEAT),
        vmem(3, 2, ff // 2, FEAT),
        vmem(ff // 2, FEAT),
        vmem(4, ff, FEAT),
        vmem(3, ff, FEAT),
        vmem(4, 256, FEAT),
        vmem(3, 256, FEAT),
        vmem(4, FEAT, 256),
        vmem(3, FEAT, 256),
        vmem(128, FEAT),
        vmem(3, 128, 2 * FEAT),
        dma((2, 16)),
        dma((2, 16)),
        dma((2, 2)),
        dma((4, RowGather.SEMS)),
        dma((4, RowGather.SEMS)),
        dma((5,)),
        dma((7, SplitGather.SEMS)),
        dma((7, SplitGather.SEMS)),
        dma((7,)),
        dma((4, RowSum.SEMS)),
        dma((4, RowSum.SEMS)),
        dma((6, SplitSum.SEMS)),
        dma((6, SplitSum.SEMS)),
        dma((2, 8)),
        dma((2, 8)),
        dma((2,)),
        dma((11,)),
        dma((11,)),
        dma((8,)),
        dma((8,)),
        dma((8,)),
        pltpu.SemaphoreType.REGULAR((4,)),
    ]
    return pl.pallas_call(
        layer_kernel,
        out_shape=outs,
        in_specs=[any_space] * 9 + [vmem_space] * 3,
        out_specs=tuple(any_space for _ in outs),
        scratch_shapes=scratch,
        compiler_params=pltpu.CompilerParams(
            collective_id=0, has_side_effects=True, vmem_limit_bytes=VMEM_BYTES
        ),
        cost_estimate=pl.CostEstimate(flops=36 * 10**9, bytes_accessed=60 * 10**6, transcendentals=0),
        name="decoder_layer",
    )(*args)


def finish_kernel(
    layer,
    inner,
    d_own,
    d_far,
    g_own,
    g_far,
    u_own,
    u_far,
    o_own,
    o_far,
    q_own,
    q_far,
    kv,
    gains,
    layer_output,
    grad_input,
    grad_down,
    grad_gate,
    grad_up,
    grad_out,
    grad_query,
    grad_key,
    grad_value,
    grad_attn_gain,
    grad_mlp_gain,
):
    layer_output[...] = layer[...]
    grad_input[...] = inner[...].astype(F32)
    for total, own, far in (
        (grad_down, d_own, d_far),
        (grad_up, u_own, u_far),
        (grad_out, o_own, o_far),
        (grad_query, q_own, q_far),
    ):
        total[...] = own[...].astype(F32) + far[...].astype(F32)
    half = lax.rem(lax.axis_index("dp") + lax.axis_index("col"), 2)
    mine = pl.program_id(0) == half

    @pl.when(mine)
    def _():
        grad_gate[...] = g_own[...].astype(F32)

    @pl.when(jnp.logical_not(mine))
    def _():
        grad_gate[...] = g_far[...].astype(F32)

    width = grad_key.shape[0]
    grad_key[...] = kv[pl.ds(0, width), :]
    grad_value[...] = kv[pl.ds(width, width), :]
    grad_attn_gain[...] = gains[pl.ds(0, 1), :]
    grad_mlp_gain[...] = gains[pl.ds(1, 1), :]


def finish_call(*args):
    steps = 2
    ff = args[2].shape[0]

    def block(rows, index=lambda i: (i, 0)):
        return pl.BlockSpec((rows, FEAT), index)

    tall, wide, square = block(LEN // steps), block(ff // steps), block(256 // steps)
    halves = block(ff // steps, lambda i: (0, 0))
    whole = block(HD, lambda i: (0, 0))
    kept = block(HD // 2, lambda i: (0, 0))
    gain_block, row = block(8, lambda i: (0, 0)), block(1, lambda i: (0, 0))

    def full(rows, dtype=F32):
        return jax.ShapeDtypeStruct((rows, FEAT), dtype)

    return pl.pallas_call(
        finish_kernel,
        grid=(steps,),
        out_shape=(
            full(LEN, BF16),
            full(LEN),
            full(ff),
            full(ff),
            full(ff),
            full(256),
            full(256),
            full(HD // 2),
            full(HD // 2),
            full(1),
            full(1),
        ),
        in_specs=[tall, tall, wide, wide, halves, halves, wide, wide] + [square] * 4 + [whole, gain_block],
        out_specs=(tall, tall, wide, wide, wide, square, square, kept, kept, row, row),
        name="finish_outputs",
    )(*args)


def body(
    hidden_in,
    segment_ids,
    attn_gain,
    w_query,
    w_key,
    w_value,
    w_out,
    mlp_gain,
    w_gate,
    w_up,
    w_down,
    grad_output,
):
    (
        layer_output,
        grad_input,
        gd_own,
        gd_far,
        gg_own,
        gg_far,
        gu_own,
        gu_far,
        go_own,
        go_far,
        gq_own,
        gq_far,
        grad_kv,
        d_gains,
        _,
        _,
    ) = layer_call(
        hidden_in,
        grad_output,
        w_query,
        w_key.T,
        w_value.T,
        w_out,
        w_gate.T,
        w_up.T,
        w_down,
        attn_gain[None],
        mlp_gain[None],
        segment_ids,
    )

    (
        layer_output,
        grad_input,
        grad_down,
        grad_gate,
        grad_up,
        grad_out_proj,
        grad_query,
        grad_key,
        grad_value,
        grad_attn_gain,
        grad_mlp_gain,
    ) = finish_call(
        layer_output,
        grad_input,
        gd_own,
        gd_far,
        gg_own,
        gg_far,
        gu_own,
        gu_far,
        go_own,
        go_far,
        gq_own,
        gq_far,
        grad_kv,
        d_gains,
    )
    return (
        layer_output,
        grad_input,
        grad_attn_gain[0],
        grad_query,
        grad_key.T,
        grad_value.T,
        grad_out_proj,
        grad_mlp_gain[0],
        grad_gate.T,
        grad_up.T,
        grad_down,
    )


def solution(mesh):
    return jax.shard_map(
        body,
        mesh=mesh,
        in_specs=(
            P(("dp", "row"), "col"),
            P(("dp", "col"), None),
            P("col"),
            P("col", "row"),
            P("col", "row"),
            P("col", "row"),
            P("row", "col"),
            P("col"),
            P("col", "row"),
            P("col", "row"),
            P("row", "col"),
            P(("dp", "row"), "col"),
        ),
        out_specs=(
            P(("dp", "row"), "col"),
            P(("dp", "row"), "col"),
            P("col"),
            P("col", "row"),
            P("col", "row"),
            P("col", "row"),
            P("row", "col"),
            P("col"),
            P("col", "row"),
            P("col", "row"),
            P("row", "col"),
        ),
        check_vma=False,
    )
```

```python
import functools
import math

import jax
import jax.numpy as jnp
from jax import lax
from jax.experimental import pallas as pl
from jax.experimental.pallas import tpu as pltpu
from jax.sharding import PartitionSpec as P

D = 2048
HD = 64
LEN = 1024
ROWS = 8
CHIPS = 4
TOK = LEN // ROWS
FEAT = D // 8
EPSILON = 1e-05
FLOOR_SCORE = -1e30
BF16 = jnp.bfloat16
F32 = jnp.float32
MESH = pl.DeviceIdType.MESH
VMEM_BYTES = 62 * 2**20


def remote(src, dst, send, recv, device):
    return pltpu.make_async_remote_copy(
        src_ref=src, dst_ref=dst, send_sem=send, recv_sem=recv, device_id=device, device_id_type=MESH
    )


def meet(peers):
    barrier = pltpu.get_barrier_semaphore()
    for peer in peers:
        pl.semaphore_signal(barrier, inc=1, device_id=peer, device_id_type=MESH)
    pl.semaphore_wait(barrier, len(peers))


def ds(start, size):
    return pl.ds(pl.multiple_of(start, size), size)


class Place:
    def __init__(self):
        self.d = lax.axis_index("dp")
        self.r = lax.axis_index("row")
        self.c = lax.axis_index("col")
        self.y, self.k = self.r // 2, lax.rem(self.r, 2)
        self.x, self.h = self.c // 2, lax.rem(self.c, 2)
        self.partner = {"row": self.y * 2 + 1 - self.k}
        self.up = {"row": self.row_of(1)}
        self.down = {"row": self.row_of(3)}
        self.other = {"dp": 1 - self.d, "col": self.x * 2 + 1 - self.h}
        self.twin = {"dp": 1 - self.d}
        self.half = lax.rem(self.d + self.h, 2)
        self.x_peers = [{"col": self.col_of(s)} for s in (1, 3, 2)]

    def row_of(self, step):
        return lax.rem(self.y + step, CHIPS) * 2 + self.k

    def col_of(self, step):
        return lax.rem(self.x + step, 4) * 2 + self.h

    def col_from(self, step):
        return lax.rem(self.x + 4 - step, 4) * 2 + self.h


class RowGather:
    SEMS = 13

    def __init__(self, here, place, shard, send, recv):
        self.here, self.place = here, place
        y, k = here.y, here.k
        self.low, self.high, self.far_row = here.row_of(3), here.row_of(1), here.row_of(2)
        self.ups = [
            remote(shard(a), place(here.r, a), send.at[a], recv.at[a], here.up) for a in (0, 1)
        ]
        self.downs = [
            remote(shard(a), place(here.r, a), send.at[2 + a], recv.at[2 + a], here.down)
            for a in (0, 1)
        ]
        self.fars = [
            self.hand_on(self.low, 0, send.at[4], recv.at[4], here.up),
            self.hand_on(self.high, 1, send.at[5], recv.at[5], here.down),
        ]
        self.passes = {}
        for index, (row, a) in enumerate(
            [(self.low, 0), (self.low, 1), (self.high, 0), (self.high, 1), (self.far_row, 0), (self.far_row, 1)]
        ):
            self.passes[index] = self.hand_on(
                row, a, send.at[6 + index], recv.at[6 + index], here.partner
            )
        self.own = [
            remote(shard(None), place(here.r, None), send.at[12], recv.at[12], here.partner)
        ]

    def hand_on(self, row, a, send, recv, device):
        return remote(self.place(row, a), self.place(row, a), send, recv, device)

    def start(self):
        for a, b in ((0, 1), (1, 0)):
            self.ups[a].start()
            self.downs[b].start()
        self.own[0].start()

    def near(self):
        for a, b in ((0, 1), (1, 0)):
            self.ups[a].wait_recv()
            if a == 0:
                self.fars[0].start()
            self.passes[a].start()
            self.downs[b].wait_recv()
            if b == 1:
                self.fars[1].start()
            self.passes[2 + b].start()

    def far(self):
        for a in (0, 1):
            self.fars[a].wait_recv()
            self.passes[4 + a].start()

    def got_own(self):
        self.own[0].wait_recv()

    def got_near(self):
        for index in range(4):
            self.passes[index].wait_recv()

    def got_far(self):
        for index in (4, 5):
            self.passes[index].wait_recv()

    def sent(self):
        for copy in self.ups + self.downs + self.fars + self.own + list(self.passes.values()):
            copy.wait_send()


class ColGather:
    SEMS = 7

    def __init__(self, here, shard, place, send, recv, local, across_first):
        self.here, self.place, self.across_first = here, place, across_first
        self.local = pltpu.make_async_copy(shard, place(here.c), local)
        self.lines = [
            remote(shard, place(here.c), send.at[i], recv.at[i], here.x_peers[i]) for i in range(3)
        ]
        self.across = [remote(shard, place(here.c), send.at[3], recv.at[3], here.other)]
        there = here.x * 2 + 1 - here.h
        if across_first:
            self.seconds = [
                remote(place(there), place(there), send.at[4 + i], recv.at[4 + i], here.x_peers[i])
                for i in range(3)
            ]
        else:
            self.seconds = []
            for i, step in enumerate((1, 3, 2)):
                source = here.col_from(step)
                self.seconds.append(
                    remote(place(source), place(source), send.at[4 + i], recv.at[4 + i], here.other)
                )

    def start(self):
        self.start_across()
        self.start_lines()

    def start_across(self):
        self.local.start()
        self.across[0].start()

    def start_lines(self):
        for copy in self.lines:
            copy.start()

    def middle(self):
        if self.across_first:
            self.across[0].wait_recv()
            for copy in self.seconds:
                copy.start()
        else:
            for copy, second in zip(self.lines, self.seconds):
                copy.wait_recv()
                second.start()

    def end(self):
        self.local.wait()
        if self.across_first:
            for copy in self.lines:
                copy.wait_recv()
        else:
            self.across[0].wait_recv()
        for copy in self.seconds:
            copy.wait_recv()
        for copy in self.lines + self.across + self.seconds:
            copy.wait_send()


class SplitGather:
    SEMS = 14

    def __init__(self, here, shard, place, send, recv, local):
        self.here, self.place = here, place
        half = here.half
        self.local = pltpu.make_async_copy(shard(None), place(here.c, None), local)

        def hand_on(c, index, device):
            return remote(place(c, half), place(c, half), send.at[index], recv.at[index], device)

        own = place(here.c, half)
        self.across = remote(shard(half), own, send.at[0], recv.at[0], here.other)
        self.lines = [
            remote(shard(half), own, send.at[1 + i], recv.at[1 + i], here.x_peers[i]) for i in range(3)
        ]
        there = here.x * 2 + 1 - here.h
        self.seconds = [hand_on(there, 4 + i, here.x_peers[i]) for i in range(3)]
        sources = [here.col_from(step) for step in (1, 3, 2)]
        others = [source + 1 - 2 * here.h for source in sources]
        self.swaps = [
            hand_on(c, 7 + i, here.twin) for i, c in enumerate([there] + sources + others)
        ]

    def start_across(self):
        self.local.start()
        self.across.start()

    def start_lines(self):
        for copy in self.lines:
            copy.start()

    def middle(self):
        self.across.wait_recv()
        for copy in self.seconds:
            copy.start()
        self.swaps[0].start()

    def late(self, which):
        copies = self.seconds if which else self.lines
        for copy, swap in zip(copies, self.swaps[1 + 3 * which :]):
            copy.wait_recv()
            swap.start()

    def end(self):
        self.local.wait()
        for swap in self.swaps:
            swap.wait_recv()
        for copy in [self.across] + self.lines + self.seconds + self.swaps:
            copy.wait_send()


class RowSum:
    SEMS = 10

    def __init__(self, here, blocks, paired, relayed, landed, send, recv):
        self.here, self.blocks, self.paired = here, blocks, paired
        self.relayed, self.landed = relayed, landed
        k, half = here.k, TOK // 2
        self.mine, self.half = k * TOK, half
        self.pairs = [
            remote(
                blocks.at[s, ds((1 - k) * TOK, TOK)], paired.at[s], send.at[s], recv.at[s], here.partner
            )
            for s in range(4)
        ]
        self.fars = [
            remote(self.part(2, 0), relayed.at[0], send.at[4], recv.at[4], here.up),
            remote(self.part(2, 1), relayed.at[1], send.at[5], recv.at[5], here.down),
        ]
        self.nears = {}
        for index, (s, a, device) in enumerate(
            [(1, 1, here.up), (3, 0, here.down), (1, 0, here.up), (3, 1, here.down)]
        ):
            slot = 0 if s == 1 else 1
            self.nears[s, a] = remote(
                self.part(s, a),
                landed.at[slot, pl.ds(a * half, half)],
                send.at[6 + index],
                recv.at[6 + index],
                device,
            )

    def part(self, s, a):
        return self.blocks.at[s, ds(self.mine + a * self.half, self.half)]

    def add(self, s, a, other):
        part = self.part(s, a)
        part[...] = (part[...].astype(F32) + other[...].astype(F32)).astype(BF16)

    def pair(self, s):
        self.pairs[s].start()

    def join(self, s):
        self.pairs[s].wait_recv()
        for a in (0, 1):
            self.add(s, a, self.paired.at[s, pl.ds(a * self.half, self.half)])

    def far(self):
        self.join(2)
        self.fars[0].start()
        self.fars[1].start()

    def near(self):
        self.join(1)
        self.nears[1, 1].start()
        self.join(3)
        self.nears[3, 0].start()

    def relay(self):
        self.fars[0].wait_recv()
        self.add(1, 0, self.relayed.at[0])
        self.nears[1, 0].start()
        self.fars[1].wait_recv()
        self.add(3, 1, self.relayed.at[1])
        self.nears[3, 1].start()

    def arrive(self):
        self.pairs[0].wait_recv()
        for copy in self.nears.values():
            copy.wait_recv()

    def total(self, start, rows):
        own = self.blocks[0, pl.ds(pl.multiple_of(self.mine + start, rows), rows)].astype(F32)
        here = pl.ds(pl.multiple_of(start, rows), rows)
        return (
            own
            + self.paired[0, here].astype(F32)
            + self.landed[0, here].astype(F32)
            + self.landed[1, here].astype(F32)
        )

    def sent(self):
        for copy in self.pairs + self.fars + list(self.nears.values()):
            copy.wait_send()


def add_rows(rows, target, others):
    kind = target.dtype

    def step(t, carry):
        at = ds(t * rows, rows)
        total = target[at, :].astype(F32)
        for other in others:
            total = total + other[at, :].astype(F32)
        target[at, :] = total.astype(kind)
        return carry

    lax.fori_loop(0, target.shape[0] // rows, step, 0)


class WeightSum:
    SEMS = 8

    def __init__(self, here, part, wide_part, rows, z_land, x_land, far_part, send, recv, across_first):
        self.here, self.part, self.across_first, self.rows = here, part, across_first, rows
        self.z_land, self.x_land = z_land, x_land
        self.own = part(here.c)
        steps = (1, 3, 2)
        if across_first:
            self.mine = [part(x * 2 + here.h) for x in range(4)]
            self.across = [
                remote(part(x * 2 + 1 - here.h), z_land.at[x], send.at[x], recv.at[x], here.other)
                for x in range(4)
            ]
            self.lines = [
                remote(
                    part(here.col_of(step)), x_land.at[i], send.at[4 + i], recv.at[4 + i], here.x_peers[i]
                )
                for i, step in enumerate(steps)
            ]
        else:
            self.wide = wide_part(here.x)
            self.across = [
                remote(
                    part(here.x * 2 + 1 - here.h), z_land, send.at[3], recv.at[3], here.other
                )
            ]
            self.lines = [
                remote(
                    wide_part(lax.rem(here.x + step, 4)),
                    x_land.at[i],
                    send.at[i],
                    recv.at[i],
                    here.x_peers[i],
                )
                for i, step in enumerate(steps)
            ]
        self.swap = remote(self.own, far_part, send.at[7], recv.at[7], here.twin)

    def add(self, target, others):
        add_rows(self.rows, target, others)

    def start(self):
        for copy in self.across if self.across_first else self.lines:
            copy.start()

    def middle(self):
        if self.across_first:
            for x in range(4):
                self.across[x].wait_recv()
                self.add(self.mine[x], [self.z_land.at[x]])
            for copy in self.lines:
                copy.start()
        else:
            for copy in self.lines:
                copy.wait_recv()
            self.add(self.wide, [self.x_land.at[i] for i in range(3)])
            self.across[0].start()

    def last(self):
        if self.across_first:
            for copy in self.lines:
                copy.wait_recv()
            self.add(self.own, [self.x_land.at[i] for i in range(3)])
        else:
            self.across[0].wait_recv()
            self.add(self.own, [self.z_land])
        self.swap.start()

    def end(self):
        self.swap.wait()
        for copy in self.across + self.lines:
            copy.wait_send()


class SplitSum:
    SEMS = 16

    def __init__(self, here, part, rows, twin_land, x_land, z_land, far_part, send, recv):
        self.here, self.rows = here, rows
        self.twin_land, self.x_land, self.z_land = twin_land, x_land, z_land
        half, x, h = here.half, here.x, here.h
        self.mine = [part(c, half) for c in range(8)]
        self.twins = [
            remote(part(c, 1 - half), twin_land.at[c], send.at[c], recv.at[c], here.twin)
            for c in range(8)
        ]
        self.lines = []
        for i, step in enumerate((1, 3, 2)):
            target = lax.rem(x + step, 4) * 2
            for side in range(2):
                index = 8 + 2 * i + side
                self.lines.append(
                    remote(
                        part(target + side, half),
                        x_land.at[i, side],
                        send.at[index],
                        recv.at[index],
                        here.x_peers[i],
                    )
                )
        self.sides = [part(x * 2 + side, half) for side in range(2)]
        self.across = remote(part(x * 2 + 1 - h, half), z_land, send.at[14], recv.at[14], here.other)
        self.own = part(here.c, half)
        self.swap = remote(self.own, far_part, send.at[15], recv.at[15], here.twin)

    def add(self, target, others):
        add_rows(self.rows, target, others)

    def start(self):
        for copy in self.twins:
            copy.start()

    def middle(self):
        for c in range(8):
            self.twins[c].wait_recv()
            self.add(self.mine[c], [self.twin_land.at[c]])
        for copy in self.lines:
            copy.start()

    def late(self):
        for copy in self.lines:
            copy.wait_recv()
        for side in range(2):
            self.add(self.sides[side], [self.x_land.at[i, side] for i in range(3)])
        self.across.start()

    def last(self):
        self.across.wait_recv()
        self.add(self.own, [self.z_land])
        self.swap.start()

    def end(self):
        self.swap.wait()
        for copy in self.twins + self.lines + [self.across]:
            copy.wait_send()


class Spread:
    def __init__(self, here, source, target, send, recv, local, first, rows):
        self.here = here
        self.same = here.r == here.c
        self.copies = []
        place = target.at[ds(here.r * TOK + first, rows)]
        part = source.at[pl.ds(first, rows)]
        for j in range(8):
            shard = part.at[:, pl.ds(j * FEAT, FEAT)]
            self.copies.append(
                (
                    remote(shard, place, send.at[j], recv.at[here.r], {"row": here.c, "col": j}),
                    pltpu.make_async_copy(shard, place, local),
                )
            )
        self.arrivals = [
            remote(
                part.at[:, pl.ds(0, FEAT)],
                target.at[pl.ds(i * TOK + first, rows)],
                send.at[i],
                recv.at[i],
                {"row": here.c, "col": i},
            )
            for i in range(8)
        ]

    def each(self, index, other, own):
        itself = self.same & (self.here.r == index)
        pl.when(itself)(own)
        pl.when(jnp.logical_not(itself))(other)

    def start(self):
        for j, (copy, local) in enumerate(self.copies):
            self.each(j, copy.start, local.start)

    def end(self):
        for j, (copy, local) in enumerate(self.copies):
            self.each(j, copy.wait_send, local.wait)
        for i, copy in enumerate(self.arrivals):
            self.each(i, copy.wait_recv, lambda: None)


class Collect:
    def __init__(self, here, source, middle, target, send, recv, local):
        self.here = here
        r, c = here.r, here.c
        self.local = pltpu.make_async_copy(source.at[ds(r * TOK, TOK)], middle.at[r], local.at[0])
        self.firsts = []
        self.seconds = []
        lanes = target.at[:, ds(c * FEAT, FEAT)]
        for k in range(1, 8):
            i = lax.rem(r + k, 8)
            self.firsts.append(
                remote(
                    source.at[ds(i * TOK, TOK)], middle.at[r], send.at[k], recv.at[k], {"row": i}
                )
            )
        for k in range(8):
            a = lax.rem(r + 8 - k, 8)
            self.seconds.append(
                (
                    a == c,
                    remote(middle.at[a], lanes, send.at[8 + k], recv.at[8 + c], {"col": a}),
                    pltpu.make_async_copy(middle.at[a], lanes, local.at[1]),
                )
            )
        self.arrivals = [
            (
                c == j,
                remote(
                    middle.at[0],
                    target.at[:, pl.ds(j * FEAT, FEAT)],
                    send.at[8 + j],
                    recv.at[8 + j],
                    {"col": j},
                ),
            )
            for j in range(8)
        ]

    def start(self):
        self.local.start()
        for copy in self.firsts:
            copy.start()

    def turn(self):
        self.local.wait()
        for k, (itself, copy, local) in enumerate(self.seconds):
            if k > 0:
                self.firsts[k - 1].wait_recv()
            pl.when(itself)(local.start)
            pl.when(jnp.logical_not(itself))(copy.start)

    def arrive(self):
        for itself, copy, local in self.seconds:
            pl.when(itself)(local.wait)
        for itself, copy in self.arrivals:
            pl.when(jnp.logical_not(itself))(copy.wait_recv)

    def sent(self):
        for copy in self.firsts:
            copy.wait_send()
        for itself, copy, local in self.seconds:
            pl.when(jnp.logical_not(itself))(copy.wait_send)


def nn(a, b):
    return jnp.dot(a, b, preferred_element_type=F32)


def nt(a, b):
    return lax.dot_general(a, b, (((1,), (1,)), ((), ())), preferred_element_type=F32)


def tn(a, b):
    return lax.dot_general(a, b, (((0,), (0,)), ((), ())), preferred_element_type=F32)


def swap_halves(values):
    width = values.shape[-1]
    lane = lax.broadcasted_iota(jnp.int32, values.shape, 1)
    return jnp.where(
        lax.rem(lane, HD) < HD // 2, pltpu.roll(values, width - HD // 2, 1), pltpu.roll(values, HD // 2, 1)
    )


def turn(values, cos, sin):
    return values * cos + swap_halves(values) * sin


def gain_row(gains, which):
    return jnp.concatenate([gains[pl.ds(8 * j + which, 1), :] for j in range(8)], axis=1)


def layer_kernel(
    x_in,
    g_in,
    wq_in,
    wk_in,
    wv_in,
    wo_in,
    wg_in,
    wu_in,
    wd_in,
    attn_in,
    mlp_in,
    seg_in,
    layer_out,
    input_out,
    gd_own,
    gd_far,
    gg_own,
    gg_far,
    gu_own,
    gu_far,
    go_own,
    go_far,
    gq_own,
    gq_far,
    kv_out,
    gains_out,
    normed_kept,
    g_middle,
    x_middle,
    x_mine,
    low_rows,
    wide,
    g_all,
    act,
    gate,
    up,
    wd,
    gd,
    wg,
    wu,
    wo,
    wq,
    wkv,
    kv_shard,
    kv_far,
    kv_total,
    kv_land,
    kv_final,
    gain_shard,
    gains,
    cos,
    sin,
    seg_col,
    query,
    k_low,
    k_high,
    v_low,
    v_high,
    mixed,
    totals,
    d_mixed,
    d_projected,
    dk_low,
    dk_high,
    dv_low,
    dv_high,
    blocks,
    paired,
    relayed,
    landed,
    residual,
    d_residual,
    gain_sums,
    gain_cols,
    gain_far,
    gain_rows,
    gd_z,
    gd_x,
    gg_twin,
    gg_x,
    gg_z,
    gu_z,
    gu_x,
    go_z,
    go_x,
    gq_z,
    gq_x,
    kv_z,
    kv_x,
    collect_send,
    collect_recv,
    collect_local,
    gather_send,
    gather_recv,
    gather_local,
    w_send,
    w_recv,
    w_local,
    rows_send,
    rows_recv,
    sum_send,
    sum_recv,
    spread_send,
    spread_recv,
    spread_local,
    last_send,
    last_recv,
    gain_send,
    gain_recv,
    keep_sem,
    free,
):
    here = Place()
    same = here.r == here.c
    barrier = pltpu.get_barrier_semaphore()
    row_peers = [{"row": lax.rem(here.r + k, ROWS)} for k in range(1, ROWS)]
    col_peers = [{"col": lax.rem(here.c + k, 8)} for k in range(1, 8)]
    peers = row_peers + col_peers + [here.other, here.twin]
    for peer in peers:
        pl.semaphore_signal(barrier, inc=1, device_id=peer, device_id_type=MESH)
    for i in range(8):

        @pl.when(jnp.logical_not(same & (here.r == i)))
        def _():
            pl.semaphore_signal(
                barrier, inc=1, device_id={"row": i, "col": here.r}, device_id_type=MESH
            )

    pl.semaphore_wait(barrier, len(peers) + 8 - same.astype(jnp.int32))

    def token_place(ref):
        def place(row, a):
            if a is None:
                return ref.at[ds(row * TOK, TOK)]
            return ref.at[ds(row * TOK + a * (TOK // 2), TOK // 2)]

        return place

    def own_part(ref):
        place = token_place(ref)
        return lambda a: place(here.r, a)

    def low_part(a):
        return low_rows if a is None else low_rows.at[pl.ds(a * (TOK // 2), TOK // 2)]

    def row_gather(index, ref, shard):
        return RowGather(here, token_place(ref), shard, gather_send.at[index], gather_recv.at[index])

    def row_sum(index):
        return RowSum(here, blocks, paired, relayed, landed, rows_send.at[index], rows_recv.at[index])

    def collect(index, source, middle, target):
        return Collect(
            here,
            source,
            middle,
            target,
            collect_send.at[index],
            collect_recv.at[index],
            collect_local.at[index],
        )

    def spread(index, target, first, rows):
        return Spread(
            here,
            low_rows,
            target,
            spread_send.at[index],
            spread_recv.at[index],
            spread_local.at[index],
            first,
            rows,
        )

    def col_gather(index, shard, place, across_first):
        return ColGather(
            here, shard, place, w_send.at[index], w_recv.at[index], w_local.at[index], across_first
        )

    def split_gather(index, shard, ref):
        half = ref.shape[0] // 2

        def place(c, a):
            lanes = ds(c * FEAT, FEAT)
            return ref.at[:, lanes] if a is None else ref.at[ds(a * half, half), lanes]

        def part(a):
            return shard if a is None else shard.at[ds(a * half, half)]

        return SplitGather(
            here, part, place, w_send.at[index], w_recv.at[index], w_local.at[index]
        )

    def weight_sum(index, parts, rows, z_land, x_land, far_part, across_first):
        return WeightSum(
            here,
            parts[0],
            parts[1],
            rows,
            z_land,
            x_land,
            far_part,
            sum_send.at[index],
            sum_recv.at[index],
            across_first,
        )

    def rows_of(ref):
        return lambda c: ref.at[ds(c * FEAT, FEAT)], lambda x: ref.at[ds(x * 2 * FEAT, 2 * FEAT)]

    def lanes_of(ref):
        return (
            lambda c: ref.at[:, ds(c * FEAT, FEAT)],
            lambda x: ref.at[:, ds(x * 2 * FEAT, 2 * FEAT)],
        )

    def credit(index):
        for peer in (here.partner, here.up, here.down):
            pl.semaphore_signal(free.at[index], inc=1, device_id=peer, device_id_type=MESH)

    def chip_rows(s):
        return ds(lax.rem(here.y + s, CHIPS) * 256, 256)

    kept = []

    def keep(src, dst):
        copy = pltpu.make_async_copy(src, dst, keep_sem.at[len(kept)])
        copy.start()
        kept.append(copy)
        return copy

    x_collect = collect(0, x_in, x_middle, x_mine)
    g_collect = collect(1, g_in, g_middle, low_rows)
    n1_gather = row_gather(0, wide, own_part(wide))
    g_gather = row_gather(1, g_all, low_part)
    n2_gather = row_gather(2, wide, own_part(wide))
    d_gather = row_gather(3, g_all, low_part)
    gain_gather = col_gather(0, gain_shard, lambda c: gains.at[ds(c * 8, 8)], True)
    wq_gather = col_gather(1, wq_in, lambda c: wq.at[ds(c * FEAT, FEAT)], False)
    kv_gather = col_gather(2, kv_shard, lambda c: wkv.at[:, ds(c * FEAT, FEAT)], False)
    wo_gather = col_gather(3, wo_in, lambda c: wo.at[:, ds(c * FEAT, FEAT)], False)
    wd_gather = col_gather(4, wd_in, lambda c: wd.at[:, ds(c * FEAT, FEAT)], False)
    wg_gather = split_gather(5, wg_in, wg)
    wu_gather = split_gather(6, wu_in, wu)
    d_sum = weight_sum(0, lanes_of(gd), 32, gd_z, gd_x, gd_far, False)
    u_sum = weight_sum(1, lanes_of(wu), 64, gu_z, gu_x, gu_far, True)
    o_sum = weight_sum(2, lanes_of(wo), 64, go_z, go_x, go_far, True)
    q_sum = weight_sum(3, rows_of(wq), 64, gq_z, gq_x, gq_far, True)
    kv_sum = weight_sum(4, lanes_of(wkv), 32, kv_z, kv_x, kv_far, False)
    g_half = wg.shape[0] // 2
    g_sum = SplitSum(
        here,
        lambda c, a: wg.at[ds(a * g_half, g_half), ds(c * FEAT, FEAT)],
        32,
        gg_twin,
        gg_x,
        gg_z,
        gg_far,
        sum_send.at[5],
        sum_recv.at[5],
    )
    kv_copies = []
    for index, part in enumerate((wk_in, wv_in)):
        rows = ds(index * HD + here.k * (HD // 2), HD // 2)
        local = pltpu.make_async_copy(part, kv_shard.at[rows], gather_local.at[3 + index])
        other = remote(
            part, kv_shard.at[rows], last_send.at[9 + index], last_recv.at[9 + index], here.partner
        )
        kv_copies += [local, other]

    for copy in kv_copies:
        copy.start()
    gain_shard[pl.ds(0, 4), :] = jnp.broadcast_to(attn_in[...], (4, FEAT))
    gain_shard[pl.ds(4, 4), :] = jnp.broadcast_to(mlp_in[...], (4, FEAT))
    gain_gather.start()
    wu_gather.start_across()
    x_collect.start()
    wq_gather.start_across()
    wg_gather.start_across()
    wq_gather.start_lines()
    segments = seg_in[0:1, :]
    places = lax.broadcasted_iota(jnp.int32, (1, LEN), 1)
    for number in range(3):
        count = jnp.sum((segments == number).astype(F32), axis=1, keepdims=True).astype(jnp.int32)
        places = places - jnp.where(segments > number, count, 0)
    tall = jnp.transpose(jnp.broadcast_to(places.astype(F32), (128, LEN)))
    lanes = lax.broadcasted_iota(jnp.int32, (1, 128), 1)
    step = (2 * lax.rem(lanes, HD // 2)).astype(F32)
    angles = tall * jnp.exp(step * (-math.log(10000.0) / HD))
    sign = jnp.where(lax.rem(lanes, HD) < HD // 2, -1.0, 1.0)
    cos[...] = jnp.cos(angles)
    sin[...] = jnp.sin(angles) * sign
    seg_col[...] = jnp.transpose(jnp.broadcast_to(segments.astype(F32), (128, LEN)))
    seg_row = segments.astype(F32)
    for copy in kv_copies:
        copy.wait()
    gain_gather.middle()
    kv_gather.start_across()
    kv_gather.start_lines()
    x_collect.turn()
    g_collect.start()
    wq_gather.middle()
    wo_gather.start()
    gain_gather.end()
    gain_one = gain_row(gains, 0)
    x_collect.arrive()

    def norm_rows(t, carry):
        values = x_mine[ds(t * 16, 16), :].astype(F32)
        scale = lax.rsqrt(jnp.sum(values * values, axis=1, keepdims=True) * (1.0 / D) + EPSILON)
        wide[ds(here.r * TOK + t * 16, 16), :] = (values * scale * gain_one).astype(BF16)
        return carry

    lax.fori_loop(0, TOK // 16, norm_rows, 0)
    wu_gather.start_lines()
    n1_gather.start()
    kv_gather.middle()
    wo_gather.middle()
    wu_gather.middle()
    lane = lax.broadcasted_iota(jnp.int32, (256, 128), 1)

    def project(s):
        rows = chip_rows(s)
        values = wide[rows, :]
        projected = nn(values, wq[...])
        cos_rows, sin_rows = cos[rows, :], sin[rows, :]
        for p in range(2):
            pair = turn(projected[:, p * 128 : (p + 1) * 128], cos_rows, sin_rows)
            query[rows, pl.ds(p * 128, 128)] = (pair * HD**-0.5).astype(BF16)
        key_value = nt(values, wkv[...])
        key = jnp.where(lane < HD, turn(key_value, cos_rows, sin_rows), 0.0)
        value = jnp.where(lane < HD, 0.0, key_value)
        k_low[rows, :] = key.astype(BF16)
        k_high[rows, :] = pltpu.roll(key, HD, 1).astype(BF16)
        v_high[rows, :] = value.astype(BF16)
        v_low[rows, :] = pltpu.roll(value, HD, 1).astype(BF16)

    n1_gather.near()
    g_collect.turn()
    wu_gather.late(0)
    wq_gather.end()
    kv_gather.end()
    n1_gather.got_own()
    project(0)
    n1_gather.got_near()
    project(1)
    n1_gather.far()
    project(3)
    n1_gather.got_far()
    project(2)
    normed_copy = keep(wide, normed_kept)
    g_collect.arrive()
    own_g = pltpu.make_async_copy(low_rows, token_place(g_all)(here.r, None), gather_local.at[0])
    own_g.start()
    g_gather.start()

    def bias_of(block, keys):
        first = block * 256
        row = lax.broadcasted_iota(jnp.int32, (256, keys), 0) + first
        key = lax.broadcasted_iota(jnp.int32, (256, keys), 1)
        alike = seg_col[pl.ds(first, 256), 0:1] == seg_row[:, :keys]
        return jnp.where(alike & (key <= row), 0.0, FLOOR_SCORE)

    def attend(block):
        keys = (block + 1) * 256
        rows, seen = pl.ds(block * 256, 256), pl.ds(0, keys)
        bias = bias_of(block, keys)

        def one_pair(p, sums):
            lanes = ds(p * 128, 128)
            pair = query[rows, lanes]
            out = jnp.zeros((256, 128), F32)
            for side, (key, value) in enumerate(((k_low, v_low), (k_high, v_high))):
                scores = nt(pair, key[seen, :]) + bias
                row_max = jnp.max(scores, axis=1, keepdims=True)
                exps = jnp.exp(scores - row_max)
                row_sum = jnp.sum(exps, axis=1, keepdims=True)
                out = out + nn(exps.astype(BF16), value[seen, :]) * (1.0 / row_sum)
                sums = jnp.where(lane == 2 * p + side, row_max + jnp.log(row_sum), sums)
            mixed[rows, lanes] = out.astype(BF16)
            return sums

        totals[rows, :] = lax.fori_loop(0, 2, one_pair, jnp.zeros((256, 128), F32))

    attend(0)
    wg_gather.start_lines()
    attend(1)
    wg_gather.middle()
    attend(2)
    attend(3)
    wu_gather.late(1)
    wo_gather.end()
    normed_copy.wait()
    n1_gather.sent()
    out_sum = row_sum(0)
    for s in (2, 1, 3, 0):
        blocks[s] = nn(mixed[chip_rows(s), :], wo[...]).astype(BF16)
        out_sum.pair(s)
        if s == 1:
            out_sum.far()
    out_sum.near()
    wg_gather.late(0)
    out_sum.relay()
    wd_gather.start()
    out_sum.arrive()
    wg_gather.late(1)
    gain_two = gain_row(gains, 4)

    def residual_rows(t, carry):
        rows = ds(t * 16, 16)
        values = x_mine[rows, :].astype(F32) + out_sum.total(t * 16, 16)
        residual[rows, :] = values
        scale = lax.rsqrt(jnp.sum(values * values, axis=1, keepdims=True) * (1.0 / D) + EPSILON)
        wide[ds(here.r * TOK + t * 16, 16), :] = (values * scale * gain_two).astype(BF16)
        return carry

    lax.fori_loop(0, TOK // 16, residual_rows, 0)
    n2_gather.start()
    wd_gather.middle()
    g_gather.near()
    credit(0)
    out_sum.sent()

    def feed(s):
        rows = chip_rows(s)
        values = wide[rows, :]
        gate_rows = nt(values, wg[...])
        up_rows = nt(values, wu[...])
        gate[rows, :] = gate_rows.astype(BF16)
        up[rows, :] = up_rows.astype(BF16)
        act[rows, :] = (gate_rows * (1.0 / (1.0 + jnp.exp(-gate_rows))) * up_rows).astype(BF16)

    n2_gather.near()
    wg_gather.end()
    wu_gather.end()
    n2_gather.got_own()
    feed(0)
    n2_gather.got_near()
    feed(1)
    g_gather.far()
    feed(3)
    n2_gather.far()
    n2_gather.got_far()
    feed(2)

    g_gather.got_own()
    g_gather.got_near()
    g_gather.got_far()
    own_g.wait()
    wd_gather.end()
    first_sum = row_sum(1)
    pl.semaphore_wait(free.at[0], 3)

    def down_grad(j, carry):
        lanes = ds(j * 512, 512)
        gd[:, lanes] = tn(act[...], g_all[:, lanes]).astype(BF16)
        return carry

    for s in (2, 1, 3, 0):
        rows = chip_rows(s)
        d_act = nt(g_all[rows, :], wd[...])
        gate_rows = gate[rows, :].astype(F32)
        up_rows = up[rows, :].astype(F32)
        sig = 1.0 / (1.0 + jnp.exp(-gate_rows))
        d_up = (d_act * (gate_rows * sig)).astype(BF16)
        d_gate = (d_act * up_rows * (sig * (1.0 + gate_rows * (1.0 - sig)))).astype(BF16)
        gate[rows, :] = d_gate
        up[rows, :] = d_up
        blocks[s] = (nn(d_gate, wg[...]) + nn(d_up, wu[...])).astype(BF16)
        first_sum.pair(s)
        if s == 1:
            first_sum.far()
    first_sum.near()
    lax.fori_loop(0, 4, down_grad, 0)
    d_sum.start()
    g_gather.sent()
    credit(1)
    first_sum.relay()
    n2_gather.sent()

    def gate_grad(j, carry):
        lanes = ds(j * 512, 512)
        wg[:, lanes] = tn(gate[...], wide[:, lanes]).astype(BF16)
        return carry

    lax.fori_loop(0, 4, gate_grad, 0)
    g_sum.start()

    first_sum.arrive()
    gain_sums[...] = jnp.zeros_like(gain_sums)

    def norm_back(total, values, gain, which):
        scale = lax.rsqrt(jnp.sum(values * values, axis=1, keepdims=True) * (1.0 / D) + EPSILON)
        scaled = total * gain
        inner = jnp.sum(scaled * values, axis=1, keepdims=True) * (1.0 / D)
        part = jnp.sum(total * values * scale, axis=0, keepdims=True)
        gain_sums[pl.ds(which, 1), :] = gain_sums[pl.ds(which, 1), :] + part
        return scale * scaled - values * (scale * scale * scale * inner)

    def residual_back_rows(t, carry):
        rows = ds(t * 16, 16)
        back = norm_back(first_sum.total(t * 16, 16), residual[rows, :], gain_two, 1)
        total = low_rows[rows, :].astype(F32) + back
        d_residual[rows, :] = total
        low_rows[rows, :] = total.astype(BF16)
        return carry

    lax.fori_loop(0, TOK // 16, residual_back_rows, 0)
    credit(2)
    pl.semaphore_wait(free.at[1], 3)
    own_rows = pltpu.make_async_copy(low_rows, token_place(g_all)(here.r, None), gather_local.at[2])
    own_rows.start()
    d_gather.start()
    first_sum.sent()
    layer_sum = row_sum(2)

    def up_grad(j, carry):
        lanes = ds(j * 512, 512)
        wu[:, lanes] = tn(up[...], wide[:, lanes]).astype(BF16)
        return carry

    lax.fori_loop(0, 4, up_grad, 0)
    u_sum.start()
    normed_again = pltpu.make_async_copy(normed_kept, wide, gather_local.at[1])
    normed_again.start()


    def down_block(s):
        blocks[s] = nn(act[chip_rows(s), :], wd[...]).astype(BF16)

    for s in (2, 1):
        down_block(s)
    d_gather.near()
    for s in (3, 0):
        down_block(s)
    pl.semaphore_wait(free.at[2], 3)
    for s in (2, 1, 3, 0):
        layer_sum.pair(s)
    d_gather.far()
    layer_sum.far()
    g_sum.middle()

    def mix_back(s):
        rows = chip_rows(s)
        d_mixed[rows, :] = nt(g_all[rows, :], wo[...]).astype(BF16)

    own_rows.wait()
    d_gather.got_own()
    mix_back(0)
    d_gather.got_near()
    mix_back(1)
    mix_back(3)
    d_gather.got_far()
    mix_back(2)
    d_sum.middle()

    def out_grad(j, carry):
        lanes = ds(j * 512, 512)
        wo[:, lanes] = tn(mixed[...], g_all[:, lanes]).astype(BF16)
        return carry

    lax.fori_loop(0, 4, out_grad, 0)
    layer_sum.near()
    for sums in (dk_low, dk_high, dv_low, dv_high):
        sums[...] = jnp.zeros_like(sums)

    def attend_back(block):
        keys = (block + 1) * 256
        rows, seen = pl.ds(block * 256, 256), pl.ds(0, keys)
        bias = bias_of(block, keys)
        cos_rows, sin_rows = cos[rows, :], sin[rows, :]

        def one_pair(p, carry):
            lanes = ds(p * 128, 128)
            pair = query[rows, lanes]
            grads = d_mixed[rows, lanes]
            product = grads.astype(F32) * mixed[rows, lanes].astype(F32)
            out = jnp.zeros((256, 128), F32)
            for side, (key, value, dk, dv) in enumerate(
                ((k_low, v_low, dk_low, dv_low), (k_high, v_high, dk_high, dv_high))
            ):
                half = (lane < HD) if side == 0 else (lane >= HD)
                inner = jnp.sum(jnp.where(half, product, 0.0), axis=1, keepdims=True)
                total = jnp.sum(
                    jnp.where(lane == 2 * p + side, totals[rows, :], 0.0), axis=1, keepdims=True
                )
                probs = jnp.exp(nt(pair, key[seen, :]) + bias - total)
                d_probs = nt(grads, value[seen, :])
                d_scores = (probs * (d_probs - inner)).astype(BF16)
                out = out + nn(d_scores, key[seen, :])
                dk[seen, :] = dk[seen, :] + tn(d_scores, pair)
                dv[seen, :] = dv[seen, :] + tn(probs.astype(BF16), grads)
            d_projected[rows, lanes] = turn(out * HD**-0.5, cos_rows, -sin_rows).astype(BF16)
            return carry

        lax.fori_loop(0, 2, one_pair, 0)

    attend_back(3)
    layer_sum.relay()
    attend_back(2)
    u_sum.middle()
    o_sum.start()
    attend_back(1)
    attend_back(0)
    g_sum.late()

    def key_rows(t, carry):
        rows = ds(t * 256, 256)
        key = dk_low[rows, :] + pltpu.roll(dk_high[rows, :], HD, 1)
        value = dv_high[rows, :] + pltpu.roll(dv_low[rows, :], HD, 1)
        key = turn(key, cos[rows, :], -sin[rows, :])
        d_projected[rows, pl.ds(256, 128)] = jnp.where(lane < HD, key, value).astype(BF16)
        return carry

    lax.fori_loop(0, 4, key_rows, 0)
    layer_sum.arrive()
    d_gather.sent()

    def layer_rows(t, carry):
        rows = ds(t * 16, 16)
        low_rows[rows, :] = (residual[rows, :] + layer_sum.total(t * 16, 16)).astype(BF16)
        return carry

    lax.fori_loop(0, TOK // 16, layer_rows, 0)
    d_sum.last()
    credit(3)
    layer_sum.sent()
    last_sum = row_sum(3)
    pl.semaphore_wait(free.at[3], 3)
    for s in (2, 1, 3, 0):
        rows = chip_rows(s)
        back = nt(d_projected[rows, pl.ds(0, 256)], wq[...])
        back = back + nn(d_projected[rows, pl.ds(256, 128)], wkv[...])
        blocks[s] = back.astype(BF16)
        last_sum.pair(s)
        if s == 1:
            last_sum.far()
    last_sum.near()
    layer_spread = spread(0, layer_out, 0, TOK)
    layer_spread.start()
    normed_again.wait()

    def project_grad(j, carry):
        lanes = ds(j * 512, 512)
        values = wide[:, lanes]
        wq[lanes, :] = tn(values, d_projected[:, pl.ds(0, 256)]).astype(BF16)
        wkv[:, lanes] = tn(d_projected[:, pl.ds(256, 128)], values).astype(BF16)
        return carry

    lax.fori_loop(0, 4, project_grad, 0)
    q_sum.start()
    g_sum.last()
    o_sum.middle()
    u_sum.last()
    kv_sum.start()
    last_sum.relay()
    q_sum.middle()
    kv_sum.middle()
    o_sum.last()
    layer_spread.end()
    last_sum.arrive()
    kv_sum.last()
    gain_one = gain_row(gains, 0)

    def input_rows(t, carry):
        rows = ds(t * 16, 16)
        values = x_mine[rows, :].astype(F32)
        back = norm_back(last_sum.total(t * 16, 16), values, gain_one, 0)
        low_rows[rows, :] = (d_residual[rows, :] + back).astype(BF16)
        return carry

    input_spreads = []
    for index in range(2):
        lax.fori_loop(index * (TOK // 32), (index + 1) * (TOK // 32), input_rows, 0)
        input_spreads.append(spread(1 + index, input_out, index * (TOK // 2), TOK // 2))
        input_spreads[index].start()
    keep(d_sum.own, gd_own)
    keep(g_sum.own, gg_own)
    keep(u_sum.own, gu_own)
    keep(o_sum.own, go_own)
    col_copies = []
    for k in range(7):
        target = lax.rem(here.c + k + 1, 8)
        col_copies.append(
            remote(
                gain_sums.at[:, ds(target * FEAT, FEAT)],
                gain_cols.at[here.c],
                gain_send.at[k],
                gain_recv.at[k],
                col_peers[k],
            )
        )
        col_copies[k].start()
    gain_cols[here.c] = gain_sums[:, ds(here.c * FEAT, FEAT)]
    for copy in col_copies:
        copy.wait()
    total = gain_cols[0]
    for c in range(1, 8):
        total = total + gain_cols[c]
    gain_rows[here.r] = total
    row_copies = [
        remote(
            gain_rows.at[here.r], gain_rows.at[here.r], last_send.at[k], last_recv.at[k], row_peers[k]
        )
        for k in range(7)
    ]
    for copy in row_copies:
        copy.start()
    q_sum.last()
    kv_sum.end()
    kv_total[...] = kv_sum.own[...].astype(F32) + kv_far[...].astype(F32)
    kv_swaps = []
    for index in range(2):
        theirs = ds(index * HD + (1 - here.k) * (HD // 2), HD // 2)
        land = kv_land.at[pl.ds(index * (HD // 2), HD // 2)]
        kv_swaps.append(
            remote(
                kv_total.at[theirs], land, last_send.at[7 + index], last_recv.at[7 + index], here.partner
            )
        )
        kv_swaps[index].start()
    keep(q_sum.own, gq_own)
    for index in range(2):
        kv_swaps[index].wait()
        mine = kv_total[ds(index * HD + here.k * (HD // 2), HD // 2), :]
        there = pl.ds(index * (HD // 2), HD // 2)
        kv_final[there, :] = mine + kv_land[there, :]
    keep(kv_final, kv_out)
    for sums in (d_sum, g_sum, u_sum, o_sum, q_sum):
        sums.end()
    for copy in row_copies:
        copy.wait()
    total = gain_rows[0]
    for r in range(1, 8):
        total = total + gain_rows[r]
    gain_cols[0] = total
    twin_copy = remote(gain_cols.at[0], gain_far, gain_send.at[7], gain_recv.at[7], here.twin)
    twin_copy.start()
    twin_copy.wait()
    gain_cols[0] = total + gain_far[...]
    keep(gain_cols.at[0], gains_out)
    for part in input_spreads:
        part.end()
    last_sum.sent()
    x_collect.sent()
    g_collect.sent()
    for copy in kept:
        if copy is not normed_copy:
            copy.wait()


def layer_call(*args):
    ff = args[6].shape[0]
    any_space = pl.BlockSpec(memory_space=pl.ANY)
    vmem_space = pl.BlockSpec(memory_space=pltpu.VMEM)
    dma = pltpu.SemaphoreType.DMA

    def low(*shape):
        return jax.ShapeDtypeStruct(shape, BF16)

    outs = (
        low(LEN, FEAT),
        low(LEN, FEAT),
        low(ff, FEAT),
        low(ff, FEAT),
        low(ff // 2, FEAT),
        low(ff // 2, FEAT),
        low(ff, FEAT),
        low(ff, FEAT),
        low(256, FEAT),
        low(256, FEAT),
        low(FEAT, 256),
        low(FEAT, 256),
        jax.ShapeDtypeStruct((HD, FEAT), F32),
        jax.ShapeDtypeStruct((8, FEAT), F32),
        low(LEN, D),
        low(8, TOK, FEAT),
    )

    def vmem(*shape, dtype=BF16):
        return pltpu.VMEM(shape, dtype)

    scratch = [
        vmem(8, TOK, FEAT),
        vmem(TOK, D),
        vmem(TOK, D),
        vmem(LEN, D),
        vmem(LEN, D),
        vmem(LEN, ff),
        vmem(LEN, ff),
        vmem(LEN, ff),
        vmem(ff, D),
        vmem(ff, D),
        vmem(ff, D),
        vmem(ff, D),
        vmem(256, D),
        vmem(D, 256),
        vmem(128, D),
        vmem(128, FEAT),
        vmem(128, FEAT),
        vmem(128, FEAT, dtype=F32),
        vmem(HD, FEAT, dtype=F32),
        vmem(HD, FEAT, dtype=F32),
        vmem(8, FEAT, dtype=F32),
        vmem(64, 256, dtype=F32),
        vmem(LEN, 128, dtype=F32),
        vmem(LEN, 128, dtype=F32),
        vmem(LEN, 128, dtype=F32),
        vmem(LEN, 256),
        vmem(LEN, 128),
        vmem(LEN, 128),
        vmem(LEN, 128),
        vmem(LEN, 128),
        vmem(LEN, 256),
        vmem(LEN, 128, dtype=F32),
        vmem(LEN, 256),
        vmem(LEN, 384),
        vmem(LEN, 128, dtype=F32),
        vmem(LEN, 128, dtype=F32),
        vmem(LEN, 128, dtype=F32),
        vmem(LEN, 128, dtype=F32),
        vmem(4, 256, D),
        vmem(4, TOK, D),
        vmem(2, TOK // 2, D),
        vmem(2, TOK, D),
        vmem(TOK, D, dtype=F32),
        vmem(TOK, D, dtype=F32),
        vmem(8, D, dtype=F32),
        vmem(8, 8, FEAT, dtype=F32),
        vmem(8, FEAT, dtype=F32),
        vmem(8, 8, FEAT, dtype=F32),
        vmem(ff, FEAT),
        vmem(3, ff, 2 * FEAT),
        vmem(8, ff // 2, FEAT),
        vmem(3, 2, ff // 2, FEAT),
        vmem(ff // 2, FEAT),
        vmem(4, ff, FEAT),
        vmem(3, ff, FEAT),
        vmem(4, 256, FEAT),
        vmem(3, 256, FEAT),
        vmem(4, FEAT, 256),
        vmem(3, FEAT, 256),
        vmem(128, FEAT),
        vmem(3, 128, 2 * FEAT),
        dma((2, 16)),
        dma((2, 16)),
        dma((2, 2)),
        dma((4, RowGather.SEMS)),
        dma((4, RowGather.SEMS)),
        dma((5,)),
        dma((7, SplitGather.SEMS)),
        dma((7, SplitGather.SEMS)),
        dma((7,)),
        dma((4, RowSum.SEMS)),
        dma((4, RowSum.SEMS)),
        dma((6, SplitSum.SEMS)),
        dma((6, SplitSum.SEMS)),
        dma((3, 8)),
        dma((3, 8)),
        dma((3,)),
        dma((11,)),
        dma((11,)),
        dma((8,)),
        dma((8,)),
        dma((8,)),
        pltpu.SemaphoreType.REGULAR((4,)),
    ]
    return pl.pallas_call(
        layer_kernel,
        out_shape=outs,
        in_specs=[any_space] * 9 + [vmem_space] * 3,
        out_specs=tuple(any_space for _ in outs),
        scratch_shapes=scratch,
        compiler_params=pltpu.CompilerParams(
            collective_id=0, has_side_effects=True, vmem_limit_bytes=VMEM_BYTES
        ),
        cost_estimate=pl.CostEstimate(flops=36 * 10**9, bytes_accessed=60 * 10**6, transcendentals=0),
        name="decoder_layer",
    )(*args)


def finish_kernel(
    layer,
    inner,
    d_own,
    d_far,
    g_own,
    g_far,
    u_own,
    u_far,
    o_own,
    o_far,
    q_own,
    q_far,
    kv,
    gains,
    layer_output,
    grad_input,
    grad_down,
    grad_gate,
    grad_up,
    grad_out,
    grad_query,
    grad_key,
    grad_value,
    grad_attn_gain,
    grad_mlp_gain,
):
    layer_output[...] = layer[...]
    grad_input[...] = inner[...].astype(F32)
    for total, own, far in (
        (grad_down, d_own, d_far),
        (grad_up, u_own, u_far),
        (grad_out, o_own, o_far),
        (grad_query, q_own, q_far),
    ):
        total[...] = own[...].astype(F32) + far[...].astype(F32)
    half = lax.rem(lax.axis_index("dp") + lax.axis_index("col"), 2)
    mine = pl.program_id(0) == half

    @pl.when(mine)
    def _():
        grad_gate[...] = g_own[...].astype(F32)

    @pl.when(jnp.logical_not(mine))
    def _():
        grad_gate[...] = g_far[...].astype(F32)

    width = grad_key.shape[0]
    grad_key[...] = kv[pl.ds(0, width), :]
    grad_value[...] = kv[pl.ds(width, width), :]
    grad_attn_gain[...] = gains[pl.ds(0, 1), :]
    grad_mlp_gain[...] = gains[pl.ds(1, 1), :]


def finish_call(*args):
    steps = 2
    ff = args[2].shape[0]

    def block(rows, index=lambda i: (i, 0)):
        return pl.BlockSpec((rows, FEAT), index)

    tall, wide, square = block(LEN // steps), block(ff // steps), block(256 // steps)
    halves = block(ff // steps, lambda i: (0, 0))
    whole = block(HD, lambda i: (0, 0))
    kept = block(HD // 2, lambda i: (0, 0))
    gain_block, row = block(8, lambda i: (0, 0)), block(1, lambda i: (0, 0))

    def full(rows, dtype=F32):
        return jax.ShapeDtypeStruct((rows, FEAT), dtype)

    return pl.pallas_call(
        finish_kernel,
        grid=(steps,),
        out_shape=(
            full(LEN, BF16),
            full(LEN),
            full(ff),
            full(ff),
            full(ff),
            full(256),
            full(256),
            full(HD // 2),
            full(HD // 2),
            full(1),
            full(1),
        ),
        in_specs=[tall, tall, wide, wide, halves, halves, wide, wide] + [square] * 4 + [whole, gain_block],
        out_specs=(tall, tall, wide, wide, wide, square, square, kept, kept, row, row),
        name="finish_outputs",
    )(*args)


def body(
    hidden_in,
    segment_ids,
    attn_gain,
    w_query,
    w_key,
    w_value,
    w_out,
    mlp_gain,
    w_gate,
    w_up,
    w_down,
    grad_output,
):
    (
        layer_output,
        grad_input,
        gd_own,
        gd_far,
        gg_own,
        gg_far,
        gu_own,
        gu_far,
        go_own,
        go_far,
        gq_own,
        gq_far,
        grad_kv,
        d_gains,
        _,
        _,
    ) = layer_call(
        hidden_in,
        grad_output,
        w_query,
        w_key.T,
        w_value.T,
        w_out,
        w_gate.T,
        w_up.T,
        w_down,
        attn_gain[None],
        mlp_gain[None],
        segment_ids,
    )

    (
        layer_output,
        grad_input,
        grad_down,
        grad_gate,
        grad_up,
        grad_out_proj,
        grad_query,
        grad_key,
        grad_value,
        grad_attn_gain,
        grad_mlp_gain,
    ) = finish_call(
        layer_output,
        grad_input,
        gd_own,
        gd_far,
        gg_own,
        gg_far,
        gu_own,
        gu_far,
        go_own,
        go_far,
        gq_own,
        gq_far,
        grad_kv,
        d_gains,
    )
    return (
        layer_output,
        grad_input,
        grad_attn_gain[0],
        grad_query,
        grad_key.T,
        grad_value.T,
        grad_out_proj,
        grad_mlp_gain[0],
        grad_gate.T,
        grad_up.T,
        grad_down,
    )


def solution(mesh):
    return jax.shard_map(
        body,
        mesh=mesh,
        in_specs=(
            P(("dp", "row"), "col"),
            P(("dp", "col"), None),
            P("col"),
            P("col", "row"),
            P("col", "row"),
            P("col", "row"),
            P("row", "col"),
            P("col"),
            P("col", "row"),
            P("col", "row"),
            P("row", "col"),
            P(("dp", "row"), "col"),
        ),
        out_specs=(
            P(("dp", "row"), "col"),
            P(("dp", "row"), "col"),
            P("col"),
            P("col", "row"),
            P("col", "row"),
            P("col", "row"),
            P("row", "col"),
            P("col"),
            P("col", "row"),
            P("col", "row"),
            P("row", "col"),
        ),
        check_vma=False,
    )
```
